256 devices in a mesh: seq: 64 (over x, z, core), head: 4 (over y).
Axes of the slice: x: 4, y: 4, z: 8, core: 2. Of those that a mesh axis runs over, the one named last changes fastest.
Arguments:
- queries: bfloat16 [8192, 8192], P('seq', 'head'), may hold values from -6 to 6
- key_vectors: bfloat16 [8192, 8192], P('seq', 'head'), may hold values from -6 to 6
- value_vectors: bfloat16 [8192, 8192], P('seq', 'head'), may hold values from -6 to 6
- cotangent: bfloat16 [8192, 8192], P('seq', 'head'), may hold values from -6 to 6
- member_ids: int32 [512], P('seq'), may hold values from 0 to 3
- in_scale: float32 [4, 8192], P(None, 'head'), may hold values from 0.3 to 3
- out_scale: float32 [4, 8192], P(None, 'head'), may hold values from 0.4 to 2.5
Outputs:
- query_grad: bfloat16 [8192, 8192], P('seq', 'head')
- key_grad: bfloat16 [8192, 8192], P('seq', 'head')
- value_grad: bfloat16 [8192, 8192], P('seq', 'head')
- in_scale_grad: float32 [4, 8192], P(None, 'head')
- out_scale_grad: float32 [4, 8192], P(None, 'head')
The draws below stay inside these ranges and needn't reach their ends.
All inputs are finite; a program needn't handle non-finite values.
Results may differ from the reference program's by a relative error of at most 0.015.
Values may be sent and summed in bfloat16 or wider, within the bound.
No kernel may reach another device: no remote copies, remote signals or barrier semaphores. Data moves between devices by JAX's collectives and lax.ppermute only.
A program may use at most 192 MiB of HBM per device.

```python
import math
import jax
import jax.numpy as jnp
from jax import lax

H = 64
DH = 128
TOK_DEV = 128
SPAN = 16
MEMBERS = 4
TOKENS = 8192
NCHUNKS = 512
N_SEQ = 64


def with_ends(result, rng, low, largest):
    longest = result.shape.index(max(result.shape))
    spots = []
    for shift in (0, 1):
        where = [jax.random.randint(jax.random.fold_in(rng, axis), (), 0, length) for axis, length in enumerate(result.shape)]
        where[longest] = (where[longest] + shift) % result.shape[longest]
        spots.append(tuple(where))
    return result.at[spots[0]].set(low).at[spots[1]].set(largest)


def steps_of(key, shape, split, low, top_value):
    level, own = 1.0, jax.random.fold_in(key, 6)
    for position, blocks in split:
        heights = jnp.exp(jax.random.uniform(jax.random.fold_in(own, position), (blocks,), jnp.float32, low / len(split), top_value / len(split)))
        level = level * jnp.repeat(heights, shape[position] // blocks).reshape([-1 if axis == position else 1 for axis in range(len(shape))])
    return level


def normal_values(rng, dims, spread, bound, shards=(), kind=jnp.bfloat16):
    gain = steps_of(rng, dims, shards, -0.22, 0.18) if shards else 1.0
    result = jax.random.normal(rng, dims, jnp.float32) * spread * gain
    return jnp.minimum(jnp.maximum(result, -bound), bound).astype(kind)


def setup_inputs(seed: int = 0) -> dict:
    arg_keys = jax.random.split(jax.random.key(seed), 8)
    return {
        "queries": normal_values(arg_keys[0], (TOKENS, H * DH), 1.0, 6.0, ((0, 64), (1, 4))),
        "key_vectors": normal_values(arg_keys[1], (TOKENS, H * DH), 1.0, 6.0, ((0, 64), (1, 4))),
        "value_vectors": normal_values(arg_keys[2], (TOKENS, H * DH), 1.0, 6.0, ((0, 64), (1, 4))),
        "cotangent": normal_values(arg_keys[3], (TOKENS, H * DH), 1.0, 6.0, ((0, 64), (1, 4))),
        "member_ids": with_ends(jax.random.randint(arg_keys[4], (NCHUNKS,), 0, MEMBERS), jax.random.fold_in(arg_keys[4], 1), 0, MEMBERS - 1).astype(jnp.int32),
        "in_scale": jnp.clip(jnp.exp(math.log(3.0) - 2.3025851 * jax.random.uniform(arg_keys[5], (MEMBERS, H * DH), jnp.float32) ** steps_of(arg_keys[5], (MEMBERS, H * DH), ((1, 4),), -0.2, 0.2)), 0.3, 3.0),
        "out_scale": jnp.clip(jnp.exp(math.log(2.5) - 1.8325814 * jax.random.uniform(arg_keys[6], (MEMBERS, H * DH), jnp.float32) ** steps_of(arg_keys[6], (MEMBERS, H * DH), ((1, 4),), -0.2, 0.2)), 0.4, 2.5),
    }


EPS = 1e-06
HIGH = lax.Precision.HIGHEST

def member_table(ids_block):
    per_token = jnp.repeat(ids_block, SPAN)
    return (per_token[:, None] == jnp.arange(MEMBERS, dtype=jnp.int32)[None, :]).astype(jnp.float32)

def reference(queries, key_vectors, value_vectors, cotangent, member_ids, in_scale, out_scale):
    full_width = H * DH
    query_blocks = queries.reshape(N_SEQ, TOK_DEV, full_width)
    key_blocks = key_vectors.reshape(N_SEQ, TOK_DEV, full_width)
    value_blocks = value_vectors.reshape(N_SEQ, TOK_DEV, full_width)
    cot_blocks = cotangent.reshape(N_SEQ, TOK_DEV, full_width)
    id_blocks = member_ids.reshape(N_SEQ, TOK_DEV // SPAN)
    causal = jnp.arange(TOK_DEV)[:, None] >= jnp.arange(TOK_DEV)[None, :]

    def scaled_values(value_block, ids_block):
        onehot = member_table(ids_block)
        in_tok = jnp.dot(onehot, in_scale, precision=HIGH)
        scaled = (in_tok * value_block.astype(jnp.float32)).astype(jnp.bfloat16)
        return (onehot, in_tok, scaled)

    def forward_step(state, inputs):
        key_block, value_block, ids_block = inputs
        _, _, scaled = scaled_values(value_block, ids_block)
        delta = jnp.einsum('jhd,jhe->hde', key_block.reshape(TOK_DEV, H, DH).astype(jnp.float32), scaled.reshape(TOK_DEV, H, DH).astype(jnp.float32))
        return (state + delta, state)
    _, states_in = lax.scan(forward_step, jnp.zeros((H, DH, DH), jnp.float32), (key_blocks, value_blocks, id_blocks))

    def backward_step(carry, inputs):
        state_after, in_sum, out_sum = carry
        query_block, key_block, value_block, cot_block, ids_block, state_in = inputs
        onehot, in_tok, scaled = scaled_values(value_block, ids_block)
        out_tok = jnp.dot(onehot, out_scale, precision=HIGH)
        query_heads = query_block.reshape(TOK_DEV, H, DH).astype(jnp.float32)
        key_heads = key_block.reshape(TOK_DEV, H, DH).astype(jnp.float32)
        scaled_heads = scaled.reshape(TOK_DEV, H, DH).astype(jnp.float32)
        state_low = state_in.astype(jnp.bfloat16).astype(jnp.float32)
        scores = jnp.einsum('thd,jhd->htj', query_heads, key_heads)
        weights = jnp.where(causal[None], scores, 0.0).astype(jnp.bfloat16).astype(jnp.float32)
        mixed = jnp.einsum('htj,jhe->the', weights, scaled_heads) + jnp.einsum('thd,hde->the', query_heads, state_low)
        mixed = mixed.reshape(TOK_DEV, full_width)
        cot_float = cot_block.astype(jnp.float32)
        scaled_cot = out_tok * cot_float
        square_sum = lax.optimization_barrier(jnp.sum(mixed * mixed, axis=1))
        cross_sum = lax.optimization_barrier(jnp.sum(scaled_cot * mixed, axis=1))
        rms_row = jnp.sqrt(square_sum / full_width + EPS)
        out_part = jnp.dot(onehot.T, cot_float * (mixed / rms_row[:, None]), precision=HIGH)
        grad_mixed = (scaled_cot / rms_row[:, None] - mixed * (cross_sum / (full_width * rms_row ** 3))[:, None]).astype(jnp.bfloat16)
        grad_heads = grad_mixed.reshape(TOK_DEV, H, DH).astype(jnp.float32)
        grad_scores = jnp.einsum('the,jhe->htj', grad_heads, scaled_heads)
        grad_weights = jnp.where(causal[None], grad_scores, 0.0).astype(jnp.bfloat16).astype(jnp.float32)
        query_grad = jnp.einsum('htj,jhd->thd', grad_weights, key_heads) + jnp.einsum('the,hde->thd', grad_heads, state_low)
        delta_suffix = jnp.einsum('thd,the->hde', query_heads, grad_heads)
        suffix_low = state_after.astype(jnp.bfloat16).astype(jnp.float32)
        key_grad = jnp.einsum('htj,thd->jhd', grad_weights, query_heads) + jnp.einsum('jhe,hde->jhd', scaled_heads, suffix_low)
        scaled_grad = jnp.einsum('htj,the->jhe', weights, grad_heads) + jnp.einsum('jhd,hde->jhe', key_heads, suffix_low)
        scaled_grad = scaled_grad.reshape(TOK_DEV, full_width)
        value_grad = (in_tok * scaled_grad).astype(jnp.bfloat16)
        in_part = jnp.dot(onehot.T, value_block.astype(jnp.float32) * scaled_grad, precision=HIGH)
        outputs = (query_grad.reshape(TOK_DEV, full_width).astype(jnp.bfloat16), key_grad.reshape(TOK_DEV, full_width).astype(jnp.bfloat16), value_grad)
        return ((state_after + delta_suffix, in_sum + in_part, out_sum + out_part), outputs)
    start = (jnp.zeros((H, DH, DH), jnp.float32), jnp.zeros((MEMBERS, full_width), jnp.float32), jnp.zeros((MEMBERS, full_width), jnp.float32))
    (_, in_total, out_total), (query_grad, key_grad, value_grad) = lax.scan(backward_step, start, (query_blocks, key_blocks, value_blocks, cot_blocks, id_blocks, states_in), reverse=True)
    return (query_grad.reshape(TOKENS, full_width), key_grad.reshape(TOKENS, full_width), value_grad.reshape(TOKENS, full_width), in_total, out_total)
```

```python
import functools

import jax
import jax.numpy as jnp
from jax import lax
from jax.experimental import pallas as pl
from jax.experimental.pallas import tpu as pltpu
from jax.sharding import PartitionSpec as P

DH = 128
SPAN = 16
MEMBERS = 4
EPS = 1e-06
CORES = 2
STEP_HEADS = 4
F32 = jnp.float32
BF16 = jnp.bfloat16

NN = (((1,), (0,)), ((), ()))
NT = (((1,), (1,)), ((), ()))
TN = (((0,), (0,)), ((), ()))


def dot(a, b, dims):
    return lax.dot_general(a, b, dims, preferred_element_type=F32)


def pair(own, other, lanes):
    return jnp.concatenate([own[:, lanes], other[:, lanes]], axis=0)


def rows_of_members(meta, scale, lanes, spans):
    choices = [scale[m : m + 1, lanes] for m in range(MEMBERS)]
    rows = []
    for s in range(spans):
        row = choices[0]
        for m in range(1, MEMBERS):
            row = jnp.where(meta[1 + s] == m, choices[m], row)
        rows.append(jnp.broadcast_to(row, (SPAN, DH)))
    return jnp.concatenate(rows, axis=0)


def member_sums(meta, x, spans):
    totals = [jnp.zeros((8, DH), F32) for _ in range(MEMBERS)]
    for s in range(spans):
        part = x[s * SPAN : s * SPAN + 8] + x[s * SPAN + 8 : (s + 1) * SPAN]
        for m in range(MEMBERS):
            keep = jnp.where(meta[1 + s] == m, 1.0, 0.0).astype(F32)
            totals[m] = totals[m] + keep * part
    return jnp.concatenate([jnp.sum(t, axis=0, keepdims=True) for t in totals], axis=0)


def causal_mask(meta, tok):
    size = 2 * tok
    core = meta[0]
    base_own = core * tok
    base_other = (1 - core) * tok - tok

    def place(axis):
        at = lax.broadcasted_iota(jnp.int32, (size, size), axis)
        return at + jnp.where(at < tok, base_own, base_other)

    return place(0) >= place(1)


def lanes_of(h):
    return pl.ds(h * DH, DH)


def states_kernel(meta, scale, k_own, k_other, v_own, v_other, scaled, delta):
    tok = k_own.shape[0]
    spans = 2 * tok // SPAN
    for h in range(delta.shape[0]):
        lanes = lanes_of(h)
        value = pair(v_own, v_other, lanes).astype(F32)
        low = (rows_of_members(meta, scale, lanes, spans) * value).astype(BF16)
        scaled[:, lanes] = low
        delta[h] = dot(pair(k_own, k_other, lanes), low, TN).astype(BF16)


def inside_kernel(meta, q_own, q_other, k_own, k_other, scaled, inside):
    tok = q_own.shape[0]
    causal = causal_mask(meta, tok)
    for h in range(scaled.shape[1] // DH):
        lanes = lanes_of(h)
        scores = dot(pair(q_own, q_other, lanes), pair(k_own, k_other, lanes), NT)
        weights = jnp.where(causal, scores, 0.0).astype(BF16)
        inside[:, lanes] = dot(weights, scaled[:, lanes], NN)


def mixed_kernel(
    meta, scale, q_own, q_other, c_own, c_other, state, inside, mixed, sums, squares, crosses
):
    tok = q_own.shape[0]
    spans = 2 * tok // SPAN
    step = pl.program_id(0)

    @pl.when(step == 0)
    def _():
        squares[...] = jnp.zeros_like(squares)
        crosses[...] = jnp.zeros_like(crosses)

    square, cross = squares[...], crosses[...]
    for h in range(state.shape[0]):
        lanes = lanes_of(h)
        mix = inside[:, lanes] + dot(pair(q_own, q_other, lanes), state[h], NN)
        mixed[:, lanes] = mix
        cot = pair(c_own, c_other, lanes).astype(F32)
        square = square + mix * mix
        cross = cross + rows_of_members(meta, scale, lanes, spans) * cot * mix
    squares[...] = square
    crosses[...] = cross

    @pl.when(step == pl.num_programs(0) - 1)
    def _():
        sums[0:1] = jnp.sum(jnp.transpose(square), axis=0, keepdims=True)
        sums[1:2] = jnp.sum(jnp.transpose(cross), axis=0, keepdims=True)


def grads_kernel(
    full_width, meta, scale, q_own, q_other, c_own, c_other, mixed, sums, grad, delta, out_part
):
    tok = q_own.shape[0]
    spans = 2 * tok // SPAN
    rms = jnp.sqrt(sums[0:1] / full_width + EPS)
    inverse = 1.0 / rms
    factor = sums[1:2] / (full_width * rms * rms * rms)
    inverse = jnp.transpose(jnp.broadcast_to(inverse, (DH, 2 * tok)))
    factor = jnp.transpose(jnp.broadcast_to(factor, (DH, 2 * tok)))
    for h in range(delta.shape[0]):
        lanes = lanes_of(h)
        cot = pair(c_own, c_other, lanes).astype(F32) * inverse
        mix = mixed[:, lanes]
        low = (rows_of_members(meta, scale, lanes, spans) * cot - mix * factor).astype(BF16)
        grad[:, lanes] = low
        delta[h] = dot(pair(q_own, q_other, lanes), low, TN).astype(BF16)
        out_part[:, lanes] = member_sums(meta, cot * mix, spans)


def back_kernel(
    meta, q_own, q_other, k_own, k_other, scaled, grad, state, query_own, query_other, key_in, value_in
):
    tok = q_own.shape[0]
    causal = causal_mask(meta, tok)
    for h in range(state.shape[0]):
        lanes = lanes_of(h)
        query = pair(q_own, q_other, lanes)
        key = pair(k_own, k_other, lanes)
        low = scaled[:, lanes]
        g = grad[:, lanes]
        weights = jnp.where(causal, dot(query, key, NT), 0.0).astype(BF16)
        grad_weights = jnp.where(causal, dot(g, low, NT), 0.0).astype(BF16)
        query_grad = (dot(grad_weights, key, NN) + dot(g, state[h], NT)).astype(BF16)
        query_own[:, lanes] = query_grad[:tok]
        query_other[:, lanes] = query_grad[tok:]
        key_in[:, lanes] = dot(grad_weights, query, TN)
        value_in[:, lanes] = dot(weights, g, TN)


def last_kernel(
    meta, scale, k_own, k_other, v_own, v_other, scaled, state, key_in, value_in,
    key_grad_own, key_grad_other, value_grad_own, value_grad_other, in_part,
):
    tok = k_own.shape[0]
    spans = 2 * tok // SPAN
    for h in range(state.shape[0]):
        lanes = lanes_of(h)
        key_grad = (key_in[:, lanes] + dot(scaled[:, lanes], state[h], NT)).astype(BF16)
        key_grad_own[:, lanes] = key_grad[:tok]
        key_grad_other[:, lanes] = key_grad[tok:]
        scaled_grad = value_in[:, lanes] + dot(pair(k_own, k_other, lanes), state[h], NN)
        value_grad = (rows_of_members(meta, scale, lanes, spans) * scaled_grad).astype(BF16)
        value_grad_own[:, lanes] = value_grad[:tok]
        value_grad_other[:, lanes] = value_grad[tok:]
        value = pair(v_own, v_other, lanes).astype(F32)
        in_part[:, lanes] = member_sums(meta, value * scaled_grad, spans)


def running_kernel(backward, pieces, sums):
    count = pieces.shape[0]
    total = jnp.zeros(pieces.shape[1:], F32)
    order = range(count - 1, -1, -1) if backward else range(count)
    for at in order:
        sums[at] = total.astype(BF16)
        total = total + pieces[at].astype(F32)


class Local:
    def __init__(self, meta, tok, width):
        self.meta = meta
        self.tok = tok
        self.width = width
        self.block = STEP_HEADS * DH
        self.steps = width // self.block

    def shared(self, rows):
        steps = self.steps
        return pl.BlockSpec((rows, self.block), lambda i, meta: (0, meta[0] * steps + i))

    def cols(self, rows):
        return pl.BlockSpec((rows, self.block), lambda i, meta: (0, i))

    def state(self):
        return pl.BlockSpec((STEP_HEADS, DH, DH), lambda i, meta: (i, 0, 0))

    def whole(self, shape):
        return pl.BlockSpec(shape, lambda i, meta: (0,) * len(shape))

    def call(self, body, ins, outs, args, shapes, name, scratch=(), flops=0):
        moved = sum(a.size * a.dtype.itemsize for a in args)
        return pl.pallas_call(
            body,
            grid_spec=pltpu.PrefetchScalarGridSpec(
                num_scalar_prefetch=1,
                grid=(self.steps,),
                in_specs=ins,
                out_specs=outs,
                scratch_shapes=scratch,
            ),
            out_shape=shapes,
            name=name,
            compiler_params=pltpu.CompilerParams(vmem_limit_bytes=32 * 2**20),
            cost_estimate=pl.CostEstimate(flops=flops, bytes_accessed=2 * moved, transcendentals=0),
        )(self.meta, *args)


def running_sums(pieces, backward):
    return pl.pallas_call(
        functools.partial(running_kernel, backward),
        out_shape=jax.ShapeDtypeStruct(pieces.shape, BF16),
        name="running_sums",
        compiler_params=pltpu.CompilerParams(vmem_limit_bytes=32 * 2**20),
    )(pieces)


def make_shards(n_seq, n_head):
    chips = n_seq // CORES
    core_swap = [(i, i ^ 1) for i in range(n_seq)]
    same_core = [[CORES * i + c for i in range(chips)] for c in range(CORES)]

    def swap(x):
        return lax.ppermute(x, "seq", core_swap)

    def scanned(delta, backward):
        heads = delta.shape[0]
        pieces = delta.reshape(chips, heads * DH // chips, DH)
        pieces = lax.all_to_all(
            pieces, "seq", 0, 0, axis_index_groups=same_core, tiled=True
        )
        sums = running_sums(pieces, backward)
        sums = lax.all_to_all(sums, "seq", 0, 0, axis_index_groups=same_core, tiled=True)
        return sums.reshape(heads, DH, DH)

    def side_by_side(core, own, other):
        return jnp.where(
            core == 0,
            jnp.concatenate([own, other], axis=1),
            jnp.concatenate([other, own], axis=1),
        )

    def shards(queries, key_vectors, value_vectors, cotangent, member_ids, in_scale, out_scale):
        tok, both = queries.shape
        width = both // CORES
        heads = width // DH
        full_width = both * n_head
        rows = 2 * tok
        core = lax.axis_index("seq") % CORES

        other_ids = swap(member_ids)
        v_other = swap(value_vectors)
        k_other = swap(key_vectors)
        meta = jnp.concatenate([core[None].astype(jnp.int32), member_ids, other_ids])
        local = Local(meta, tok, width)
        shared, cols, state = local.shared, local.cols, local.state
        sds = jax.ShapeDtypeStruct
        half = sds((tok, width), BF16)
        states = sds((heads, DH, DH), BF16)
        part = sds((MEMBERS, width), F32)
        wide = sds((rows, width), F32)
        pairs = [shared(tok), shared(tok)]
        unit = 2 * heads * rows * DH * DH

        scaled, delta = local.call(
            states_kernel,
            [shared(MEMBERS)] + pairs * 2,
            [cols(rows), state()],
            (in_scale, key_vectors, k_other, value_vectors, v_other),
            [sds((rows, width), BF16), states],
            "states",
            flops=unit,
        )
        queries_late, cotangent_late, delta = lax.optimization_barrier((queries, cotangent, delta))
        q_other = swap(queries_late)
        c_other = swap(cotangent_late)
        state_in = scanned(delta, False)
        inside = local.call(
            inside_kernel,
            pairs * 2 + [cols(rows)],
            cols(rows),
            (queries, q_other, key_vectors, k_other, scaled),
            wide,
            "inside",
            flops=4 * unit,
        )
        mixed, sums = local.call(
            mixed_kernel,
            [shared(MEMBERS)] + pairs * 2 + [state(), cols(rows)],
            [cols(rows), local.whole((2, rows))],
            (out_scale, queries, q_other, cotangent, c_other, state_in, inside),
            [wide, sds((2, rows), F32)],
            "mixed",
            scratch=[pltpu.VMEM((rows, DH), F32)] * 2,
            flops=unit,
        )
        across = swap(sums)
        sums = sums + jnp.concatenate([across[:, tok:], across[:, :tok]], axis=1)
        step = 1
        while step < n_head:
            sums = sums + lax.ppermute(sums, "head", [(i, i ^ step) for i in range(n_head)])
            step *= 2
        grad, delta_after, out_part = local.call(
            functools.partial(grads_kernel, full_width),
            [shared(MEMBERS)] + pairs * 2 + [cols(rows), local.whole((2, rows))],
            [cols(rows), state(), cols(MEMBERS)],
            (out_scale, queries, q_other, cotangent, c_other, mixed, sums),
            [sds((rows, width), BF16), states, part],
            "grads",
            flops=unit,
        )
        state_after = scanned(delta_after, True)
        query_own, query_send, key_in, value_in = local.call(
            back_kernel,
            pairs * 2 + [cols(rows), cols(rows), state()],
            [cols(tok), cols(tok), cols(rows), cols(rows)],
            (queries, q_other, key_vectors, k_other, scaled, grad, state_in),
            [half, half, wide, wide],
            "back",
            flops=11 * unit,
        )
        query_grad = side_by_side(core, query_own, swap(query_send))
        key_own, key_send, value_own, value_send, in_part = local.call(
            last_kernel,
            [shared(MEMBERS)] + pairs * 2 + [cols(rows), state(), cols(rows), cols(rows)],
            [cols(tok)] * 4 + [cols(MEMBERS)],
            (in_scale, key_vectors, k_other, value_vectors, v_other, scaled, state_after, key_in, value_in),
            [half] * 4 + [part],
            "last",
            flops=2 * unit,
        )
        parts = jnp.concatenate([in_part, out_part], axis=0)
        step = CORES
        while step < n_seq:
            parts = parts + lax.ppermute(parts, "seq", [(i, i ^ step) for i in range(n_seq)])
            step *= 2
        parts = side_by_side(core, parts, swap(parts))
        key_grad = side_by_side(core, key_own, swap(key_send))
        value_grad = side_by_side(core, value_own, swap(value_send))
        return query_grad, key_grad, value_grad, parts[:MEMBERS], parts[MEMBERS:]

    return shards


def solution(mesh):
    n_seq, n_head = mesh.shape["seq"], mesh.shape["head"]
    shards = make_shards(n_seq, n_head)
    placed = (
        P("seq", "head"),
        P("seq", "head"),
        P("seq", "head"),
        P("seq", "head"),
        P("seq"),
        P(None, "head"),
        P(None, "head"),
    )
    return jax.shard_map(
        shards,
        mesh=mesh,
        in_specs=placed,
        out_specs=(
            P("seq", "head"),
            P("seq", "head"),
            P("seq", "head"),
            P(None, "head"),
            P(None, "head"),
        ),
        check_vma=False,
    )
```

```python
import functools

import jax
import jax.numpy as jnp
from jax import lax
from jax.experimental import pallas as pl
from jax.experimental.pallas import tpu as pltpu
from jax.sharding import PartitionSpec as P

DH = 128
SPAN = 16
MEMBERS = 4
EPS = 1e-06
CORES = 2
STEP_HEADS = 4
VMEM_BYTES = 56 * 2**20
F32 = jnp.float32
BF16 = jnp.bfloat16

NN = (((1,), (0,)), ((), ()))
NT = (((1,), (1,)), ((), ()))
TN = (((0,), (0,)), ((), ()))


def dot(a, b, dims):
    return lax.dot_general(a, b, dims, preferred_element_type=F32)


def pair(own, other, lanes):
    return jnp.concatenate([own[:, lanes], other[:, lanes]], axis=0)


def rows_of_members(meta, scale, lanes, spans):
    choices = [scale[m : m + 1, lanes] for m in range(MEMBERS)]
    rows = []
    for s in range(spans):
        row = choices[0]
        for m in range(1, MEMBERS):
            row = jnp.where(meta[1 + s] == m, choices[m], row)
        rows.append(jnp.broadcast_to(row, (SPAN, DH)))
    return jnp.concatenate(rows, axis=0)


def member_sums(meta, x, spans):
    totals = [jnp.zeros((8, DH), F32) for _ in range(MEMBERS)]
    for s in range(spans):
        part = x[s * SPAN : s * SPAN + 8] + x[s * SPAN + 8 : (s + 1) * SPAN]
        for m in range(MEMBERS):
            keep = jnp.where(meta[1 + s] == m, 1.0, 0.0).astype(F32)
            totals[m] = totals[m] + keep * part
    return jnp.concatenate([jnp.sum(t, axis=0, keepdims=True) for t in totals], axis=0)


def causal_mask(meta, tok):
    size = 2 * tok
    core = meta[0]
    base_own = core * tok
    base_other = (1 - core) * tok - tok

    def place(axis):
        at = lax.broadcasted_iota(jnp.int32, (size, size), axis)
        return at + jnp.where(at < tok, base_own, base_other)

    return place(0) >= place(1)


def lanes_of(h):
    return pl.ds(h * DH, DH)


def states_kernel(meta, scale, k_own, k_other, v_own, v_other, scaled, delta):
    tok = k_own.shape[0]
    spans = 2 * tok // SPAN
    for h in range(delta.shape[0]):
        lanes = lanes_of(h)
        value = pair(v_own, v_other, lanes).astype(F32)
        low = (rows_of_members(meta, scale, lanes, spans) * value).astype(BF16)
        scaled[:, lanes] = low
        delta[h] = dot(pair(k_own, k_other, lanes), low, TN).astype(BF16)


def inside_kernel(meta, q_own, q_other, k_own, k_other, scaled, inside):
    tok = q_own.shape[0]
    causal = causal_mask(meta, tok)
    for h in range(scaled.shape[1] // DH):
        lanes = lanes_of(h)
        scores = dot(pair(q_own, q_other, lanes), pair(k_own, k_other, lanes), NT)
        weights = jnp.where(causal, scores, 0.0).astype(BF16)
        inside[:, lanes] = dot(weights, scaled[:, lanes], NN)


def mixed_kernel(
    meta, scale, q_own, q_other, c_own, c_other, state, inside, mixed, sums, squares, crosses
):
    tok = q_own.shape[0]
    spans = 2 * tok // SPAN
    step = pl.program_id(0)

    @pl.when(step == 0)
    def _():
        squares[...] = jnp.zeros_like(squares)
        crosses[...] = jnp.zeros_like(crosses)

    square, cross = squares[...], crosses[...]
    for h in range(state.shape[0]):
        lanes = lanes_of(h)
        mix = inside[:, lanes] + dot(pair(q_own, q_other, lanes), state[h], NN)
        mixed[:, lanes] = mix
        cot = pair(c_own, c_other, lanes).astype(F32)
        square = square + mix * mix
        cross = cross + rows_of_members(meta, scale, lanes, spans) * cot * mix
    squares[...] = square
    crosses[...] = cross

    @pl.when(step == pl.num_programs(0) - 1)
    def _():
        sums[0:1] = jnp.sum(jnp.transpose(square), axis=0, keepdims=True)
        sums[1:2] = jnp.sum(jnp.transpose(cross), axis=0, keepdims=True)


def grads_kernel(
    full_width, meta, scale, q_own, q_other, c_own, c_other, mixed, sums, grad, delta
):
    tok = q_own.shape[0]
    spans = 2 * tok // SPAN
    rms = jnp.sqrt(sums[0:1] / full_width + EPS)
    inverse = 1.0 / rms
    factor = sums[1:2] / (full_width * rms * rms * rms)
    inverse = jnp.transpose(jnp.broadcast_to(inverse, (DH, 2 * tok)))
    factor = jnp.transpose(jnp.broadcast_to(factor, (DH, 2 * tok)))
    for h in range(delta.shape[0]):
        lanes = lanes_of(h)
        cot = pair(c_own, c_other, lanes).astype(F32) * inverse
        mix = mixed[:, lanes]
        low = (rows_of_members(meta, scale, lanes, spans) * cot - mix * factor).astype(BF16)
        grad[:, lanes] = low
        delta[h] = dot(pair(q_own, q_other, lanes), low, TN).astype(BF16)


def back_kernel(
    full_width, meta, q_own, q_other, k_own, k_other, c_own, c_other, scaled, grad, state, mixed, sums,
    query_own, query_other, key_in, value_in, out_part,
):
    tok = q_own.shape[0]
    spans = 2 * tok // SPAN
    causal = causal_mask(meta, tok)
    inverse = 1.0 / jnp.sqrt(sums[0:1] / full_width + EPS)
    inverse = jnp.transpose(jnp.broadcast_to(inverse, (DH, 2 * tok)))
    for h in range(state.shape[0]):
        lanes = lanes_of(h)
        query = pair(q_own, q_other, lanes)
        key = pair(k_own, k_other, lanes)
        low = scaled[:, lanes]
        g = grad[:, lanes]
        weights = jnp.where(causal, dot(query, key, NT), 0.0).astype(BF16)
        grad_weights = jnp.where(causal, dot(g, low, NT), 0.0).astype(BF16)
        query_grad = (dot(grad_weights, key, NN) + dot(g, state[h], NT)).astype(BF16)
        query_own[:, lanes] = query_grad[:tok]
        query_other[:, lanes] = query_grad[tok:]
        key_in[:, lanes] = dot(grad_weights, query, TN)
        value_in[:, lanes] = dot(weights, g, TN)
        normed = pair(c_own, c_other, lanes).astype(F32) * (mixed[:, lanes] * inverse)
        out_part[:, lanes] = member_sums(meta, normed, spans)


def value_kernel(
    meta, scale, k_own, k_other, v_own, v_other, state, value_in,
    value_grad_own, value_grad_other, in_part,
):
    tok = k_own.shape[0]
    spans = 2 * tok // SPAN
    for h in range(state.shape[0]):
        lanes = lanes_of(h)
        scaled_grad = value_in[:, lanes] + dot(pair(k_own, k_other, lanes), state[h], NN)
        value_grad = (rows_of_members(meta, scale, lanes, spans) * scaled_grad).astype(BF16)
        value_grad_own[:, lanes] = value_grad[:tok]
        value_grad_other[:, lanes] = value_grad[tok:]
        value = pair(v_own, v_other, lanes).astype(F32)
        in_part[:, lanes] = member_sums(meta, value * scaled_grad, spans)


def key_kernel(meta, scaled, state, key_in, key_grad_own, key_grad_other):
    tok = key_grad_own.shape[0]
    for h in range(state.shape[0]):
        lanes = lanes_of(h)
        key_grad = (key_in[:, lanes] + dot(scaled[:, lanes], state[h], NT)).astype(BF16)
        key_grad_own[:, lanes] = key_grad[:tok]
        key_grad_other[:, lanes] = key_grad[tok:]


def running_kernel(backward, pieces, sums):
    count = pieces.shape[0]
    total = jnp.zeros(pieces.shape[1:], F32)
    order = range(count - 1, -1, -1) if backward else range(count)
    for at in order:
        sums[at] = total.astype(BF16)
        total = total + pieces[at].astype(F32)


class Local:
    def __init__(self, meta, tok, width):
        self.meta = meta
        self.tok = tok
        self.width = width
        self.block = STEP_HEADS * DH
        self.steps = width // self.block

    def shared(self, rows):
        steps = self.steps
        return pl.BlockSpec((rows, self.block), lambda i, meta: (0, meta[0] * steps + i))

    def cols(self, rows):
        return pl.BlockSpec((rows, self.block), lambda i, meta: (0, i))

    def state(self):
        return pl.BlockSpec((STEP_HEADS, DH, DH), lambda i, meta: (i, 0, 0))

    def whole(self, shape):
        return pl.BlockSpec(shape, lambda i, meta: (0,) * len(shape))

    def call(self, body, ins, outs, args, shapes, name, scratch=(), flops=0):
        moved = sum(a.size * a.dtype.itemsize for a in args)
        return pl.pallas_call(
            body,
            grid_spec=pltpu.PrefetchScalarGridSpec(
                num_scalar_prefetch=1,
                grid=(self.steps,),
                in_specs=ins,
                out_specs=outs,
                scratch_shapes=scratch,
            ),
            out_shape=shapes,
            name=name,
            compiler_params=pltpu.CompilerParams(vmem_limit_bytes=VMEM_BYTES),
            cost_estimate=pl.CostEstimate(flops=flops, bytes_accessed=2 * moved, transcendentals=0),
        )(self.meta, *args)


def running_sums(pieces, backward):
    return pl.pallas_call(
        functools.partial(running_kernel, backward),
        out_shape=jax.ShapeDtypeStruct(pieces.shape, BF16),
        name="running_sums",
        compiler_params=pltpu.CompilerParams(vmem_limit_bytes=VMEM_BYTES),
    )(pieces)


def make_shards(n_seq, n_head):
    chips = n_seq // CORES
    core_swap = [(i, i ^ 1) for i in range(n_seq)]
    same_core = [[CORES * i + c for i in range(chips)] for c in range(CORES)]

    def swap(x):
        return lax.ppermute(x, "seq", core_swap)

    def scanned(delta, backward):
        heads = delta.shape[0]
        pieces = delta.reshape(chips, heads * DH // chips, DH)
        pieces = lax.all_to_all(
            pieces, "seq", 0, 0, axis_index_groups=same_core, tiled=True
        )
        sums = running_sums(pieces, backward)
        sums = lax.all_to_all(sums, "seq", 0, 0, axis_index_groups=same_core, tiled=True)
        return sums.reshape(heads, DH, DH)

    def side_by_side(core, own, other):
        return jnp.where(
            core == 0,
            jnp.concatenate([own, other], axis=1),
            jnp.concatenate([other, own], axis=1),
        )

    def shards(queries, key_vectors, value_vectors, cotangent, member_ids, in_scale, out_scale):
        tok, both = queries.shape
        width = both // CORES
        heads = width // DH
        full_width = both * n_head
        rows = 2 * tok
        core = lax.axis_index("seq") % CORES

        other_ids = swap(member_ids)
        v_other = swap(value_vectors)
        k_other = swap(key_vectors)
        meta = jnp.concatenate([core[None].astype(jnp.int32), member_ids, other_ids])
        local = Local(meta, tok, width)
        shared, cols, state = local.shared, local.cols, local.state
        sds = jax.ShapeDtypeStruct
        half = sds((tok, width), BF16)
        states = sds((heads, DH, DH), BF16)
        part = sds((MEMBERS, width), F32)
        wide = sds((rows, width), F32)
        pairs = [shared(tok), shared(tok)]
        unit = 2 * heads * rows * DH * DH

        scaled, delta = local.call(
            states_kernel,
            [shared(MEMBERS)] + pairs * 2,
            [cols(rows), state()],
            (in_scale, key_vectors, k_other, value_vectors, v_other),
            [sds((rows, width), BF16), states],
            "states",
            flops=unit,
        )
        queries_late, cotangent_late, delta = lax.optimization_barrier((queries, cotangent, delta))
        q_other = swap(queries_late)
        c_other = swap(cotangent_late)
        state_in = scanned(delta, False)
        inside = local.call(
            inside_kernel,
            pairs * 2 + [cols(rows)],
            cols(rows),
            (queries, q_other, key_vectors, k_other, scaled),
            wide,
            "inside",
            flops=4 * unit,
        )
        mixed, sums = local.call(
            mixed_kernel,
            [shared(MEMBERS)] + pairs * 2 + [state(), cols(rows)],
            [cols(rows), local.whole((2, rows))],
            (out_scale, queries, q_other, cotangent, c_other, state_in, inside),
            [wide, sds((2, rows), F32)],
            "mixed",
            scratch=[pltpu.VMEM((rows, DH), F32)] * 2,
            flops=unit,
        )
        across = swap(sums)
        sums = sums + jnp.concatenate([across[:, tok:], across[:, :tok]], axis=1)
        step = 1
        while step < n_head:
            sums = sums + lax.ppermute(sums, "head", [(i, i ^ step) for i in range(n_head)])
            step *= 2
        grad, delta_after = local.call(
            functools.partial(grads_kernel, full_width),
            [shared(MEMBERS)] + pairs * 2 + [cols(rows), local.whole((2, rows))],
            [cols(rows), state()],
            (out_scale, queries, q_other, cotangent, c_other, mixed, sums),
            [sds((rows, width), BF16), states],
            "grads",
            flops=unit,
        )
        state_after = scanned(delta_after, True)
        query_own, query_send, key_in, value_in, out_part = local.call(
            functools.partial(back_kernel, full_width),
            pairs * 3 + [cols(rows), cols(rows), state(), cols(rows), local.whole((2, rows))],
            [cols(tok), cols(tok), cols(rows), cols(rows), cols(MEMBERS)],
            (queries, q_other, key_vectors, k_other, cotangent, c_other, scaled, grad, state_in, mixed, sums),
            [half, half, wide, wide, part],
            "back",
            flops=11 * unit,
        )
        query_grad = side_by_side(core, query_own, swap(query_send))
        value_own, value_send, in_part = local.call(
            value_kernel,
            [shared(MEMBERS)] + pairs * 2 + [state(), cols(rows)],
            [cols(tok)] * 2 + [cols(MEMBERS)],
            (in_scale, key_vectors, k_other, value_vectors, v_other, state_after, value_in),
            [half] * 2 + [part],
            "value",
            flops=unit,
        )
        parts = jnp.concatenate([in_part, out_part], axis=0).astype(BF16)
        copies = jnp.broadcast_to(parts[None], (chips,) + parts.shape)
        copies = lax.all_to_all(copies, "seq", 0, 0, axis_index_groups=same_core, tiled=True)
        key_own, key_send = local.call(
            key_kernel,
            [cols(rows), state(), cols(rows)],
            [cols(tok)] * 2,
            (scaled, state_after, key_in),
            [half] * 2,
            "key",
            flops=unit,
        )
        key_grad = side_by_side(core, key_own, swap(key_send))
        value_grad = side_by_side(core, value_own, swap(value_send))
        copies, key_grad, value_grad, query_grad = lax.optimization_barrier(
            (copies, key_grad, value_grad, query_grad)
        )
        parts = jnp.sum(copies.astype(F32), axis=0)
        parts = side_by_side(core, parts, swap(parts))
        return query_grad, key_grad, value_grad, parts[:MEMBERS], parts[MEMBERS:]

    return shards


def solution(mesh):
    n_seq, n_head = mesh.shape["seq"], mesh.shape["head"]
    shards = make_shards(n_seq, n_head)
    placed = (
        P("seq", "head"),
        P("seq", "head"),
        P("seq", "head"),
        P("seq", "head"),
        P("seq"),
        P(None, "head"),
        P(None, "head"),
    )
    return jax.shard_map(
        shards,
        mesh=mesh,
        in_specs=placed,
        out_specs=(
            P("seq", "head"),
            P("seq", "head"),
            P("seq", "head"),
            P(None, "head"),
            P(None, "head"),
        ),
        check_vma=False,
    )
```

```python
import functools

import jax
import jax.numpy as jnp
from jax import lax
from jax.experimental import pallas as pl
from jax.experimental.pallas import tpu as pltpu
from jax.sharding import PartitionSpec as P

DH = 128
SPAN = 16
MEMBERS = 4
EPS = 1e-06
CORES = 2
STEP_HEADS = 4
VMEM_BYTES = 24 * 2**20
F32 = jnp.float32
BF16 = jnp.bfloat16

NN = (((1,), (0,)), ((), ()))
NT = (((1,), (1,)), ((), ()))
TN = (((0,), (0,)), ((), ()))


def dot(a, b, dims):
    return lax.dot_general(a, b, dims, preferred_element_type=F32)


def pair(own, other, lanes):
    return jnp.concatenate([own[:, lanes], other[:, lanes]], axis=0)


def rows_of_members(meta, scale, lanes, spans):
    choices = [scale[m : m + 1, lanes] for m in range(MEMBERS)]
    rows = []
    for s in range(spans):
        row = choices[0]
        for m in range(1, MEMBERS):
            row = jnp.where(meta[1 + s] == m, choices[m], row)
        rows.append(jnp.broadcast_to(row, (SPAN, DH)))
    return jnp.concatenate(rows, axis=0)


def member_sums(meta, x, spans):
    totals = [jnp.zeros((8, DH), F32) for _ in range(MEMBERS)]
    for s in range(spans):
        part = x[s * SPAN : s * SPAN + 8] + x[s * SPAN + 8 : (s + 1) * SPAN]
        for m in range(MEMBERS):
            keep = jnp.where(meta[1 + s] == m, 1.0, 0.0).astype(F32)
            totals[m] = totals[m] + keep * part
    return jnp.concatenate([jnp.sum(t, axis=0, keepdims=True) for t in totals], axis=0)


def causal_mask(meta, tok):
    size = 2 * tok
    core = meta[0]
    base_own = core * tok
    base_other = (1 - core) * tok - tok

    def place(axis):
        at = lax.broadcasted_iota(jnp.int32, (size, size), axis)
        return at + jnp.where(at < tok, base_own, base_other)

    return place(0) >= place(1)


def lanes_of(h):
    return pl.ds(h * DH, DH)


def states_kernel(meta, scale, k_own, k_other, v_own, v_other, scaled, delta):
    tok = k_own.shape[0]
    spans = 2 * tok // SPAN
    for h in range(delta.shape[0]):
        lanes = lanes_of(h)
        value = pair(v_own, v_other, lanes).astype(F32)
        low = (rows_of_members(meta, scale, lanes, spans) * value).astype(BF16)
        scaled[:, lanes] = low
        delta[h] = dot(pair(k_own, k_other, lanes), low, TN).astype(BF16)


def inside_kernel(meta, q_own, q_other, k_own, k_other, scaled, inside):
    tok = q_own.shape[0]
    causal = causal_mask(meta, tok)
    for h in range(scaled.shape[1] // DH):
        lanes = lanes_of(h)
        scores = dot(pair(q_own, q_other, lanes), pair(k_own, k_other, lanes), NT)
        weights = jnp.where(causal, scores, 0.0).astype(BF16)
        inside[:, lanes] = dot(weights, scaled[:, lanes], NN)


def mixed_kernel(
    meta, scale, q_own, q_other, c_own, c_other, state, inside, mixed, sums, squares, crosses
):
    tok = q_own.shape[0]
    spans = 2 * tok // SPAN
    step = pl.program_id(0)

    @pl.when(step == 0)
    def _():
        squares[...] = jnp.zeros_like(squares)
        crosses[...] = jnp.zeros_like(crosses)

    square, cross = squares[...], crosses[...]
    for h in range(state.shape[0]):
        lanes = lanes_of(h)
        mix = inside[:, lanes] + dot(pair(q_own, q_other, lanes), state[h], NN)
        mixed[:, lanes] = mix
        cot = pair(c_own, c_other, lanes).astype(F32)
        square = square + mix * mix
        cross = cross + rows_of_members(meta, scale, lanes, spans) * cot * mix
    squares[...] = square
    crosses[...] = cross

    @pl.when(step == pl.num_programs(0) - 1)
    def _():
        sums[0:1] = jnp.sum(jnp.transpose(square), axis=0, keepdims=True)
        sums[1:2] = jnp.sum(jnp.transpose(cross), axis=0, keepdims=True)


def grads_kernel(
    full_width, meta, scale, q_own, q_other, c_own, c_other, mixed, sums, grad, delta
):
    tok = q_own.shape[0]
    spans = 2 * tok // SPAN
    rms = jnp.sqrt(sums[0:1] / full_width + EPS)
    inverse = 1.0 / rms
    factor = sums[1:2] / (full_width * rms * rms * rms)
    inverse = jnp.transpose(jnp.broadcast_to(inverse, (DH, 2 * tok)))
    factor = jnp.transpose(jnp.broadcast_to(factor, (DH, 2 * tok)))
    for h in range(delta.shape[0]):
        lanes = lanes_of(h)
        cot = pair(c_own, c_other, lanes).astype(F32) * inverse
        mix = mixed[:, lanes]
        low = (rows_of_members(meta, scale, lanes, spans) * cot - mix * factor).astype(BF16)
        grad[:, lanes] = low
        delta[h] = dot(pair(q_own, q_other, lanes), low, TN).astype(BF16)


def back_kernel(
    full_width, meta, q_own, q_other, k_own, k_other, c_own, c_other, scaled, grad, state, mixed, sums,
    query_own, query_other, key_in, value_in, out_part,
):
    tok = q_own.shape[0]
    spans = 2 * tok // SPAN
    causal = causal_mask(meta, tok)
    inverse = 1.0 / jnp.sqrt(sums[0:1] / full_width + EPS)
    inverse = jnp.transpose(jnp.broadcast_to(inverse, (DH, 2 * tok)))
    for h in range(state.shape[0]):
        lanes = lanes_of(h)
        query = pair(q_own, q_other, lanes)
        key = pair(k_own, k_other, lanes)
        low = scaled[:, lanes]
        g = grad[:, lanes]
        weights = jnp.where(causal, dot(query, key, NT), 0.0).astype(BF16)
        grad_weights = jnp.where(causal, dot(g, low, NT), 0.0).astype(BF16)
        query_grad = (dot(grad_weights, key, NN) + dot(g, state[h], NT)).astype(BF16)
        query_own[:, lanes] = query_grad[:tok]
        query_other[:, lanes] = query_grad[tok:]
        key_in[:, lanes] = dot(grad_weights, query, TN)
        value_in[:, lanes] = dot(weights, g, TN)
        normed = pair(c_own, c_other, lanes).astype(F32) * (mixed[:, lanes] * inverse)
        out_part[:, lanes] = member_sums(meta, normed, spans)


def value_kernel(
    meta, scale, k_own, k_other, v_own, v_other, state, value_in, out_part,
    value_grad_own, value_grad_other, parts,
):
    tok = k_own.shape[0]
    spans = 2 * tok // SPAN
    for h in range(state.shape[0]):
        lanes = lanes_of(h)
        scaled_grad = value_in[:, lanes] + dot(pair(k_own, k_other, lanes), state[h], NN)
        value_grad = (rows_of_members(meta, scale, lanes, spans) * scaled_grad).astype(BF16)
        value_grad_own[:, lanes] = value_grad[:tok]
        value_grad_other[:, lanes] = value_grad[tok:]
        value = pair(v_own, v_other, lanes).astype(F32)
        in_part = member_sums(meta, value * scaled_grad, spans)
        parts[:, lanes] = jnp.concatenate([in_part, out_part[:, lanes]], axis=0)


def key_kernel(meta, scaled, state, key_in, key_grad_own, key_grad_other):
    tok = key_grad_own.shape[0]
    for h in range(state.shape[0]):
        lanes = lanes_of(h)
        key_grad = (key_in[:, lanes] + dot(scaled[:, lanes], state[h], NT)).astype(BF16)
        key_grad_own[:, lanes] = key_grad[:tok]
        key_grad_other[:, lanes] = key_grad[tok:]


def running_kernel(backward, pieces, sums):
    count = pieces.shape[0]
    total = jnp.zeros(pieces.shape[1:], F32)
    order = range(count - 1, -1, -1) if backward else range(count)
    for at in order:
        sums[at] = total.astype(BF16)
        total = total + pieces[at].astype(F32)


class Local:
    def __init__(self, tok, width):
        self.tok = tok
        self.width = width
        self.block = STEP_HEADS * DH
        self.steps = width // self.block

    def shared(self, rows):
        steps = self.steps
        return pl.BlockSpec((rows, self.block), lambda i, meta: (0, meta[0] * steps + i))

    def cols(self, rows):
        return pl.BlockSpec((rows, self.block), lambda i, meta: (0, i))

    def state(self):
        return pl.BlockSpec((STEP_HEADS, DH, DH), lambda i, meta: (i, 0, 0))

    def whole(self, shape):
        return pl.BlockSpec(shape, lambda i, meta: (0,) * len(shape))

    def call(self, body, meta, ins, outs, args, shapes, name, scratch=(), flops=0):
        moved = sum(a.size * a.dtype.itemsize for a in args)
        return pl.pallas_call(
            body,
            grid_spec=pltpu.PrefetchScalarGridSpec(
                num_scalar_prefetch=1,
                grid=(self.steps,),
                in_specs=ins,
                out_specs=outs,
                scratch_shapes=scratch,
            ),
            out_shape=shapes,
            name=name,
            compiler_params=pltpu.CompilerParams(vmem_limit_bytes=VMEM_BYTES),
            cost_estimate=pl.CostEstimate(flops=flops, bytes_accessed=2 * moved, transcendentals=0),
        )(meta, *args)


def fast(x):
    return pltpu.with_memory_space_constraint(x, pltpu.VMEM)


def slow(x):
    return pltpu.with_memory_space_constraint(x, pltpu.HBM)


def running_sums(pieces, backward):
    return pl.pallas_call(
        functools.partial(running_kernel, backward),
        out_shape=pltpu.HBM(pieces.shape, BF16),
        name="running_sums",
        compiler_params=pltpu.CompilerParams(vmem_limit_bytes=VMEM_BYTES),
    )(fast(pieces))


def make_shards(n_seq, n_head):
    chips = n_seq // CORES
    core_swap = [(i, i ^ 1) for i in range(n_seq)]
    same_core = [[CORES * i + c for i in range(chips)] for c in range(CORES)]

    def swap(x):
        return lax.ppermute(x, "seq", core_swap)

    def scanned(delta, backward):
        heads = delta.shape[0]
        pieces = delta.reshape(chips, heads * DH // chips, DH)
        pieces = lax.all_to_all(
            pieces, "seq", 0, 0, axis_index_groups=same_core, tiled=True
        )
        sums = running_sums(pieces, backward)
        sums = lax.all_to_all(sums, "seq", 0, 0, axis_index_groups=same_core, tiled=True)
        return sums.reshape(heads, DH, DH)

    def side_by_side(core, own, other):
        return jnp.where(
            core == 0,
            jnp.concatenate([own, other], axis=1),
            jnp.concatenate([other, own], axis=1),
        )

    def turned(x, tok):
        return jnp.concatenate([x[:, tok:], x[:, :tok]], axis=1)

    def over_heads(x, tok):
        got = None
        for shift in range(1, n_head // 2 + 1):
            moves = []
            for s in range(n_seq):
                for h in range(n_head):
                    if s % CORES == 0:
                        moves.append((s * n_head + h, s * n_head + (h + shift) % n_head))
                    elif 2 * shift != n_head:
                        moves.append((s * n_head + h, s * n_head + (h - shift) % n_head))
            came = lax.ppermute(x, ("seq", "head"), moves)
            got = came if got is None else got + came
        return x + got + turned(swap(got), tok)

    def shards(queries, key_vectors, value_vectors, cotangent, member_ids, in_scale, out_scale):
        tok, both = queries.shape
        width = both // CORES
        heads = width // DH
        full_width = both * n_head
        rows = 2 * tok
        core = lax.axis_index("seq") % CORES

        other_ids = swap(member_ids)
        v_other = swap(value_vectors)
        k_other = swap(key_vectors)
        place = core[None].astype(jnp.int32)
        local = Local(tok, width)
        shared, cols, state = local.shared, local.cols, local.state
        half = pltpu.HBM((tok, width), BF16)
        low = pltpu.HBM((rows, width), BF16)
        wide = pltpu.HBM((rows, width), F32)
        part = pltpu.HBM((MEMBERS, width), F32)
        sent = pltpu.HBM((heads, DH, DH), BF16)
        pairs = [shared(tok), shared(tok)]
        unit = 2 * heads * rows * DH * DH

        meta = jnp.concatenate([place, member_ids, other_ids])
        scaled, delta = local.call(
            states_kernel,
            meta,
            [shared(MEMBERS)] + pairs * 2,
            [cols(rows), state()],
            (in_scale, slow(key_vectors), fast(k_other), slow(value_vectors), fast(v_other)),
            [low, sent],
            "states",
            flops=unit,
        )
        queries_late, cotangent_late, delta = lax.optimization_barrier((queries, cotangent, delta))
        q_other = swap(queries_late)
        c_other = swap(cotangent_late)
        state_in = scanned(delta, False)
        inside = local.call(
            inside_kernel,
            meta,
            pairs * 2 + [cols(rows)],
            cols(rows),
            (slow(queries), slow(q_other), slow(key_vectors), slow(k_other), slow(scaled)),
            wide,
            "inside",
            flops=4 * unit,
        )
        mixed, sums = local.call(
            mixed_kernel,
            meta,
            [shared(MEMBERS)] + pairs * 2 + [state(), cols(rows)],
            [cols(rows), local.whole((2, rows))],
            (out_scale, slow(queries), slow(q_other), slow(cotangent), slow(c_other), fast(state_in), slow(inside)),
            [wide, pltpu.VMEM((2, rows), F32)],
            "mixed",
            scratch=[pltpu.VMEM((rows, DH), F32)] * 2,
            flops=unit,
        )
        sums = over_heads(sums + turned(swap(sums), tok), tok)
        grad, delta_after = local.call(
            functools.partial(grads_kernel, full_width),
            meta,
            [shared(MEMBERS)] + pairs * 2 + [cols(rows), local.whole((2, rows))],
            [cols(rows), state()],
            (out_scale, slow(queries), slow(q_other), slow(cotangent), slow(c_other), slow(mixed), sums),
            [low, sent],
            "grads",
            flops=unit,
        )
        state_after = scanned(delta_after, True)
        query_own, query_send, key_in, value_in, out_part = local.call(
            functools.partial(back_kernel, full_width),
            meta,
            pairs * 3 + [cols(rows), cols(rows), state(), cols(rows), local.whole((2, rows))],
            [cols(tok), cols(tok), cols(rows), cols(rows), cols(MEMBERS)],
            (
                slow(queries), slow(q_other), slow(key_vectors), slow(k_other), slow(cotangent), slow(c_other),
                slow(scaled), slow(grad), slow(state_in), slow(mixed), sums,
            ),
            [half, half, wide, wide, part],
            "back",
            flops=11 * unit,
        )
        query_grad = side_by_side(core, query_own, swap(query_send))
        value_own, value_send, parts = local.call(
            value_kernel,
            meta,
            [shared(MEMBERS)] + pairs * 2 + [state(), cols(rows), cols(MEMBERS)],
            [cols(tok)] * 2 + [cols(2 * MEMBERS)],
            (
                in_scale, slow(key_vectors), slow(k_other), slow(value_vectors), slow(v_other),
                fast(state_after), slow(value_in), slow(out_part),
            ),
            [half] * 2 + [pltpu.HBM((2 * MEMBERS, width), F32)],
            "value",
            flops=unit,
        )
        copies = jnp.broadcast_to(parts.astype(BF16)[None], (chips,) + parts.shape)
        copies = lax.all_to_all(copies, "seq", 0, 0, axis_index_groups=same_core, tiled=True)
        key_own, key_send = local.call(
            key_kernel,
            meta,
            [cols(rows), state(), cols(rows)],
            [cols(tok)] * 2,
            (slow(scaled), slow(state_after), slow(key_in)),
            [half] * 2,
            "key",
            flops=unit,
        )
        key_grad = side_by_side(core, key_own, swap(key_send))
        value_grad = side_by_side(core, value_own, swap(value_send))
        copies, key_grad, value_grad, query_grad = lax.optimization_barrier(
            (copies, key_grad, value_grad, query_grad)
        )
        parts = jnp.sum(copies.astype(F32), axis=0)
        parts = side_by_side(core, parts, swap(parts))
        return query_grad, key_grad, value_grad, parts[:MEMBERS], parts[MEMBERS:]

    return shards


def solution(mesh):
    n_seq, n_head = mesh.shape["seq"], mesh.shape["head"]
    shards = make_shards(n_seq, n_head)
    placed = (
        P("seq", "head"),
        P("seq", "head"),
        P("seq", "head"),
        P("seq", "head"),
        P("seq"),
        P(None, "head"),
        P(None, "head"),
    )
    return jax.shard_map(
        shards,
        mesh=mesh,
        in_specs=placed,
        out_specs=(
            P("seq", "head"),
            P("seq", "head"),
            P("seq", "head"),
            P(None, "head"),
            P(None, "head"),
        ),
        check_vma=False,
    )
```

```python
import functools

import jax
import jax.numpy as jnp
from jax import lax
from jax.experimental import pallas as pl
from jax.experimental.pallas import tpu as pltpu
from jax.sharding import Mesh, PartitionSpec as P

DH = 128
SPAN = 16
MEMBERS = 4
EPS = 1e-06
CORES = 2
STEP_HEADS = 4
VMEM_BYTES = 24 * 2**20
F32 = jnp.float32
BF16 = jnp.bfloat16

NN = (((1,), (0,)), ((), ()))
NT = (((1,), (1,)), ((), ()))
TN = (((0,), (0,)), ((), ()))


class Meta:
    def __init__(self, place, own_ids, other_ids):
        self.core = place[0]
        self.ids = [own_ids[s] for s in range(own_ids.shape[0])]
        self.ids += [other_ids[s] for s in range(other_ids.shape[0])]


def with_meta(body):
    def kernel(place, own_ids, other_ids, *refs):
        body(Meta(place, own_ids, other_ids), *refs)

    return kernel


def dot(a, b, dims):
    return lax.dot_general(a, b, dims, preferred_element_type=F32)


def pair(own, other, lanes):
    return jnp.concatenate([own[:, lanes], other[:, lanes]], axis=0)


def rows_of_members(meta, scale, lanes, spans):
    choices = [scale[m : m + 1, lanes] for m in range(MEMBERS)]
    rows = []
    for s in range(spans):
        row = choices[0]
        for m in range(1, MEMBERS):
            row = jnp.where(meta.ids[s] == m, choices[m], row)
        rows.append(jnp.broadcast_to(row, (SPAN, DH)))
    return jnp.concatenate(rows, axis=0)


def member_sums(meta, x, spans):
    totals = [jnp.zeros((8, DH), F32) for _ in range(MEMBERS)]
    for s in range(spans):
        part = x[s * SPAN : s * SPAN + 8] + x[s * SPAN + 8 : (s + 1) * SPAN]
        for m in range(MEMBERS):
            keep = jnp.where(meta.ids[s] == m, 1.0, 0.0).astype(F32)
            totals[m] = totals[m] + keep * part
    return jnp.concatenate([jnp.sum(t, axis=0, keepdims=True) for t in totals], axis=0)


def causal_mask(meta, tok):
    size = 2 * tok
    core = meta.core
    base_own = core * tok
    base_other = (1 - core) * tok - tok

    def place(axis):
        at = lax.broadcasted_iota(jnp.int32, (size, size), axis)
        return at + jnp.where(at < tok, base_own, base_other)

    return place(0) >= place(1)


def in_order(meta, x, tok):
    turned = jnp.concatenate([x[:, tok:], x[:, :tok]], axis=1)
    return jnp.where(meta.core == 0, x, turned)


def head_sums(meta, sums, tok):
    total = sums[0]
    for at in range(1, sums.shape[0]):
        total = total + sums[at]
    return in_order(meta, total, tok)


def lanes_of(h):
    return pl.ds(h * DH, DH)


def states_kernel(meta, scale, k_own, k_other, v_own, v_other, scaled, delta):
    tok = k_own.shape[0]
    spans = 2 * tok // SPAN
    for h in range(delta.shape[0]):
        lanes = lanes_of(h)
        value = pair(v_own, v_other, lanes).astype(F32)
        low = (rows_of_members(meta, scale, lanes, spans) * value).astype(BF16)
        scaled[:, lanes] = low
        delta[h] = dot(pair(k_own, k_other, lanes), low, TN).astype(BF16)


def inside_kernel(meta, q_own, q_other, k_own, k_other, scaled, inside):
    tok = q_own.shape[0]
    causal = causal_mask(meta, tok)
    for h in range(scaled.shape[1] // DH):
        lanes = lanes_of(h)
        scores = dot(pair(q_own, q_other, lanes), pair(k_own, k_other, lanes), NT)
        weights = jnp.where(causal, scores, 0.0).astype(BF16)
        inside[:, lanes] = dot(weights, scaled[:, lanes], NN)


def mixed_kernel(
    meta, scale, q_own, q_other, c_own, c_other, state, inside, mixed, sums, squares, crosses
):
    tok = q_own.shape[0]
    spans = 2 * tok // SPAN
    step = pl.program_id(0)

    @pl.when(step == 0)
    def _():
        squares[...] = jnp.zeros_like(squares)
        crosses[...] = jnp.zeros_like(crosses)

    square, cross = squares[...], crosses[...]
    for h in range(state.shape[0]):
        lanes = lanes_of(h)
        mix = inside[:, lanes] + dot(pair(q_own, q_other, lanes), state[h], NN)
        mixed[:, lanes] = mix
        cot = pair(c_own, c_other, lanes).astype(F32)
        square = square + mix * mix
        cross = cross + rows_of_members(meta, scale, lanes, spans) * cot * mix
    squares[...] = square
    crosses[...] = cross

    @pl.when(step == pl.num_programs(0) - 1)
    def _():
        totals = [jnp.sum(jnp.transpose(t), axis=0, keepdims=True) for t in (square, cross)]
        totals = in_order(meta, jnp.concatenate(totals, axis=0), tok)
        sums[...] = jnp.broadcast_to(totals[None], sums.shape)


def grads_kernel(
    full_width, meta, scale, q_own, q_other, c_own, c_other, mixed, sums, grad, delta
):
    tok = q_own.shape[0]
    spans = 2 * tok // SPAN
    totals = head_sums(meta, sums, tok)
    rms = jnp.sqrt(totals[0:1] / full_width + EPS)
    inverse = 1.0 / rms
    factor = totals[1:2] / (full_width * rms * rms * rms)
    inverse = jnp.transpose(jnp.broadcast_to(inverse, (DH, 2 * tok)))
    factor = jnp.transpose(jnp.broadcast_to(factor, (DH, 2 * tok)))
    for h in range(delta.shape[0]):
        lanes = lanes_of(h)
        cot = pair(c_own, c_other, lanes).astype(F32) * inverse
        mix = mixed[:, lanes]
        low = (rows_of_members(meta, scale, lanes, spans) * cot - mix * factor).astype(BF16)
        grad[:, lanes] = low
        delta[h] = dot(pair(q_own, q_other, lanes), low, TN).astype(BF16)


def back_kernel(
    full_width, meta, q_own, q_other, k_own, k_other, c_own, c_other, scaled, grad, state, mixed, sums,
    query_own, query_other, key_in, value_in, out_part,
):
    tok = q_own.shape[0]
    spans = 2 * tok // SPAN
    causal = causal_mask(meta, tok)
    totals = head_sums(meta, sums, tok)
    inverse = 1.0 / jnp.sqrt(totals[0:1] / full_width + EPS)
    inverse = jnp.transpose(jnp.broadcast_to(inverse, (DH, 2 * tok)))
    for h in range(state.shape[0]):
        lanes = lanes_of(h)
        query = pair(q_own, q_other, lanes)
        key = pair(k_own, k_other, lanes)
        low = scaled[:, lanes]
        g = grad[:, lanes]
        weights = jnp.where(causal, dot(query, key, NT), 0.0).astype(BF16)
        grad_weights = jnp.where(causal, dot(g, low, NT), 0.0).astype(BF16)
        query_grad = (dot(grad_weights, key, NN) + dot(g, state[h], NT)).astype(BF16)
        query_own[:, lanes] = query_grad[:tok]
        query_other[:, lanes] = query_grad[tok:]
        key_in[:, lanes] = dot(grad_weights, query, TN)
        value_in[:, lanes] = dot(weights, g, TN)
        normed = pair(c_own, c_other, lanes).astype(F32) * (mixed[:, lanes] * inverse)
        out_part[:, lanes] = member_sums(meta, normed, spans)


def value_kernel(
    meta, scale, k_own, k_other, v_own, v_other, state, value_in, out_part,
    value_grad_own, value_grad_other, copies, parts,
):
    tok = k_own.shape[0]
    spans = 2 * tok // SPAN
    for h in range(state.shape[0]):
        lanes = lanes_of(h)
        scaled_grad = value_in[:, lanes] + dot(pair(k_own, k_other, lanes), state[h], NN)
        value_grad = (rows_of_members(meta, scale, lanes, spans) * scaled_grad).astype(BF16)
        value_grad_own[:, lanes] = value_grad[:tok]
        value_grad_other[:, lanes] = value_grad[tok:]
        value = pair(v_own, v_other, lanes).astype(F32)
        in_part = member_sums(meta, value * scaled_grad, spans)
        here = pl.ds(pl.multiple_of(pl.program_id(0) * 2 * MEMBERS, 2 * MEMBERS), 2 * MEMBERS)
        parts[here, lanes] = jnp.concatenate([in_part, out_part[:, lanes]], axis=0)

    @pl.when(pl.program_id(0) == pl.num_programs(0) - 1)
    def _():
        copies[...] = jnp.broadcast_to(parts[...].astype(BF16)[None], copies.shape)


def key_kernel(meta, scaled, state, key_in, key_grad_own, key_grad_other):
    tok = key_grad_own.shape[0]
    for h in range(state.shape[0]):
        lanes = lanes_of(h)
        key_grad = (key_in[:, lanes] + dot(scaled[:, lanes], state[h], NT)).astype(BF16)
        key_grad_own[:, lanes] = key_grad[:tok]
        key_grad_other[:, lanes] = key_grad[tok:]


def running_kernel(backward, pieces, sums):
    count = pieces.shape[0]
    total = jnp.zeros(pieces.shape[1:], F32)
    order = range(count - 1, -1, -1) if backward else range(count)
    for at in order:
        sums[at] = total.astype(BF16)
        total = total + pieces[at].astype(F32)


class Local:
    def __init__(self, tok, width):
        self.tok = tok
        self.width = width
        self.block = STEP_HEADS * DH
        self.steps = width // self.block

    def shared(self, rows):
        steps = self.steps
        return pl.BlockSpec((rows, self.block), lambda i, place, *_: (0, place[0] * steps + i))

    def cols(self, rows):
        return pl.BlockSpec((rows, self.block), lambda i, *_: (0, i))

    def state(self):
        return pl.BlockSpec((STEP_HEADS, DH, DH), lambda i, *_: (i, 0, 0))

    def whole(self, shape):
        return pl.BlockSpec(shape, lambda i, *_: (0,) * len(shape))

    def call(self, body, meta, ins, outs, args, shapes, name, scratch=(), flops=0):
        moved = sum(a.size * a.dtype.itemsize for a in args)
        return pl.pallas_call(
            with_meta(body),
            grid_spec=pltpu.PrefetchScalarGridSpec(
                num_scalar_prefetch=len(meta),
                grid=(self.steps,),
                in_specs=ins,
                out_specs=outs,
                scratch_shapes=scratch,
            ),
            out_shape=shapes,
            name=name,
            compiler_params=pltpu.CompilerParams(vmem_limit_bytes=VMEM_BYTES),
            cost_estimate=pl.CostEstimate(flops=flops, bytes_accessed=2 * moved, transcendentals=0),
        )(*meta, *args)


def fast(x):
    return pltpu.with_memory_space_constraint(x, pltpu.VMEM)


def slow(x):
    return pltpu.with_memory_space_constraint(x, pltpu.HBM)


def running_sums(pieces, backward):
    return pl.pallas_call(
        functools.partial(running_kernel, backward),
        out_shape=pltpu.HBM(pieces.shape, BF16),
        name="running_sums",
        compiler_params=pltpu.CompilerParams(vmem_limit_bytes=VMEM_BYTES),
    )(fast(pieces))


def make_shards(n_seq, n_head):
    chips = n_seq // CORES
    group = CORES * n_head

    def swap(x):
        return lax.ppermute(x, "core", [(0, 1), (1, 0)])

    def scattered(pieces):
        return lax.all_to_all(pieces, "chip", 0, 0, tiled=True)

    def scanned(delta, backward):
        heads = delta.shape[0]
        pieces = delta.reshape(chips, heads * DH // chips, DH)
        sums = scattered(running_sums(scattered(pieces), backward))
        return sums.reshape(heads, DH, DH)

    def side_by_side(core, own, other):
        return jnp.where(
            core == 0,
            jnp.concatenate([own, other], axis=1),
            jnp.concatenate([other, own], axis=1),
        )

    def shards(queries, key_vectors, value_vectors, cotangent, member_ids, in_scale, out_scale):
        tok, both = queries.shape
        width = both // CORES
        heads = width // DH
        full_width = both * n_head
        rows = 2 * tok
        core = lax.axis_index("core")

        other_ids = swap(member_ids)
        v_other = swap(value_vectors)
        k_other = swap(key_vectors)
        place = core[None].astype(jnp.int32)
        local = Local(tok, width)
        shared, cols, state = local.shared, local.cols, local.state
        half = pltpu.HBM((tok, width), BF16)
        low = pltpu.HBM((rows, width), BF16)
        wide = pltpu.HBM((rows, width), F32)
        part = pltpu.HBM((MEMBERS, width), F32)
        sent = pltpu.HBM((heads, DH, DH), BF16)
        pairs = [shared(tok), shared(tok)]
        packed = (chips, 2 * MEMBERS * local.steps, local.block)
        unit = 2 * heads * rows * DH * DH

        meta = (place, member_ids, other_ids)
        scaled, delta = local.call(
            states_kernel,
            meta,
            [shared(MEMBERS)] + pairs * 2,
            [cols(rows), state()],
            (in_scale, slow(key_vectors), fast(k_other), slow(value_vectors), fast(v_other)),
            [low, sent],
            "states",
            flops=unit,
        )
        queries_late, cotangent_late, delta = lax.optimization_barrier((queries, cotangent, delta))
        q_other = swap(queries_late)
        c_other = swap(cotangent_late)
        state_in = scanned(delta, False)
        inside = local.call(
            inside_kernel,
            meta,
            pairs * 2 + [cols(rows)],
            cols(rows),
            (slow(queries), slow(q_other), slow(key_vectors), slow(k_other), slow(scaled)),
            wide,
            "inside",
            flops=4 * unit,
        )
        mixed, sums = local.call(
            mixed_kernel,
            meta,
            [shared(MEMBERS)] + pairs * 2 + [state(), cols(rows)],
            [cols(rows), local.whole((group, 2, rows))],
            (out_scale, slow(queries), slow(q_other), slow(cotangent), slow(c_other), fast(state_in), slow(inside)),
            [wide, pltpu.HBM((group, 2, rows), F32)],
            "mixed",
            scratch=[pltpu.VMEM((rows, DH), F32)] * 2,
            flops=unit,
        )
        sums = lax.all_to_all(sums, ("core", "head"), 0, 0, tiled=True)
        grad, delta_after = local.call(
            functools.partial(grads_kernel, full_width),
            meta,
            [shared(MEMBERS)] + pairs * 2 + [cols(rows), local.whole((group, 2, rows))],
            [cols(rows), state()],
            (out_scale, slow(queries), slow(q_other), slow(cotangent), slow(c_other), slow(mixed), sums),
            [low, sent],
            "grads",
            flops=unit,
        )
        state_after = scanned(delta_after, True)
        query_own, query_send, key_in, value_in, out_part = local.call(
            functools.partial(back_kernel, full_width),
            meta,
            pairs * 3 + [cols(rows), cols(rows), state(), cols(rows), local.whole((group, 2, rows))],
            [cols(tok), cols(tok), cols(rows), cols(rows), cols(MEMBERS)],
            (
                slow(queries), slow(q_other), slow(key_vectors), slow(k_other), slow(cotangent), slow(c_other),
                slow(scaled), slow(grad), slow(state_in), slow(mixed), sums,
            ),
            [half, half, wide, wide, part],
            "back",
            flops=11 * unit,
        )
        query_grad = side_by_side(core, query_own, swap(query_send))
        value_own, value_send, copies = local.call(
            value_kernel,
            meta,
            [shared(MEMBERS)] + pairs * 2 + [state(), cols(rows), cols(MEMBERS)],
            [cols(tok)] * 2 + [local.whole(packed)],
            (
                in_scale, slow(key_vectors), slow(k_other), slow(value_vectors), slow(v_other),
                fast(state_after), slow(value_in), slow(out_part),
            ),
            [half] * 2 + [pltpu.HBM(packed, BF16)],
            "value",
            scratch=[pltpu.VMEM(packed[1:], F32)],
            flops=unit,
        )
        copies = scattered(copies)
        key_own, key_send = local.call(
            key_kernel,
            meta,
            [cols(rows), state(), cols(rows)],
            [cols(tok)] * 2,
            (slow(scaled), slow(state_after), slow(key_in)),
            [half] * 2,
            "key",
            flops=unit,
        )
        key_grad = side_by_side(core, key_own, swap(key_send))
        value_grad = side_by_side(core, value_own, swap(value_send))
        copies, key_grad, value_grad, query_grad = lax.optimization_barrier(
            (copies, key_grad, value_grad, query_grad)
        )
        parts = jnp.sum(copies.astype(F32), axis=0)
        each = 2 * MEMBERS
        parts = jnp.concatenate([parts[i * each : (i + 1) * each] for i in range(local.steps)], axis=1)
        parts = side_by_side(core, parts, swap(parts))
        return query_grad, key_grad, value_grad, parts[:MEMBERS], parts[MEMBERS:]

    return shards


def solution(mesh):
    n_seq, n_head = mesh.shape["seq"], mesh.shape["head"]
    chips = n_seq // CORES
    finer = Mesh(mesh.devices.reshape(chips, CORES, n_head), ("chip", "core", "head"))
    tokens = ("chip", "core")
    wide = P(tokens, "head")
    scale = P(None, "head")
    return jax.shard_map(
        make_shards(n_seq, n_head),
        mesh=finer,
        in_specs=(wide, wide, wide, wide, P(tokens), scale, scale),
        out_specs=(wide, wide, wide, scale, scale),
        check_vma=False,
    )
```

```python
import functools

import jax
import jax.numpy as jnp
from jax import lax
from jax.experimental import pallas as pl
from jax.experimental.pallas import tpu as pltpu
from jax.sharding import Mesh, PartitionSpec as P

DH = 128
SPAN = 16
MEMBERS = 4
EPS = 1e-06
CORES = 2
STEP_HEADS = 4
VMEM_BYTES = 24 * 2**20
F32 = jnp.float32
BF16 = jnp.bfloat16

NN = (((1,), (0,)), ((), ()))
NT = (((1,), (1,)), ((), ()))
TN = (((0,), (0,)), ((), ()))


class Meta:
    def __init__(self, place, own_ids, other_ids):
        self.core = place[0]
        self.ids = [own_ids[s] for s in range(own_ids.shape[0])]
        self.ids += [other_ids[s] for s in range(other_ids.shape[0])]


def with_meta(body):
    def kernel(place, own_ids, other_ids, *refs):
        body(Meta(place, own_ids, other_ids), *refs)

    return kernel


def dot(a, b, dims):
    return lax.dot_general(a, b, dims, preferred_element_type=F32)


def pair(own, other, lanes):
    return jnp.concatenate([own[:, lanes], other[:, lanes]], axis=0)


def rows_of_members(meta, scale, lanes, spans):
    choices = [scale[m : m + 1, lanes] for m in range(MEMBERS)]
    rows = []
    for s in range(spans):
        row = choices[0]
        for m in range(1, MEMBERS):
            row = jnp.where(meta.ids[s] == m, choices[m], row)
        rows.append(jnp.broadcast_to(row, (SPAN, DH)))
    return jnp.concatenate(rows, axis=0)


def member_sums(meta, x, spans):
    totals = [jnp.zeros((8, DH), F32) for _ in range(MEMBERS)]
    for s in range(spans):
        part = x[s * SPAN : s * SPAN + 8] + x[s * SPAN + 8 : (s + 1) * SPAN]
        for m in range(MEMBERS):
            keep = jnp.where(meta.ids[s] == m, 1.0, 0.0).astype(F32)
            totals[m] = totals[m] + keep * part
    return jnp.concatenate([jnp.sum(t, axis=0, keepdims=True) for t in totals], axis=0)


def causal_mask(meta, tok):
    size = 2 * tok
    core = meta.core
    base_own = core * tok
    base_other = (1 - core) * tok - tok

    def place(axis):
        at = lax.broadcasted_iota(jnp.int32, (size, size), axis)
        return at + jnp.where(at < tok, base_own, base_other)

    return place(0) >= place(1)


def in_order(meta, x, tok):
    turned = jnp.concatenate([x[:, tok:], x[:, :tok]], axis=1)
    return jnp.where(meta.core == 0, x, turned)


def head_sums(meta, sums, tok):
    total = sums[0]
    for at in range(1, sums.shape[0]):
        total = total + sums[at]
    return in_order(meta, total, tok)


def lanes_of(h):
    return pl.ds(h * DH, DH)


def states_kernel(meta, scale, k_own, k_other, v_own, v_other, scaled, delta):
    tok = k_own.shape[0]
    spans = 2 * tok // SPAN
    for h in range(delta.shape[0]):
        lanes = lanes_of(h)
        value = pair(v_own, v_other, lanes).astype(F32)
        low = (rows_of_members(meta, scale, lanes, spans) * value).astype(BF16)
        scaled[:, lanes] = low
        delta[h] = dot(pair(k_own, k_other, lanes), low, TN).astype(BF16)


def inside_kernel(meta, q_own, q_other, k_own, k_other, scaled, inside):
    tok = q_own.shape[0]
    causal = causal_mask(meta, tok)
    for h in range(scaled.shape[1] // DH):
        lanes = lanes_of(h)
        scores = dot(pair(q_own, q_other, lanes), pair(k_own, k_other, lanes), NT)
        weights = jnp.where(causal, scores, 0.0).astype(BF16)
        inside[:, lanes] = dot(weights, scaled[:, lanes], NN)


def mixed_kernel(
    meta, scale, q_own, q_other, c_own, c_other, state, inside, mixed, sums, squares, crosses
):
    tok = q_own.shape[0]
    spans = 2 * tok // SPAN
    step = pl.program_id(0)

    @pl.when(step == 0)
    def _():
        squares[...] = jnp.zeros_like(squares)
        crosses[...] = jnp.zeros_like(crosses)

    square, cross = squares[...], crosses[...]
    for h in range(state.shape[0]):
        lanes = lanes_of(h)
        mix = inside[:, lanes] + dot(pair(q_own, q_other, lanes), state[h], NN)
        mixed[:, lanes] = mix
        cot = pair(c_own, c_other, lanes).astype(F32)
        square = square + mix * mix
        cross = cross + rows_of_members(meta, scale, lanes, spans) * cot * mix
    squares[...] = square
    crosses[...] = cross

    @pl.when(step == pl.num_programs(0) - 1)
    def _():
        totals = [jnp.sum(jnp.transpose(t), axis=0, keepdims=True) for t in (square, cross)]
        totals = in_order(meta, jnp.concatenate(totals, axis=0), tok)
        sums[...] = jnp.broadcast_to(totals[None], sums.shape)


def grads_kernel(
    full_width, meta, scale, q_own, q_other, c_own, c_other, mixed, sums, grad, delta, turned
):
    tok = q_own.shape[0]
    spans = 2 * tok // SPAN

    @pl.when(pl.program_id(0) == 0)
    def _():
        totals = head_sums(meta, sums, tok)
        rms = jnp.sqrt(totals[0:1] / full_width + EPS)
        turned[0] = jnp.transpose(jnp.broadcast_to(1.0 / rms, (DH, 2 * tok)))
        factor = totals[1:2] / (full_width * rms * rms * rms)
        turned[1] = jnp.transpose(jnp.broadcast_to(factor, (DH, 2 * tok)))

    inverse, factor = turned[0], turned[1]
    for h in range(delta.shape[0]):
        lanes = lanes_of(h)
        cot = pair(c_own, c_other, lanes).astype(F32) * inverse
        mix = mixed[:, lanes]
        low = (rows_of_members(meta, scale, lanes, spans) * cot - mix * factor).astype(BF16)
        grad[:, lanes] = low
        delta[h] = dot(pair(q_own, q_other, lanes), low, TN).astype(BF16)


def back_kernel(
    full_width, meta, q_own, q_other, k_own, k_other, v_own, v_other, c_own, c_other,
    scaled, grad, state, mixed, sums,
    query_own, query_other, key_in, value_in, parts,
):
    tok = q_own.shape[0]
    spans = 2 * tok // SPAN
    causal = causal_mask(meta, tok)
    totals = head_sums(meta, sums, tok)
    inverse = 1.0 / jnp.sqrt(totals[0:1] / full_width + EPS)
    inverse = jnp.transpose(jnp.broadcast_to(inverse, (DH, 2 * tok)))
    for h in range(state.shape[0]):
        lanes = lanes_of(h)
        query = pair(q_own, q_other, lanes)
        key = pair(k_own, k_other, lanes)
        low = scaled[:, lanes]
        g = grad[:, lanes]
        weights = jnp.where(causal, dot(query, key, NT), 0.0).astype(BF16)
        grad_weights = jnp.where(causal, dot(g, low, NT), 0.0).astype(BF16)
        query_grad = (dot(grad_weights, key, NN) + dot(g, state[h], NT)).astype(BF16)
        query_own[:, lanes] = query_grad[:tok]
        query_other[:, lanes] = query_grad[tok:]
        key_in[:, lanes] = dot(grad_weights, query, TN)
        inner = dot(weights, g, TN)
        value_in[:, lanes] = inner
        in_part = member_sums(meta, pair(v_own, v_other, lanes).astype(F32) * inner, spans)
        normed = pair(c_own, c_other, lanes).astype(F32) * (mixed[:, lanes] * inverse)
        out_part = member_sums(meta, normed, spans)
        parts[:, lanes] = jnp.concatenate([in_part, out_part], axis=0)


def copies_kernel(meta, k_own, k_other, v_own, v_other, state, known, copies, parts):
    tok = k_own.shape[0]
    spans = 2 * tok // SPAN
    here = pl.ds(pl.multiple_of(pl.program_id(0) * 2 * MEMBERS, 2 * MEMBERS), 2 * MEMBERS)
    for h in range(state.shape[0]):
        lanes = lanes_of(h)
        value = pair(v_own, v_other, lanes).astype(F32)
        across = dot(pair(k_own, k_other, lanes), state[h], NN)
        in_part = member_sums(meta, value * across, spans)
        more = jnp.concatenate([in_part, jnp.zeros_like(in_part)], axis=0)
        parts[here, lanes] = known[:, lanes] + more

    @pl.when(pl.program_id(0) == pl.num_programs(0) - 1)
    def _():
        copies[...] = jnp.broadcast_to(parts[...].astype(BF16)[None], copies.shape)


def last_kernel(
    meta, scale, k_own, k_other, scaled, state, key_in, value_in,
    key_grad_own, key_grad_other, value_grad_own, value_grad_other,
):
    tok = k_own.shape[0]
    spans = 2 * tok // SPAN
    for h in range(state.shape[0]):
        lanes = lanes_of(h)
        key_grad = (key_in[:, lanes] + dot(scaled[:, lanes], state[h], NT)).astype(BF16)
        key_grad_own[:, lanes] = key_grad[:tok]
        key_grad_other[:, lanes] = key_grad[tok:]
        scaled_grad = value_in[:, lanes] + dot(pair(k_own, k_other, lanes), state[h], NN)
        value_grad = (rows_of_members(meta, scale, lanes, spans) * scaled_grad).astype(BF16)
        value_grad_own[:, lanes] = value_grad[:tok]
        value_grad_other[:, lanes] = value_grad[tok:]


def running_kernel(backward, pieces, sums):
    count = pieces.shape[0]
    total = jnp.zeros(pieces.shape[1:], F32)
    order = range(count - 1, -1, -1) if backward else range(count)
    for at in order:
        sums[at] = total.astype(BF16)
        total = total + pieces[at].astype(F32)


class Local:
    def __init__(self, tok, width):
        self.tok = tok
        self.width = width
        self.block = STEP_HEADS * DH
        self.steps = width // self.block

    def shared(self, rows):
        steps = self.steps
        return pl.BlockSpec((rows, self.block), lambda i, place, *_: (0, place[0] * steps + i))

    def cols(self, rows):
        return pl.BlockSpec((rows, self.block), lambda i, *_: (0, i))

    def state(self):
        return pl.BlockSpec((STEP_HEADS, DH, DH), lambda i, *_: (i, 0, 0))

    def whole(self, shape):
        return pl.BlockSpec(shape, lambda i, *_: (0,) * len(shape))

    def call(self, body, meta, ins, outs, args, shapes, name, scratch=(), flops=0):
        moved = sum(a.size * a.dtype.itemsize for a in args)
        return pl.pallas_call(
            with_meta(body),
            grid_spec=pltpu.PrefetchScalarGridSpec(
                num_scalar_prefetch=len(meta),
                grid=(self.steps,),
                in_specs=ins,
                out_specs=outs,
                scratch_shapes=scratch,
            ),
            out_shape=shapes,
            name=name,
            compiler_params=pltpu.CompilerParams(vmem_limit_bytes=VMEM_BYTES),
            cost_estimate=pl.CostEstimate(flops=flops, bytes_accessed=2 * moved, transcendentals=0),
        )(*meta, *args)


def fast(x):
    return pltpu.with_memory_space_constraint(x, pltpu.VMEM)


def slow(x):
    return pltpu.with_memory_space_constraint(x, pltpu.HBM)


def running_sums(pieces, backward):
    return pl.pallas_call(
        functools.partial(running_kernel, backward),
        out_shape=pltpu.HBM(pieces.shape, BF16),
        name="running_sums",
        compiler_params=pltpu.CompilerParams(vmem_limit_bytes=VMEM_BYTES),
    )(fast(pieces))


def make_shards(n_seq, n_head):
    chips = n_seq // CORES
    group = CORES * n_head

    def swap(x):
        return lax.ppermute(x, "core", [(0, 1), (1, 0)])

    def scattered(pieces):
        return lax.all_to_all(pieces, "chip", 0, 0, tiled=True)

    def scanned(delta, backward):
        heads = delta.shape[0]
        pieces = delta.reshape(chips, heads * DH // chips, DH)
        sums = scattered(running_sums(scattered(pieces), backward))
        return sums.reshape(heads, DH, DH)

    def side_by_side(core, own, other):
        return jnp.where(
            core == 0,
            jnp.concatenate([own, other], axis=1),
            jnp.concatenate([other, own], axis=1),
        )

    def shards(queries, key_vectors, value_vectors, cotangent, member_ids, in_scale, out_scale):
        tok, both = queries.shape
        width = both // CORES
        heads = width // DH
        full_width = both * n_head
        rows = 2 * tok
        core = lax.axis_index("core")

        other_ids = swap(member_ids)
        v_other = swap(value_vectors)
        k_other = swap(key_vectors)
        place = core[None].astype(jnp.int32)
        local = Local(tok, width)
        shared, cols, state = local.shared, local.cols, local.state
        half = pltpu.HBM((tok, width), BF16)
        low = pltpu.HBM((rows, width), BF16)
        wide = pltpu.HBM((rows, width), F32)
        part = pltpu.HBM((2 * MEMBERS, width), F32)
        sent = pltpu.HBM((heads, DH, DH), BF16)
        pairs = [shared(tok), shared(tok)]
        packed = (chips, 2 * MEMBERS * local.steps, local.block)
        unit = 2 * heads * rows * DH * DH

        meta = (place, member_ids, other_ids)
        scaled, delta = local.call(
            states_kernel,
            meta,
            [shared(MEMBERS)] + pairs * 2,
            [cols(rows), state()],
            (slow(in_scale), slow(key_vectors), fast(k_other), slow(value_vectors), fast(v_other)),
            [low, sent],
            "states",
            flops=unit,
        )
        queries_late, cotangent_late, delta = lax.optimization_barrier((queries, cotangent, delta))
        q_other = swap(queries_late)
        c_other = swap(cotangent_late)
        state_in = scanned(delta, False)
        inside = local.call(
            inside_kernel,
            meta,
            pairs * 2 + [cols(rows)],
            cols(rows),
            (slow(queries), slow(q_other), slow(key_vectors), slow(k_other), slow(scaled)),
            wide,
            "inside",
            flops=4 * unit,
        )
        mixed, sums = local.call(
            mixed_kernel,
            meta,
            [shared(MEMBERS)] + pairs * 2 + [state(), cols(rows)],
            [cols(rows), local.whole((group, 2, rows))],
            (slow(out_scale), slow(queries), slow(q_other), slow(cotangent), slow(c_other), fast(state_in), slow(inside)),
            [wide, pltpu.HBM((group, 2, rows), F32)],
            "mixed",
            scratch=[pltpu.VMEM((rows, DH), F32)] * 2,
            flops=unit,
        )
        sums = lax.all_to_all(sums, ("core", "head"), 0, 0, tiled=True)
        grad, delta_after = local.call(
            functools.partial(grads_kernel, full_width),
            meta,
            [shared(MEMBERS)] + pairs * 2 + [cols(rows), local.whole((group, 2, rows))],
            [cols(rows), state()],
            (slow(out_scale), slow(queries), slow(q_other), slow(cotangent), slow(c_other), slow(mixed), sums),
            [low, sent],
            "grads",
            scratch=[pltpu.VMEM((2, rows, DH), F32)],
            flops=unit,
        )
        state_after = scanned(delta_after, True)
        query_own, query_send, key_in, value_in, parts = local.call(
            functools.partial(back_kernel, full_width),
            meta,
            pairs * 4 + [cols(rows), cols(rows), state(), cols(rows), local.whole((group, 2, rows))],
            [cols(tok), cols(tok), cols(rows), cols(rows), cols(2 * MEMBERS)],
            (
                slow(queries), slow(q_other), slow(key_vectors), slow(k_other),
                slow(value_vectors), slow(v_other), slow(cotangent), slow(c_other),
                slow(scaled), slow(grad), slow(state_in), slow(mixed), sums,
            ),
            [half, half, wide, wide, part],
            "back",
            flops=11 * unit,
        )
        query_grad = side_by_side(core, query_own, swap(query_send))
        copies = local.call(
            copies_kernel,
            meta,
            pairs * 2 + [state(), cols(2 * MEMBERS)],
            local.whole(packed),
            (
                slow(key_vectors), slow(k_other), slow(value_vectors), slow(v_other),
                fast(state_after), slow(parts),
            ),
            pltpu.HBM(packed, BF16),
            "copies",
            scratch=[pltpu.VMEM(packed[1:], F32)],
            flops=unit,
        )
        copies = scattered(copies)
        key_own, key_send, value_own, value_send = local.call(
            last_kernel,
            meta,
            [shared(MEMBERS)] + pairs + [cols(rows), state(), cols(rows), cols(rows)],
            [cols(tok)] * 4,
            (
                slow(in_scale), slow(key_vectors), slow(k_other), slow(scaled),
                slow(state_after), slow(key_in), slow(value_in),
            ),
            [half] * 4,
            "last",
            flops=2 * unit,
        )
        key_grad = side_by_side(core, key_own, swap(key_send))
        value_grad = side_by_side(core, value_own, swap(value_send))
        copies, key_grad, value_grad, query_grad = lax.optimization_barrier(
            (copies, key_grad, value_grad, query_grad)
        )
        parts = jnp.sum(copies.astype(F32), axis=0)
        each = 2 * MEMBERS
        parts = jnp.concatenate([parts[i * each : (i + 1) * each] for i in range(local.steps)], axis=1)
        parts = side_by_side(core, parts, swap(parts))
        return query_grad, key_grad, value_grad, parts[:MEMBERS], parts[MEMBERS:]

    return shards


def solution(mesh):
    n_seq, n_head = mesh.shape["seq"], mesh.shape["head"]
    chips = n_seq // CORES
    finer = Mesh(mesh.devices.reshape(chips, CORES, n_head), ("chip", "core", "head"))
    tokens = ("chip", "core")
    wide = P(tokens, "head")
    scale = P(None, "head")
    return jax.shard_map(
        make_shards(n_seq, n_head),
        mesh=finer,
        in_specs=(wide, wide, wide, wide, P(tokens), scale, scale),
        out_specs=(wide, wide, wide, scale, scale),
        check_vma=False,
    )
```

```python
import functools

import jax
import jax.numpy as jnp
from jax import lax
from jax.experimental import pallas as pl
from jax.experimental.pallas import tpu as pltpu
from jax.sharding import Mesh, PartitionSpec as P

DH = 128
SPAN = 16
MEMBERS = 4
EPS = 1e-06
CORES = 2
STEP_HEADS = 4
VMEM_BYTES = 24 * 2**20
F32 = jnp.float32
BF16 = jnp.bfloat16

NN = (((1,), (0,)), ((), ()))
NT = (((1,), (1,)), ((), ()))
TN = (((0,), (0,)), ((), ()))


class Meta:
    def __init__(self, place, own_ids, other_ids):
        self.core = place[0]
        self.ids = [own_ids[s] for s in range(own_ids.shape[0])]
        self.ids += [other_ids[s] for s in range(other_ids.shape[0])]


def with_meta(body):
    def kernel(place, own_ids, other_ids, *refs):
        body(Meta(place, own_ids, other_ids), *refs)

    return kernel


def dot(a, b, dims):
    return lax.dot_general(a, b, dims, preferred_element_type=F32)


def pair(own, other, lanes):
    return jnp.concatenate([own[:, lanes], other[:, lanes]], axis=0)


def rows_of_members(meta, scale, lanes, spans):
    choices = [scale[m : m + 1, lanes] for m in range(MEMBERS)]
    rows = []
    for s in range(spans):
        row = choices[0]
        for m in range(1, MEMBERS):
            row = jnp.where(meta.ids[s] == m, choices[m], row)
        rows.append(jnp.broadcast_to(row, (SPAN, DH)))
    return jnp.concatenate(rows, axis=0)


def member_sums(meta, x, spans):
    totals = [jnp.zeros((8, DH), F32) for _ in range(MEMBERS)]
    for s in range(spans):
        part = x[s * SPAN : s * SPAN + 8] + x[s * SPAN + 8 : (s + 1) * SPAN]
        for m in range(MEMBERS):
            keep = jnp.where(meta.ids[s] == m, 1.0, 0.0).astype(F32)
            totals[m] = totals[m] + keep * part
    return jnp.concatenate([jnp.sum(t, axis=0, keepdims=True) for t in totals], axis=0)


def causal_mask(meta, tok):
    size = 2 * tok
    core = meta.core
    base_own = core * tok
    base_other = (1 - core) * tok - tok

    def place(axis):
        at = lax.broadcasted_iota(jnp.int32, (size, size), axis)
        return at + jnp.where(at < tok, base_own, base_other)

    return place(0) >= place(1)


def in_order(meta, x, tok):
    turned = jnp.concatenate([x[:, tok:], x[:, :tok]], axis=1)
    return jnp.where(meta.core == 0, x, turned)


def head_sums(meta, sums, tok):
    total = sums[0]
    for at in range(1, sums.shape[0]):
        total = total + sums[at]
    return in_order(meta, total, tok)


def lanes_of(h):
    return pl.ds(h * DH, DH)


def states_kernel(meta, scale, k_own, k_other, v_own, v_other, scaled, delta):
    tok = k_own.shape[0]
    spans = 2 * tok // SPAN
    for h in range(delta.shape[0]):
        lanes = lanes_of(h)
        value = pair(v_own, v_other, lanes).astype(F32)
        low = (rows_of_members(meta, scale, lanes, spans) * value).astype(BF16)
        scaled[:, lanes] = low
        delta[h] = dot(pair(k_own, k_other, lanes), low, TN).astype(BF16)


def inside_kernel(
    meta, q_own, q_other, k_own, k_other, v_own, v_other, c_own, c_other, scaled,
    inside, q, k, v, c,
):
    tok = q_own.shape[0]
    causal = causal_mask(meta, tok)
    for both, own, other in ((q, q_own, q_other), (k, k_own, k_other), (v, v_own, v_other), (c, c_own, c_other)):
        both[:tok] = own[...]
        both[tok:] = other[...]
    for h in range(scaled.shape[1] // DH):
        lanes = lanes_of(h)
        scores = dot(q[:, lanes], k[:, lanes], NT)
        weights = jnp.where(causal, scores, 0.0).astype(BF16)
        inside[:, lanes] = dot(weights, scaled[:, lanes], NN)


def mixed_kernel(
    meta, scale, q, c, state, inside, mixed, sums, squares, crosses
):
    rows = q.shape[0]
    tok = rows // 2
    spans = rows // SPAN
    step = pl.program_id(0)

    @pl.when(step == 0)
    def _():
        squares[...] = jnp.zeros_like(squares)
        crosses[...] = jnp.zeros_like(crosses)

    square, cross = squares[...], crosses[...]
    for h in range(state.shape[0]):
        lanes = lanes_of(h)
        mix = inside[:, lanes] + dot(q[:, lanes], state[h], NN)
        mixed[:, lanes] = mix
        cot = c[:, lanes].astype(F32)
        square = square + mix * mix
        cross = cross + rows_of_members(meta, scale, lanes, spans) * cot * mix
    squares[...] = square
    crosses[...] = cross

    @pl.when(step == pl.num_programs(0) - 1)
    def _():
        totals = [jnp.sum(jnp.transpose(t), axis=0, keepdims=True) for t in (square, cross)]
        totals = in_order(meta, jnp.concatenate(totals, axis=0), tok)
        sums[...] = jnp.broadcast_to(totals[None], sums.shape)


def grads_kernel(
    full_width, meta, scale, q, c, mixed, sums, grad, delta, turned
):
    rows = q.shape[0]
    tok = rows // 2
    spans = rows // SPAN

    @pl.when(pl.program_id(0) == 0)
    def _():
        totals = head_sums(meta, sums, tok)
        rms = jnp.sqrt(totals[0:1] / full_width + EPS)
        turned[0] = jnp.transpose(jnp.broadcast_to(1.0 / rms, (DH, 2 * tok)))
        factor = totals[1:2] / (full_width * rms * rms * rms)
        turned[1] = jnp.transpose(jnp.broadcast_to(factor, (DH, 2 * tok)))

    inverse, factor = turned[0], turned[1]
    for h in range(delta.shape[0]):
        lanes = lanes_of(h)
        cot = c[:, lanes].astype(F32) * inverse
        mix = mixed[:, lanes]
        low = (rows_of_members(meta, scale, lanes, spans) * cot - mix * factor).astype(BF16)
        grad[:, lanes] = low
        delta[h] = dot(q[:, lanes], low, TN).astype(BF16)


def query_kernel(meta, k, scaled, grad, state, query_own, query_other):
    tok = k.shape[0] // 2
    causal = causal_mask(meta, tok)
    for h in range(state.shape[0]):
        lanes = lanes_of(h)
        g = grad[:, lanes]
        grad_weights = jnp.where(causal, dot(g, scaled[:, lanes], NT), 0.0).astype(BF16)
        query_grad = (dot(grad_weights, k[:, lanes], NN) + dot(g, state[h], NT)).astype(BF16)
        query_own[:, lanes] = query_grad[:tok]
        query_other[:, lanes] = query_grad[tok:]


def back_kernel(full_width, meta, q, k, v, c, scaled, grad, mixed, sums, key_in, value_in, parts):
    rows = k.shape[0]
    tok = rows // 2
    spans = rows // SPAN
    causal = causal_mask(meta, tok)
    totals = head_sums(meta, sums, tok)
    inverse = 1.0 / jnp.sqrt(totals[0:1] / full_width + EPS)
    inverse = jnp.transpose(jnp.broadcast_to(inverse, (DH, rows)))
    for h in range(scaled.shape[1] // DH):
        lanes = lanes_of(h)
        query, g = q[:, lanes], grad[:, lanes]
        weights = jnp.where(causal, dot(query, k[:, lanes], NT), 0.0).astype(BF16)
        grad_weights = jnp.where(causal, dot(g, scaled[:, lanes], NT), 0.0).astype(BF16)
        key_in[:, lanes] = dot(grad_weights, query, TN)
        inner = dot(weights, g, TN)
        value_in[:, lanes] = inner
        in_part = member_sums(meta, v[:, lanes].astype(F32) * inner, spans)
        normed = c[:, lanes].astype(F32) * (mixed[:, lanes] * inverse)
        out_part = member_sums(meta, normed, spans)
        parts[:, lanes] = jnp.concatenate([in_part, out_part], axis=0)


def copies_kernel(meta, k, v, state, known, copies, parts):
    rows = k.shape[0]
    tok = rows // 2
    spans = rows // SPAN
    here = pl.ds(pl.multiple_of(pl.program_id(0) * 2 * MEMBERS, 2 * MEMBERS), 2 * MEMBERS)
    for h in range(state.shape[0]):
        lanes = lanes_of(h)
        value = v[:, lanes].astype(F32)
        across = dot(k[:, lanes], state[h], NN)
        in_part = member_sums(meta, value * across, spans)
        more = jnp.concatenate([in_part, jnp.zeros_like(in_part)], axis=0)
        parts[here, lanes] = known[:, lanes] + more

    @pl.when(pl.program_id(0) == pl.num_programs(0) - 1)
    def _():
        copies[...] = jnp.broadcast_to(parts[...].astype(BF16)[None], copies.shape)


def last_kernel(
    meta, scale, k, scaled, state, key_in, value_in,
    key_grad_own, key_grad_other, value_grad_own, value_grad_other,
):
    rows = k.shape[0]
    tok = rows // 2
    spans = rows // SPAN
    for h in range(state.shape[0]):
        lanes = lanes_of(h)
        key_grad = (key_in[:, lanes] + dot(scaled[:, lanes], state[h], NT)).astype(BF16)
        key_grad_own[:, lanes] = key_grad[:tok]
        key_grad_other[:, lanes] = key_grad[tok:]
        scaled_grad = value_in[:, lanes] + dot(k[:, lanes], state[h], NN)
        value_grad = (rows_of_members(meta, scale, lanes, spans) * scaled_grad).astype(BF16)
        value_grad_own[:, lanes] = value_grad[:tok]
        value_grad_other[:, lanes] = value_grad[tok:]


def running_kernel(backward, pieces, sums):
    count = pieces.shape[0]
    total = jnp.zeros(pieces.shape[1:], F32)
    order = range(count - 1, -1, -1) if backward else range(count)
    for at in order:
        sums[at] = total.astype(BF16)
        total = total + pieces[at].astype(F32)


class Local:
    def __init__(self, tok, width):
        self.tok = tok
        self.width = width
        self.block = STEP_HEADS * DH
        self.steps = width // self.block

    def shared(self, rows):
        steps = self.steps
        return pl.BlockSpec((rows, self.block), lambda i, place, *_: (0, place[0] * steps + i))

    def cols(self, rows):
        return pl.BlockSpec((rows, self.block), lambda i, *_: (0, i))

    def state(self):
        return pl.BlockSpec((STEP_HEADS, DH, DH), lambda i, *_: (i, 0, 0))

    def whole(self, shape):
        return pl.BlockSpec(shape, lambda i, *_: (0,) * len(shape))

    def call(self, body, meta, ins, outs, args, shapes, name, scratch=(), flops=0):
        moved = sum(a.size * a.dtype.itemsize for a in args)
        return pl.pallas_call(
            with_meta(body),
            grid_spec=pltpu.PrefetchScalarGridSpec(
                num_scalar_prefetch=len(meta),
                grid=(self.steps,),
                in_specs=ins,
                out_specs=outs,
                scratch_shapes=scratch,
            ),
            out_shape=shapes,
            name=name,
            compiler_params=pltpu.CompilerParams(vmem_limit_bytes=VMEM_BYTES),
            cost_estimate=pl.CostEstimate(flops=flops, bytes_accessed=2 * moved, transcendentals=0),
        )(*meta, *args)


def fast(x):
    return pltpu.with_memory_space_constraint(x, pltpu.VMEM)


def slow(x):
    return pltpu.with_memory_space_constraint(x, pltpu.HBM)


def running_sums(pieces, backward):
    return pl.pallas_call(
        functools.partial(running_kernel, backward),
        out_shape=pltpu.HBM(pieces.shape, BF16),
        name="running_sums",
        compiler_params=pltpu.CompilerParams(vmem_limit_bytes=VMEM_BYTES),
    )(fast(pieces))


def make_shards(n_seq, n_head):
    chips = n_seq // CORES
    group = CORES * n_head

    def swap(x):
        return lax.ppermute(x, "core", [(0, 1), (1, 0)])

    def scattered(pieces):
        return lax.all_to_all(pieces, "chip", 0, 0, tiled=True)

    def scanned(delta, backward, beside=None):
        heads = delta.shape[0]
        pieces = scattered(delta.reshape(chips, heads * DH // chips, DH))
        if beside is not None:
            pieces, beside = lax.optimization_barrier((pieces, beside))
        state = scattered(running_sums(pieces, backward)).reshape(heads, DH, DH)
        return state if beside is None else (state, beside)

    def side_by_side(core, own, other):
        return jnp.where(
            core == 0,
            jnp.concatenate([own, other], axis=1),
            jnp.concatenate([other, own], axis=1),
        )

    def shards(queries, key_vectors, value_vectors, cotangent, member_ids, in_scale, out_scale):
        tok, both = queries.shape
        width = both // CORES
        heads = width // DH
        full_width = both * n_head
        rows = 2 * tok
        core = lax.axis_index("core")

        other_ids = swap(member_ids)
        v_other = swap(value_vectors)
        k_other = swap(key_vectors)
        place = core[None].astype(jnp.int32)
        local = Local(tok, width)
        shared, cols, state = local.shared, local.cols, local.state
        half = pltpu.HBM((tok, width), BF16)
        low = pltpu.HBM((rows, width), BF16)
        wide = pltpu.HBM((rows, width), F32)
        part = pltpu.HBM((2 * MEMBERS, width), F32)
        sent = pltpu.HBM((heads, DH, DH), BF16)
        pairs = [shared(tok), shared(tok)]
        packed = (chips, 2 * MEMBERS * local.steps, local.block)
        unit = 2 * heads * rows * DH * DH

        meta = (place, member_ids, other_ids)
        scaled, delta = local.call(
            states_kernel,
            meta,
            [shared(MEMBERS)] + pairs * 2,
            [cols(rows), state()],
            (slow(in_scale), slow(key_vectors), fast(k_other), slow(value_vectors), fast(v_other)),
            [low, sent],
            "states",
            flops=unit,
        )
        queries_late, cotangent_late, delta = lax.optimization_barrier((queries, cotangent, delta))
        q_other = swap(queries_late)
        c_other = swap(cotangent_late)
        state_in = scanned(delta, False)
        inside, q, k, v, c = local.call(
            inside_kernel,
            meta,
            pairs * 4 + [cols(rows)],
            [cols(rows)] * 5,
            (
                slow(queries), slow(q_other), slow(key_vectors), slow(k_other),
                slow(value_vectors), slow(v_other), slow(cotangent), slow(c_other), slow(scaled),
            ),
            [wide] + [low] * 4,
            "inside",
            flops=4 * unit,
        )
        q, k, v, c = slow(q), slow(k), slow(v), slow(c)
        mixed, sums = local.call(
            mixed_kernel,
            meta,
            [shared(MEMBERS), cols(rows), cols(rows), state(), cols(rows)],
            [cols(rows), local.whole((group, 2, rows))],
            (slow(out_scale), q, c, fast(state_in), slow(inside)),
            [wide, pltpu.HBM((group, 2, rows), F32)],
            "mixed",
            scratch=[pltpu.VMEM((rows, DH), F32)] * 2,
            flops=unit,
        )
        sums = lax.all_to_all(sums, ("core", "head"), 0, 0, tiled=True)
        grad, delta_after = local.call(
            functools.partial(grads_kernel, full_width),
            meta,
            [shared(MEMBERS)] + [cols(rows)] * 3 + [local.whole((group, 2, rows))],
            [cols(rows), state()],
            (slow(out_scale), q, c, slow(mixed), sums),
            [low, sent],
            "grads",
            scratch=[pltpu.VMEM((2, rows, DH), F32)],
            flops=unit,
        )
        query_own, query_send = local.call(
            query_kernel,
            meta,
            [cols(rows)] * 3 + [state()],
            [cols(tok)] * 2,
            (k, slow(scaled), slow(grad), slow(state_in)),
            [half] * 2,
            "query",
            flops=5 * unit,
        )
        state_after, query_own = scanned(delta_after, True, query_own)
        key_in, value_in, parts = local.call(
            functools.partial(back_kernel, full_width),
            meta,
            [cols(rows)] * 7 + [local.whole((group, 2, rows))],
            [cols(rows), cols(rows), cols(2 * MEMBERS)],
            (q, k, v, c, slow(scaled), slow(grad), slow(mixed), sums),
            [wide, wide, part],
            "back",
            flops=8 * unit,
        )
        query_grad = side_by_side(core, query_own, swap(query_send))
        copies = local.call(
            copies_kernel,
            meta,
            [cols(rows), cols(rows), state(), cols(2 * MEMBERS)],
            local.whole(packed),
            (k, v, fast(state_after), slow(parts)),
            pltpu.HBM(packed, BF16),
            "copies",
            scratch=[pltpu.VMEM(packed[1:], F32)],
            flops=unit,
        )
        copies = scattered(copies)
        key_own, key_send, value_own, value_send = local.call(
            last_kernel,
            meta,
            [shared(MEMBERS), cols(rows), cols(rows), state(), cols(rows), cols(rows)],
            [cols(tok)] * 4,
            (slow(in_scale), k, slow(scaled), slow(state_after), slow(key_in), slow(value_in)),
            [half] * 4,
            "last",
            flops=2 * unit,
        )
        key_grad = side_by_side(core, key_own, swap(key_send))
        value_grad = side_by_side(core, value_own, swap(value_send))
        copies, key_grad, value_grad, query_grad = lax.optimization_barrier(
            (copies, key_grad, value_grad, query_grad)
        )
        parts = jnp.sum(copies.astype(F32), axis=0)
        each = 2 * MEMBERS
        parts = jnp.concatenate([parts[i * each : (i + 1) * each] for i in range(local.steps)], axis=1)
        parts = side_by_side(core, parts, swap(parts))
        return query_grad, key_grad, value_grad, parts[:MEMBERS], parts[MEMBERS:]

    return shards


def solution(mesh):
    n_seq, n_head = mesh.shape["seq"], mesh.shape["head"]
    chips = n_seq // CORES
    finer = Mesh(mesh.devices.reshape(chips, CORES, n_head), ("chip", "core", "head"))
    tokens = ("chip", "core")
    wide = P(tokens, "head")
    scale = P(None, "head")
    return jax.shard_map(
        make_shards(n_seq, n_head),
        mesh=finer,
        in_specs=(wide, wide, wide, wide, P(tokens), scale, scale),
        out_specs=(wide, wide, wide, scale, scale),
        check_vma=False,
    )
```

```python
import functools

import jax
import jax.numpy as jnp
from jax import lax
from jax.experimental import pallas as pl
from jax.experimental.pallas import tpu as pltpu
from jax.sharding import Mesh, PartitionSpec as P

DH = 128
SPAN = 16
MEMBERS = 4
EPS = 1e-06
CORES = 2
STEP_HEADS = 4
LANE_GROUPS = 4
VMEM_BYTES = 24 * 2**20
F32 = jnp.float32
BF16 = jnp.bfloat16

NN = (((1,), (0,)), ((), ()))
NT = (((1,), (1,)), ((), ()))
TN = (((0,), (0,)), ((), ()))


class Meta:
    def __init__(self, place, own_ids, other_ids):
        self.core = place[0]
        self.ids = [own_ids[s] for s in range(own_ids.shape[0])]
        self.ids += [other_ids[s] for s in range(other_ids.shape[0])]


def with_meta(body):
    def kernel(place, own_ids, other_ids, *refs):
        body(Meta(place, own_ids, other_ids), *refs)

    return kernel


def dot(a, b, dims):
    return lax.dot_general(a, b, dims, preferred_element_type=F32)


def pair(own, other, lanes):
    return jnp.concatenate([own[:, lanes], other[:, lanes]], axis=0)


def rows_of_members(meta, scale, lanes, spans):
    choices = [scale[m : m + 1, lanes] for m in range(MEMBERS)]
    rows = []
    for s in range(spans):
        row = choices[0]
        for m in range(1, MEMBERS):
            row = jnp.where(meta.ids[s] == m, choices[m], row)
        rows.append(jnp.broadcast_to(row, (SPAN, DH)))
    return jnp.concatenate(rows, axis=0)


def member_sums(meta, x, spans):
    totals = [jnp.zeros((8, DH), F32) for _ in range(MEMBERS)]
    for s in range(spans):
        part = x[s * SPAN : s * SPAN + 8] + x[s * SPAN + 8 : (s + 1) * SPAN]
        for m in range(MEMBERS):
            keep = jnp.where(meta.ids[s] == m, 1.0, 0.0).astype(F32)
            totals[m] = totals[m] + keep * part
    return jnp.concatenate([jnp.sum(t, axis=0, keepdims=True) for t in totals], axis=0)


def causal_mask(meta, tok):
    size = 2 * tok
    core = meta.core
    base_own = core * tok
    base_other = (1 - core) * tok - tok

    def place(axis):
        at = lax.broadcasted_iota(jnp.int32, (size, size), axis)
        return at + jnp.where(at < tok, base_own, base_other)

    return place(0) >= place(1)


def in_order(meta, x, tok):
    turned = jnp.concatenate([x[:, tok:], x[:, :tok]], axis=1)
    return jnp.where(meta.core == 0, x, turned)


def head_sums(meta, sums, tok):
    total = sums[0]
    for at in range(1, sums.shape[0]):
        total = total + sums[at]
    return in_order(meta, total, tok)


def lanes_of(h):
    return pl.ds(h * DH, DH)


def states_kernel(meta, scale, k_own, k_other, v_own, v_other, scaled, delta):
    tok = k_own.shape[0]
    spans = 2 * tok // SPAN
    for h in range(delta.shape[0]):
        lanes = lanes_of(h)
        value = pair(v_own, v_other, lanes).astype(F32)
        low = (rows_of_members(meta, scale, lanes, spans) * value).astype(BF16)
        scaled[:, lanes] = low
        delta[h] = dot(pair(k_own, k_other, lanes), low, TN).astype(BF16)


def inside_kernel(
    meta, q_own, q_other, k_own, k_other, v_own, v_other, c_own, c_other, scaled,
    inside, q, k, v, c,
):
    tok = q_own.shape[0]
    causal = causal_mask(meta, tok)
    for both, own, other in ((q, q_own, q_other), (k, k_own, k_other), (v, v_own, v_other), (c, c_own, c_other)):
        both[:tok] = own[...]
        both[tok:] = other[...]
    for h in range(scaled.shape[1] // DH):
        lanes = lanes_of(h)
        scores = dot(q[:, lanes], k[:, lanes], NT)
        weights = jnp.where(causal, scores, 0.0).astype(BF16)
        inside[:, lanes] = dot(weights, scaled[:, lanes], NN)


def mixed_kernel(
    meta, scale, q, c, state, inside, mixed, sums, squares, crosses
):
    rows = q.shape[0]
    tok = rows // 2
    spans = rows // SPAN
    step = pl.program_id(0)

    @pl.when(step == 0)
    def _():
        squares[...] = jnp.zeros_like(squares)
        crosses[...] = jnp.zeros_like(crosses)

    square, cross = squares[...], crosses[...]
    for h in range(state.shape[0]):
        lanes = lanes_of(h)
        mix = inside[:, lanes] + dot(q[:, lanes], state[h], NN)
        mixed[:, lanes] = mix
        cot = c[:, lanes].astype(F32)
        square = square + mix * mix
        cross = cross + rows_of_members(meta, scale, lanes, spans) * cot * mix
    squares[...] = square
    crosses[...] = cross

    @pl.when(step == pl.num_programs(0) - 1)
    def _():
        totals = [jnp.sum(jnp.transpose(t), axis=0, keepdims=True) for t in (square, cross)]
        totals = in_order(meta, jnp.concatenate(totals, axis=0), tok)
        sums[...] = jnp.broadcast_to(totals[None], sums.shape)


def grads_kernel(
    full_width, meta, scale, q, c, mixed, sums, grad, delta, turned
):
    rows = q.shape[0]
    tok = rows // 2
    spans = rows // SPAN

    @pl.when(pl.program_id(0) == 0)
    def _():
        totals = head_sums(meta, sums, tok)
        rms = jnp.sqrt(totals[0:1] / full_width + EPS)
        turned[0] = jnp.transpose(jnp.broadcast_to(1.0 / rms, (DH, 2 * tok)))
        factor = totals[1:2] / (full_width * rms * rms * rms)
        turned[1] = jnp.transpose(jnp.broadcast_to(factor, (DH, 2 * tok)))

    inverse, factor = turned[0], turned[1]
    for h in range(delta.shape[0]):
        lanes = lanes_of(h)
        cot = c[:, lanes].astype(F32) * inverse
        mix = mixed[:, lanes]
        low = (rows_of_members(meta, scale, lanes, spans) * cot - mix * factor).astype(BF16)
        grad[:, lanes] = low
        delta[h] = dot(q[:, lanes], low, TN).astype(BF16)


def query_kernel(meta, k, scaled, grad, state, query_own, query_other):
    tok = k.shape[0] // 2
    causal = causal_mask(meta, tok)
    for h in range(state.shape[0]):
        lanes = lanes_of(h)
        g = grad[:, lanes]
        grad_weights = jnp.where(causal, dot(g, scaled[:, lanes], NT), 0.0).astype(BF16)
        query_grad = (dot(grad_weights, k[:, lanes], NN) + dot(g, state[h], NT)).astype(BF16)
        query_own[:, lanes] = query_grad[:tok]
        query_other[:, lanes] = query_grad[tok:]


def outs_kernel(full_width, meta, c, mixed, sums, out_part):
    rows = c.shape[0]
    spans = rows // SPAN
    totals = head_sums(meta, sums, rows // 2)
    inverse = 1.0 / jnp.sqrt(totals[0:1] / full_width + EPS)
    inverse = jnp.transpose(jnp.broadcast_to(inverse, (DH, rows)))
    for h in range(mixed.shape[1] // DH):
        lanes = lanes_of(h)
        normed = c[:, lanes].astype(F32) * (mixed[:, lanes] * inverse)
        out_part[:, lanes] = member_sums(meta, normed, spans)


def back_kernel(meta, q, k, v, scaled, grad, key_in, value_in, in_part):
    rows = k.shape[0]
    tok = rows // 2
    spans = rows // SPAN
    causal = causal_mask(meta, tok)
    for h in range(scaled.shape[1] // DH):
        lanes = lanes_of(h)
        query, g = q[:, lanes], grad[:, lanes]
        weights = jnp.where(causal, dot(query, k[:, lanes], NT), 0.0).astype(BF16)
        grad_weights = jnp.where(causal, dot(g, scaled[:, lanes], NT), 0.0).astype(BF16)
        key_in[:, lanes] = dot(grad_weights, query, TN)
        inner = dot(weights, g, TN)
        value_in[:, lanes] = inner
        in_part[:, lanes] = member_sums(meta, v[:, lanes].astype(F32) * inner, spans)


def copies_kernel(meta, k, v, state, known, extra, copies, parts):
    spans = k.shape[0] // SPAN
    step = pl.program_id(0)
    found = []
    for h in range(state.shape[0]):
        lanes = lanes_of(h)
        value = v[:, lanes].astype(F32)
        across = dot(k[:, lanes], state[h], NN)
        found.append(known[:, lanes] + member_sums(meta, value * across, spans))
    per_row = parts.shape[1] // DH
    rows = [
        jnp.concatenate(found[at : at + per_row], axis=1) for at in range(0, len(found), per_row)
    ]
    rows = jnp.concatenate(rows, axis=0)
    count = rows.shape[0]
    parts[pl.ds(pl.multiple_of(step * count, count), count)] = rows

    @pl.when(step == pl.num_programs(0) - 1)
    def _():
        whole = jnp.concatenate([parts[...], extra[...]], axis=1).astype(BF16)
        copies[...] = jnp.broadcast_to(whole[None], copies.shape)


def last_kernel(
    meta, scale, k, scaled, state, key_in, value_in,
    key_grad_own, key_grad_other, value_grad_own, value_grad_other,
):
    rows = k.shape[0]
    tok = rows // 2
    spans = rows // SPAN
    for h in range(state.shape[0]):
        lanes = lanes_of(h)
        key_grad = (key_in[:, lanes] + dot(scaled[:, lanes], state[h], NT)).astype(BF16)
        key_grad_own[:, lanes] = key_grad[:tok]
        key_grad_other[:, lanes] = key_grad[tok:]
        scaled_grad = value_in[:, lanes] + dot(k[:, lanes], state[h], NN)
        value_grad = (rows_of_members(meta, scale, lanes, spans) * scaled_grad).astype(BF16)
        value_grad_own[:, lanes] = value_grad[:tok]
        value_grad_other[:, lanes] = value_grad[tok:]


def total_kernel(copies, parts):
    count, _, lanes = copies.shape
    halves = []
    for first in range(2):
        total = copies[first].astype(F32)
        for at in range(first + 2, count, 2):
            total = total + copies[at].astype(F32)
        halves.append(total)
    wide_line = lanes - DH
    both = halves[0][:, :wide_line] + halves[1][:, :wide_line]
    groups = [both[i : i + MEMBERS] for i in range(0, both.shape[0], MEMBERS)]
    found = [jnp.concatenate(groups, axis=1)]
    for total in halves:
        lines = total[:, wide_line:]
        width = parts.shape[1] // DH
        for m in range(lines.shape[0] // width):
            row = [lines[m * width + i : m * width + i + 1] for i in range(width)]
            found.append(jnp.concatenate(row, axis=1))
    parts[...] = jnp.concatenate(found, axis=0)


def running_kernel(backward, pieces, sums):
    count = pieces.shape[0]
    total = jnp.zeros(pieces.shape[1:], F32)
    order = range(count - 1, -1, -1) if backward else range(count)
    for at in order:
        sums[at] = total.astype(BF16)
        total = total + pieces[at].astype(F32)


class Local:
    def __init__(self, tok, width):
        self.tok = tok
        self.width = width
        self.block = STEP_HEADS * DH
        self.steps = width // self.block

    def shared(self, rows):
        steps = self.steps
        return pl.BlockSpec((rows, self.block), lambda i, place, *_: (0, place[0] * steps + i))

    def cols(self, rows):
        return pl.BlockSpec((rows, self.block), lambda i, *_: (0, i))

    def state(self):
        return pl.BlockSpec((STEP_HEADS, DH, DH), lambda i, *_: (i, 0, 0))

    def whole(self, shape):
        return pl.BlockSpec(shape, lambda i, *_: (0,) * len(shape))

    def call(self, body, meta, ins, outs, args, shapes, name, scratch=(), flops=0):
        moved = sum(a.size * a.dtype.itemsize for a in args)
        return pl.pallas_call(
            with_meta(body),
            grid_spec=pltpu.PrefetchScalarGridSpec(
                num_scalar_prefetch=len(meta),
                grid=(self.steps,),
                in_specs=ins,
                out_specs=outs,
                scratch_shapes=scratch,
            ),
            out_shape=shapes,
            name=name,
            compiler_params=pltpu.CompilerParams(vmem_limit_bytes=VMEM_BYTES),
            cost_estimate=pl.CostEstimate(flops=flops, bytes_accessed=2 * moved, transcendentals=0),
        )(*meta, *args)


def fast(x):
    return pltpu.with_memory_space_constraint(x, pltpu.VMEM)


def slow(x):
    return pltpu.with_memory_space_constraint(x, pltpu.HBM)


def running_sums(pieces, backward):
    return pl.pallas_call(
        functools.partial(running_kernel, backward),
        out_shape=pltpu.HBM(pieces.shape, BF16),
        name="running_sums",
        compiler_params=pltpu.CompilerParams(vmem_limit_bytes=VMEM_BYTES),
    )(fast(pieces))


def make_shards(n_seq, n_head):
    chips = n_seq // CORES
    group = CORES * n_head

    def swap(x):
        return lax.ppermute(x, "core", [(0, 1), (1, 0)])

    def scattered(pieces):
        return lax.all_to_all(pieces, "chip", 0, 0, tiled=True)

    def scanned(delta, backward, beside=None):
        heads = delta.shape[0]
        pieces = scattered(delta.reshape(chips, heads * DH // chips, DH))
        if beside is not None:
            pieces, beside = lax.optimization_barrier((pieces, beside))
        state = scattered(running_sums(pieces, backward)).reshape(heads, DH, DH)
        return state if beside is None else (state,) + beside

    def side_by_side(core, own, other):
        return jnp.where(
            core == 0,
            jnp.concatenate([own, other], axis=1),
            jnp.concatenate([other, own], axis=1),
        )

    def shards(queries, key_vectors, value_vectors, cotangent, member_ids, in_scale, out_scale):
        tok, both = queries.shape
        width = both // CORES
        heads = width // DH
        full_width = both * n_head
        rows = 2 * tok
        core = lax.axis_index("core")

        other_ids = swap(member_ids)
        v_other = swap(value_vectors)
        k_other = swap(key_vectors)
        place = core[None].astype(jnp.int32)
        local = Local(tok, width)
        shared, cols, state = local.shared, local.cols, local.state
        half = pltpu.HBM((tok, width), BF16)
        low = pltpu.HBM((rows, width), BF16)
        wide = pltpu.HBM((rows, width), F32)
        part = pltpu.HBM((MEMBERS, width), F32)
        sent = pltpu.HBM((heads, DH, DH), BF16)
        pairs = [shared(tok), shared(tok)]
        lines, wide_line = LANE_GROUPS * MEMBERS, width // LANE_GROUPS
        packed = (chips, lines, wide_line + DH)
        unit = 2 * heads * rows * DH * DH

        meta = (place, member_ids, other_ids)
        scaled, delta = local.call(
            states_kernel,
            meta,
            [shared(MEMBERS)] + pairs * 2,
            [cols(rows), state()],
            (slow(in_scale), slow(key_vectors), fast(k_other), slow(value_vectors), fast(v_other)),
            [low, sent],
            "states",
            flops=unit,
        )
        queries_late, cotangent_late, delta = lax.optimization_barrier((queries, cotangent, delta))
        q_other = swap(queries_late)
        c_other = swap(cotangent_late)
        state_in = scanned(delta, False)
        inside, q, k, v, c = local.call(
            inside_kernel,
            meta,
            pairs * 4 + [cols(rows)],
            [cols(rows)] * 5,
            (
                slow(queries), slow(q_other), slow(key_vectors), slow(k_other),
                slow(value_vectors), slow(v_other), slow(cotangent), slow(c_other), slow(scaled),
            ),
            [wide] + [low] * 4,
            "inside",
            flops=4 * unit,
        )
        q, k, v, c = slow(q), slow(k), slow(v), slow(c)
        mixed, sums = local.call(
            mixed_kernel,
            meta,
            [shared(MEMBERS), cols(rows), cols(rows), state(), cols(rows)],
            [cols(rows), local.whole((group, 2, rows))],
            (slow(out_scale), q, c, fast(state_in), slow(inside)),
            [wide, pltpu.HBM((group, 2, rows), F32)],
            "mixed",
            scratch=[pltpu.VMEM((rows, DH), F32)] * 2,
            flops=unit,
        )
        sums = lax.all_to_all(sums, ("core", "head"), 0, 0, tiled=True)
        grad, delta_after = local.call(
            functools.partial(grads_kernel, full_width),
            meta,
            [shared(MEMBERS)] + [cols(rows)] * 3 + [local.whole((group, 2, rows))],
            [cols(rows), state()],
            (slow(out_scale), q, c, slow(mixed), sums),
            [low, sent],
            "grads",
            scratch=[pltpu.VMEM((2, rows, DH), F32)],
            flops=unit,
        )
        out_part = local.call(
            functools.partial(outs_kernel, full_width),
            meta,
            [cols(rows)] * 2 + [local.whole((group, 2, rows))],
            cols(MEMBERS),
            (c, slow(mixed), sums),
            part,
            "outs",
        )
        query_own, query_send = local.call(
            query_kernel,
            meta,
            [cols(rows)] * 3 + [state()],
            [cols(tok)] * 2,
            (k, slow(scaled), slow(grad), slow(state_in)),
            [half] * 2,
            "query",
            flops=5 * unit,
        )
        out_part = out_part + lax.ppermute(out_part, "chip", [(i, i ^ 1) for i in range(chips)])
        mine = MEMBERS // 2
        first = lax.axis_index("chip") % 2 * mine
        extra = lax.dynamic_slice_in_dim(out_part, first, mine, 0).reshape(lines, DH)
        state_after, query_own, extra = scanned(delta_after, True, (query_own, extra))
        key_in, value_in, in_part = local.call(
            back_kernel,
            meta,
            [cols(rows)] * 5,
            [cols(rows), cols(rows), cols(MEMBERS)],
            (q, k, v, slow(scaled), slow(grad)),
            [wide, wide, part],
            "back",
            flops=8 * unit,
        )
        query_grad = side_by_side(core, query_own, swap(query_send))
        copies = local.call(
            copies_kernel,
            meta,
            [cols(rows), cols(rows), state(), cols(MEMBERS), local.whole((lines, DH))],
            local.whole(packed),
            (k, v, fast(state_after), slow(in_part), extra),
            pltpu.HBM(packed, BF16),
            "copies",
            scratch=[pltpu.VMEM((lines, wide_line), F32)],
            flops=unit,
        )
        copies = scattered(copies)
        key_own, key_send, value_own, value_send = local.call(
            last_kernel,
            meta,
            [shared(MEMBERS), cols(rows), cols(rows), state(), cols(rows), cols(rows)],
            [cols(tok)] * 4,
            (slow(in_scale), k, slow(scaled), slow(state_after), slow(key_in), slow(value_in)),
            [half] * 4,
            "last",
            flops=2 * unit,
        )
        key_grad = side_by_side(core, key_own, swap(key_send))
        value_grad = side_by_side(core, value_own, swap(value_send))
        copies, key_grad, value_grad, query_grad = lax.optimization_barrier(
            (copies, key_grad, value_grad, query_grad)
        )
        parts = pl.pallas_call(
            total_kernel,
            out_shape=jax.ShapeDtypeStruct((2 * MEMBERS, width), F32),
            name="total",
            compiler_params=pltpu.CompilerParams(vmem_limit_bytes=VMEM_BYTES),
        )(copies)
        parts = side_by_side(core, parts, swap(parts))
        return query_grad, key_grad, value_grad, parts[:MEMBERS], parts[MEMBERS:]

    return shards


def solution(mesh):
    n_seq, n_head = mesh.shape["seq"], mesh.shape["head"]
    chips = n_seq // CORES
    finer = Mesh(mesh.devices.reshape(chips, CORES, n_head), ("chip", "core", "head"))
    tokens = ("chip", "core")
    wide = P(tokens, "head")
    scale = P(None, "head")
    return jax.shard_map(
        make_shards(n_seq, n_head),
        mesh=finer,
        in_specs=(wide, wide, wide, wide, P(tokens), scale, scale),
        out_specs=(wide, wide, wide, scale, scale),
        check_vma=False,
    )
```

```python
import functools

import jax
import jax.numpy as jnp
from jax import lax
from jax.experimental import pallas as pl
from jax.experimental.pallas import tpu as pltpu
from jax.sharding import Mesh, PartitionSpec as P

DH = 128
SPAN = 16
MEMBERS = 4
EPS = 1e-06
CORES = 2
STEP_HEADS = 4
FLOW_HEADS = 2
LANE_GROUPS = 4
VMEM_BYTES = 24 * 2**20
F32 = jnp.float32
BF16 = jnp.bfloat16

NN = (((1,), (0,)), ((), ()))
NT = (((1,), (1,)), ((), ()))
TN = (((0,), (0,)), ((), ()))


class Meta:
    def __init__(self, place, own_ids, other_ids):
        self.core = place[0]
        self.ids = [own_ids[s] for s in range(own_ids.shape[0])]
        self.ids += [other_ids[s] for s in range(other_ids.shape[0])]


def with_meta(body):
    def kernel(place, own_ids, other_ids, *refs):
        body(Meta(place, own_ids, other_ids), *refs)

    return kernel


def dot(a, b, dims):
    return lax.dot_general(a, b, dims, preferred_element_type=F32)


def pair(own, other, lanes):
    return jnp.concatenate([own[:, lanes], other[:, lanes]], axis=0)


def rows_of_members(meta, scale, lanes, spans):
    choices = [scale[m : m + 1, lanes] for m in range(MEMBERS)]
    rows = []
    for s in range(spans):
        row = choices[0]
        for m in range(1, MEMBERS):
            row = jnp.where(meta.ids[s] == m, choices[m], row)
        rows.append(jnp.broadcast_to(row, (SPAN, DH)))
    return jnp.concatenate(rows, axis=0)


def member_sums(meta, x, spans):
    totals = [jnp.zeros((8, DH), F32) for _ in range(MEMBERS)]
    for s in range(spans):
        part = x[s * SPAN : s * SPAN + 8] + x[s * SPAN + 8 : (s + 1) * SPAN]
        for m in range(MEMBERS):
            keep = jnp.where(meta.ids[s] == m, 1.0, 0.0).astype(F32)
            totals[m] = totals[m] + keep * part
    return jnp.concatenate([jnp.sum(t, axis=0, keepdims=True) for t in totals], axis=0)


def causal_mask(meta, tok):
    size = 2 * tok
    core = meta.core
    base_own = core * tok
    base_other = (1 - core) * tok - tok

    def place(axis):
        at = lax.broadcasted_iota(jnp.int32, (size, size), axis)
        return at + jnp.where(at < tok, base_own, base_other)

    return place(0) >= place(1)


def in_order(meta, x, tok):
    turned = jnp.concatenate([x[:, tok:], x[:, :tok]], axis=1)
    return jnp.where(meta.core == 0, x, turned)


def head_sums(meta, sums, tok):
    total = sums[0]
    for at in range(1, sums.shape[0]):
        total = total + sums[at]
    return in_order(meta, total, tok)


def lanes_of(h):
    return pl.ds(h * DH, DH)


def states_kernel(meta, scale, k_own, k_other, v_own, v_other, scaled, delta):
    tok = k_own.shape[0]
    spans = 2 * tok // SPAN
    for h in range(delta.shape[0]):
        lanes = lanes_of(h)
        value = pair(v_own, v_other, lanes).astype(F32)
        low = (rows_of_members(meta, scale, lanes, spans) * value).astype(BF16)
        scaled[:, lanes] = low
        delta[h] = dot(pair(k_own, k_other, lanes), low, TN).astype(BF16)


def inside_kernel(
    meta, q_own, q_other, k_own, k_other, v_own, v_other, c_own, c_other, scaled,
    inside, q, k, v, c,
):
    tok = q_own.shape[0]
    causal = causal_mask(meta, tok)
    for both, own, other in ((q, q_own, q_other), (k, k_own, k_other), (v, v_own, v_other), (c, c_own, c_other)):
        both[:tok] = own[...]
        both[tok:] = other[...]
    for h in range(scaled.shape[1] // DH):
        lanes = lanes_of(h)
        scores = dot(q[:, lanes], k[:, lanes], NT)
        weights = jnp.where(causal, scores, 0.0).astype(BF16)
        inside[:, lanes] = dot(weights, scaled[:, lanes], NN)


def mixed_kernel(meta, step, steps, scale, q, c, state, inside, mixed, sums, squares, crosses):
    rows = q.shape[0]
    tok = rows // 2
    spans = rows // SPAN
    empty = jnp.zeros(squares.shape, F32)
    square, cross = (empty, empty) if step == 0 else (squares[...], crosses[...])
    for h in range(state.shape[0]):
        lanes = lanes_of(h)
        mix = inside[:, lanes] + dot(q[:, lanes], state[h], NN)
        mixed[:, lanes] = mix
        cot = c[:, lanes].astype(F32)
        square = square + mix * mix
        cross = cross + rows_of_members(meta, scale, lanes, spans) * cot * mix
    if step < steps - 1:
        squares[...] = square
        crosses[...] = cross
    else:
        totals = [jnp.sum(jnp.transpose(t), axis=0, keepdims=True) for t in (square, cross)]
        totals = in_order(meta, jnp.concatenate(totals, axis=0), tok)
        sums[...] = jnp.broadcast_to(totals[None], sums.shape)


def grads_kernel(
    full_width, meta, step, steps, scale, q, c, mixed, sums, grad, delta, turned
):
    rows = q.shape[0]
    tok = rows // 2
    spans = rows // SPAN

    if step == 0:
        totals = head_sums(meta, sums, tok)
        rms = jnp.sqrt(totals[0:1] / full_width + EPS)
        turned[0] = jnp.transpose(jnp.broadcast_to(1.0 / rms, (DH, 2 * tok)))
        factor = totals[1:2] / (full_width * rms * rms * rms)
        turned[1] = jnp.transpose(jnp.broadcast_to(factor, (DH, 2 * tok)))

    inverse, factor = turned[0], turned[1]
    for h in range(delta.shape[0]):
        lanes = lanes_of(h)
        cot = c[:, lanes].astype(F32) * inverse
        mix = mixed[:, lanes]
        low = (rows_of_members(meta, scale, lanes, spans) * cot - mix * factor).astype(BF16)
        grad[:, lanes] = low
        delta[h] = dot(q[:, lanes], low, TN).astype(BF16)


def query_kernel(meta, k, scaled, grad, state, query_own, query_other):
    tok = k.shape[0] // 2
    causal = causal_mask(meta, tok)
    for h in range(state.shape[0]):
        lanes = lanes_of(h)
        g = grad[:, lanes]
        grad_weights = jnp.where(causal, dot(g, scaled[:, lanes], NT), 0.0).astype(BF16)
        query_grad = (dot(grad_weights, k[:, lanes], NN) + dot(g, state[h], NT)).astype(BF16)
        query_own[:, lanes] = query_grad[:tok]
        query_other[:, lanes] = query_grad[tok:]


def outs_kernel(full_width, meta, c, mixed, sums, out_part):
    rows = c.shape[0]
    spans = rows // SPAN
    totals = head_sums(meta, sums, rows // 2)
    inverse = 1.0 / jnp.sqrt(totals[0:1] / full_width + EPS)
    inverse = jnp.transpose(jnp.broadcast_to(inverse, (DH, rows)))
    for h in range(mixed.shape[1] // DH):
        lanes = lanes_of(h)
        normed = c[:, lanes].astype(F32) * (mixed[:, lanes] * inverse)
        out_part[:, lanes] = member_sums(meta, normed, spans)


def back_kernel(meta, q, k, v, scaled, grad, key_in, value_in, in_part):
    rows = k.shape[0]
    tok = rows // 2
    spans = rows // SPAN
    causal = causal_mask(meta, tok)
    for h in range(scaled.shape[1] // DH):
        lanes = lanes_of(h)
        query, g = q[:, lanes], grad[:, lanes]
        weights = jnp.where(causal, dot(query, k[:, lanes], NT), 0.0).astype(BF16)
        grad_weights = jnp.where(causal, dot(g, scaled[:, lanes], NT), 0.0).astype(BF16)
        key_in[:, lanes] = dot(grad_weights, query, TN)
        inner = dot(weights, g, TN)
        value_in[:, lanes] = inner
        in_part[:, lanes] = member_sums(meta, v[:, lanes].astype(F32) * inner, spans)


def copies_kernel(meta, step, steps, k, v, state, known, extra, copies, parts):
    spans = k.shape[0] // SPAN
    found = []
    for h in range(state.shape[0]):
        lanes = lanes_of(h)
        value = v[:, lanes].astype(F32)
        across = dot(k[:, lanes], state[h], NN)
        found.append(known[:, lanes] + member_sums(meta, value * across, spans))
    per_row = parts.shape[1] // DH
    rows = [
        jnp.concatenate(found[at : at + per_row], axis=1) for at in range(0, len(found), per_row)
    ]
    rows = jnp.concatenate(rows, axis=0)
    count = rows.shape[0]
    parts[step * count : (step + 1) * count] = rows
    if step == steps - 1:
        whole = jnp.concatenate([parts[...], extra[...]], axis=1).astype(BF16)
        copies[...] = jnp.broadcast_to(whole[None], copies.shape)


def last_kernel(
    meta, scale, k, scaled, state, key_in, value_in,
    key_grad_own, key_grad_other, value_grad_own, value_grad_other,
):
    rows = k.shape[0]
    tok = rows // 2
    spans = rows // SPAN
    for h in range(state.shape[0]):
        lanes = lanes_of(h)
        key_grad = (key_in[:, lanes] + dot(scaled[:, lanes], state[h], NT)).astype(BF16)
        key_grad_own[:, lanes] = key_grad[:tok]
        key_grad_other[:, lanes] = key_grad[tok:]
        scaled_grad = value_in[:, lanes] + dot(k[:, lanes], state[h], NN)
        value_grad = (rows_of_members(meta, scale, lanes, spans) * scaled_grad).astype(BF16)
        value_grad_own[:, lanes] = value_grad[:tok]
        value_grad_other[:, lanes] = value_grad[tok:]


def total_kernel(copies, parts):
    count, _, lanes = copies.shape
    halves = []
    for first in range(2):
        total = copies[first].astype(F32)
        for at in range(first + 2, count, 2):
            total = total + copies[at].astype(F32)
        halves.append(total)
    wide_line = lanes - DH
    both = halves[0][:, :wide_line] + halves[1][:, :wide_line]
    groups = [both[i : i + MEMBERS] for i in range(0, both.shape[0], MEMBERS)]
    found = [jnp.concatenate(groups, axis=1)]
    for total in halves:
        lines = total[:, wide_line:]
        width = parts.shape[1] // DH
        for m in range(lines.shape[0] // width):
            row = [lines[m * width + i : m * width + i + 1] for i in range(width)]
            found.append(jnp.concatenate(row, axis=1))
    parts[...] = jnp.concatenate(found, axis=0)


def running_kernel(backward, pieces, sums):
    count = pieces.shape[0]
    total = jnp.zeros(pieces.shape[1:], F32)
    order = range(count - 1, -1, -1) if backward else range(count)
    for at in order:
        sums[at] = total.astype(BF16)
        total = total + pieces[at].astype(F32)


def streamed_kernel(body, kinds, scratch_count, width, place, own_ids, other_ids, *refs):
    meta = Meta(place, own_ids, other_ids)
    ins, outs = kinds
    steps = width // (FLOW_HEADS * DH)
    taken = [refs[: len(ins)], refs[len(ins) : len(ins) + len(outs)]]
    rest = refs[len(ins) + len(outs) :]
    in_bufs, out_bufs = rest[: len(ins)], rest[len(ins) : len(ins) + len(outs)]
    sent, got = rest[len(ins) + len(outs) : len(ins) + len(outs) + 2]
    extra = rest[len(ins) + len(outs) + 2 :]

    def part(kind, ref, step):
        if kind == "cols":
            return ref.at[:, pl.ds(step * FLOW_HEADS * DH, FLOW_HEADS * DH)]
        if kind == "state":
            return ref.at[pl.ds(step * FLOW_HEADS, FLOW_HEADS)]
        return ref

    arrivals = []
    for step in range(steps):
        here = []
        for at, kind in enumerate(ins):
            source, target = taken[0][at], in_bufs[at]
            if kind == "held" or (kind != "cols" and step > 0):
                continue
            if kind == "scale":
                start = pl.multiple_of(meta.core * width, width)
                source = source.at[:, pl.ds(start, width)]
            copy = pltpu.make_async_copy(
                part(kind, source, step), part(kind, target, step), got.at[at, step]
            )
            copy.start()
            here.append(copy)
        arrivals.append(here)
    leaving = []
    for step in range(steps):
        for copy in arrivals[step]:
            copy.wait()
        views = []
        for at, kind in enumerate(ins):
            if kind == "held":
                views.append(part("state", taken[0][at], step))
            else:
                views.append(part("cols" if kind == "scale" else kind, in_bufs[at], step))
        views += [part(kind, out_bufs[at], step) for at, kind in enumerate(outs)]
        body(meta, step, steps, *views, *extra)
        for at, kind in enumerate(outs):
            if kind == "whole" and step < steps - 1:
                continue
            copy = pltpu.make_async_copy(
                part(kind, out_bufs[at], step), part(kind, taken[1][at], step), sent.at[at, step]
            )
            copy.start()
            leaving.append(copy)
    for copy in leaving:
        copy.wait()


class Local:
    def __init__(self, tok, width):
        self.tok = tok
        self.width = width
        self.block = STEP_HEADS * DH
        self.steps = width // self.block

    def shared(self, rows):
        steps = self.steps
        return pl.BlockSpec((rows, self.block), lambda i, place, *_: (0, place[0] * steps + i))

    def cols(self, rows):
        return pl.BlockSpec((rows, self.block), lambda i, *_: (0, i))

    def state(self):
        return pl.BlockSpec((STEP_HEADS, DH, DH), lambda i, *_: (i, 0, 0))

    def whole(self, shape):
        return pl.BlockSpec(shape, lambda i, *_: (0,) * len(shape))

    def flow(self, body, meta, kinds, args, shapes, name, scratch=(), flops=0):
        ins, outs = kinds
        steps = self.width // (FLOW_HEADS * DH)
        buffers = []
        for kind, arg in zip(ins, args):
            shape = (arg.shape[0], self.width) if kind == "scale" else arg.shape
            buffers.append(pltpu.VMEM((8, DH) if kind == "held" else shape, arg.dtype))
        buffers += [pltpu.VMEM(x.shape, x.dtype) for x in shapes]
        sems = [
            pltpu.SemaphoreType.DMA((len(outs), steps)),
            pltpu.SemaphoreType.DMA((len(ins), steps)),
        ]
        spaces = [pltpu.VMEM if kind == "held" else pltpu.HBM for kind in ins]
        moved = sum(a.size * a.dtype.itemsize for a in args)
        return pl.pallas_call(
            functools.partial(streamed_kernel, body, kinds, len(scratch), self.width),
            in_specs=[pl.BlockSpec(memory_space=pltpu.SMEM)] * len(meta)
            + [pl.BlockSpec(memory_space=space) for space in spaces],
            out_specs=[pl.BlockSpec(memory_space=pltpu.HBM) for _ in outs],
            out_shape=shapes,
            scratch_shapes=buffers + sems + list(scratch),
            name=name,
            compiler_params=pltpu.CompilerParams(vmem_limit_bytes=VMEM_BYTES),
            cost_estimate=pl.CostEstimate(flops=flops, bytes_accessed=2 * moved, transcendentals=0),
        )(*meta, *args)

    def call(self, body, meta, ins, outs, args, shapes, name, scratch=(), flops=0):
        moved = sum(a.size * a.dtype.itemsize for a in args)
        return pl.pallas_call(
            with_meta(body),
            grid_spec=pltpu.PrefetchScalarGridSpec(
                num_scalar_prefetch=len(meta),
                grid=(self.steps,),
                in_specs=ins,
                out_specs=outs,
                scratch_shapes=scratch,
            ),
            out_shape=shapes,
            name=name,
            compiler_params=pltpu.CompilerParams(vmem_limit_bytes=VMEM_BYTES),
            cost_estimate=pl.CostEstimate(flops=flops, bytes_accessed=2 * moved, transcendentals=0),
        )(*meta, *args)


def fast(x):
    return pltpu.with_memory_space_constraint(x, pltpu.VMEM)


def slow(x):
    return pltpu.with_memory_space_constraint(x, pltpu.HBM)


def running_sums(pieces, backward):
    return pl.pallas_call(
        functools.partial(running_kernel, backward),
        out_shape=pltpu.HBM(pieces.shape, BF16),
        name="running_sums",
        compiler_params=pltpu.CompilerParams(vmem_limit_bytes=VMEM_BYTES),
    )(fast(pieces))


def make_shards(n_seq, n_head):
    chips = n_seq // CORES
    group = CORES * n_head

    def swap(x):
        return lax.ppermute(x, "core", [(0, 1), (1, 0)])

    def scattered(pieces):
        return lax.all_to_all(pieces, "chip", 0, 0, tiled=True)

    def scanned(delta, backward, beside=None):
        heads = delta.shape[0]
        pieces = scattered(delta.reshape(chips, heads * DH // chips, DH))
        if beside is not None:
            pieces, beside = lax.optimization_barrier((pieces, beside))
        state = scattered(running_sums(pieces, backward)).reshape(heads, DH, DH)
        return state if beside is None else (state,) + beside

    def side_by_side(core, own, other):
        return jnp.where(
            core == 0,
            jnp.concatenate([own, other], axis=1),
            jnp.concatenate([other, own], axis=1),
        )

    def shards(queries, key_vectors, value_vectors, cotangent, member_ids, in_scale, out_scale):
        tok, both = queries.shape
        width = both // CORES
        heads = width // DH
        full_width = both * n_head
        rows = 2 * tok
        core = lax.axis_index("core")

        other_ids = swap(member_ids)
        v_other = swap(value_vectors)
        k_other = swap(key_vectors)
        place = core[None].astype(jnp.int32)
        local = Local(tok, width)
        shared, cols, state = local.shared, local.cols, local.state
        half = pltpu.HBM((tok, width), BF16)
        low = pltpu.HBM((rows, width), BF16)
        wide = pltpu.HBM((rows, width), F32)
        part = pltpu.HBM((MEMBERS, width), F32)
        sent = pltpu.HBM((heads, DH, DH), BF16)
        pairs = [shared(tok), shared(tok)]
        lines, wide_line = LANE_GROUPS * MEMBERS, width // LANE_GROUPS
        packed = (chips, lines, wide_line + DH)
        unit = 2 * heads * rows * DH * DH

        meta = (place, member_ids, other_ids)
        scaled, delta = local.call(
            states_kernel,
            meta,
            [shared(MEMBERS)] + pairs * 2,
            [cols(rows), state()],
            (slow(in_scale), slow(key_vectors), fast(k_other), slow(value_vectors), fast(v_other)),
            [low, sent],
            "states",
            flops=unit,
        )
        queries_late, cotangent_late, delta = lax.optimization_barrier((queries, cotangent, delta))
        q_other = swap(queries_late)
        c_other = swap(cotangent_late)
        state_in = scanned(delta, False)
        inside, q, k, v, c = local.call(
            inside_kernel,
            meta,
            pairs * 4 + [cols(rows)],
            [cols(rows)] * 5,
            (
                slow(queries), slow(q_other), slow(key_vectors), slow(k_other),
                slow(value_vectors), slow(v_other), slow(cotangent), slow(c_other), slow(scaled),
            ),
            [wide] + [low] * 4,
            "inside",
            flops=4 * unit,
        )
        q, k, v, c = slow(q), slow(k), slow(v), slow(c)
        mixed, sums = local.flow(
            mixed_kernel,
            meta,
            (("scale", "cols", "cols", "held", "cols"), ("cols", "whole")),
            (slow(out_scale), q, c, fast(state_in), slow(inside)),
            [wide, pltpu.HBM((group, 2, rows), F32)],
            "mixed",
            scratch=[pltpu.VMEM((rows, DH), F32)] * 2,
            flops=unit,
        )
        sums = lax.all_to_all(sums, ("core", "head"), 0, 0, tiled=True)
        grad, delta_after = local.flow(
            functools.partial(grads_kernel, full_width),
            meta,
            (("scale", "cols", "cols", "cols", "whole"), ("cols", "state")),
            (slow(out_scale), q, c, slow(mixed), sums),
            [low, sent],
            "grads",
            scratch=[pltpu.VMEM((2, rows, DH), F32)],
            flops=unit,
        )
        out_part = local.call(
            functools.partial(outs_kernel, full_width),
            meta,
            [cols(rows)] * 2 + [local.whole((group, 2, rows))],
            cols(MEMBERS),
            (c, slow(mixed), sums),
            part,
            "outs",
        )
        query_own, query_send = local.call(
            query_kernel,
            meta,
            [cols(rows)] * 3 + [state()],
            [cols(tok)] * 2,
            (k, slow(scaled), slow(grad), slow(state_in)),
            [half] * 2,
            "query",
            flops=5 * unit,
        )
        out_part = out_part + lax.ppermute(out_part, "chip", [(i, i ^ 1) for i in range(chips)])
        mine = MEMBERS // 2
        first = lax.axis_index("chip") % 2 * mine
        extra = lax.dynamic_slice_in_dim(out_part, first, mine, 0).reshape(lines, DH)
        state_after, query_own, extra = scanned(delta_after, True, (query_own, extra))
        key_in, value_in, in_part = local.call(
            back_kernel,
            meta,
            [cols(rows)] * 5,
            [cols(rows), cols(rows), cols(MEMBERS)],
            (q, k, v, slow(scaled), slow(grad)),
            [wide, wide, part],
            "back",
            flops=8 * unit,
        )
        query_grad = side_by_side(core, query_own, swap(query_send))
        copies, = local.flow(
            copies_kernel,
            meta,
            (("cols", "cols", "held", "cols", "whole"), ("whole",)),
            (k, v, fast(state_after), slow(in_part), slow(extra)),
            [pltpu.HBM(packed, BF16)],
            "copies",
            scratch=[pltpu.VMEM((lines, wide_line), F32)],
            flops=unit,
        )
        copies = scattered(copies)
        key_own, key_send, value_own, value_send = local.call(
            last_kernel,
            meta,
            [shared(MEMBERS), cols(rows), cols(rows), state(), cols(rows), cols(rows)],
            [cols(tok)] * 4,
            (slow(in_scale), k, slow(scaled), slow(state_after), slow(key_in), slow(value_in)),
            [half] * 4,
            "last",
            flops=2 * unit,
        )
        key_grad = side_by_side(core, key_own, swap(key_send))
        value_grad = side_by_side(core, value_own, swap(value_send))
        copies, key_grad, value_grad, query_grad = lax.optimization_barrier(
            (copies, key_grad, value_grad, query_grad)
        )
        parts = pl.pallas_call(
            total_kernel,
            out_shape=jax.ShapeDtypeStruct((2 * MEMBERS, width), F32),
            name="total",
            compiler_params=pltpu.CompilerParams(vmem_limit_bytes=VMEM_BYTES),
        )(copies)
        parts = side_by_side(core, parts, swap(parts))
        return query_grad, key_grad, value_grad, parts[:MEMBERS], parts[MEMBERS:]

    return shards


def solution(mesh):
    n_seq, n_head = mesh.shape["seq"], mesh.shape["head"]
    chips = n_seq // CORES
    finer = Mesh(mesh.devices.reshape(chips, CORES, n_head), ("chip", "core", "head"))
    tokens = ("chip", "core")
    wide = P(tokens, "head")
    scale = P(None, "head")
    return jax.shard_map(
        make_shards(n_seq, n_head),
        mesh=finer,
        in_specs=(wide, wide, wide, wide, P(tokens), scale, scale),
        out_specs=(wide, wide, wide, scale, scale),
        check_vma=False,
    )
```

```python
import functools

import jax
import jax.numpy as jnp
from jax import lax
from jax.experimental import pallas as pl
from jax.experimental.pallas import tpu as pltpu
from jax.sharding import Mesh, PartitionSpec as P

DH = 128
SPAN = 16
MEMBERS = 4
EPS = 1e-06
CORES = 2
STEP_HEADS = 4
LANE_GROUPS = 4
VMEM_BYTES = 24 * 2**20
F32 = jnp.float32
BF16 = jnp.bfloat16

NN = (((1,), (0,)), ((), ()))
NT = (((1,), (1,)), ((), ()))
TN = (((0,), (0,)), ((), ()))


class Meta:
    def __init__(self, place, own_ids, other_ids):
        self.core = place[0]
        self.ids = [own_ids[s] for s in range(own_ids.shape[0])]
        self.ids += [other_ids[s] for s in range(other_ids.shape[0])]


def with_meta(body):
    def kernel(place, own_ids, other_ids, *refs):
        body(Meta(place, own_ids, other_ids), *refs)

    return kernel


def dot(a, b, dims):
    return lax.dot_general(a, b, dims, preferred_element_type=F32)


def pair(own, other, lanes):
    return jnp.concatenate([own[:, lanes], other[:, lanes]], axis=0)


def rows_of_members(meta, scale, lanes, spans):
    choices = [scale[m : m + 1, lanes] for m in range(MEMBERS)]
    rows = []
    for s in range(spans):
        row = choices[0]
        for m in range(1, MEMBERS):
            row = jnp.where(meta.ids[s] == m, choices[m], row)
        rows.append(jnp.broadcast_to(row, (SPAN, DH)))
    return jnp.concatenate(rows, axis=0)


def member_sums(meta, x, spans):
    totals = [jnp.zeros((8, DH), F32) for _ in range(MEMBERS)]
    for s in range(spans):
        part = x[s * SPAN : s * SPAN + 8] + x[s * SPAN + 8 : (s + 1) * SPAN]
        for m in range(MEMBERS):
            keep = jnp.where(meta.ids[s] == m, 1.0, 0.0).astype(F32)
            totals[m] = totals[m] + keep * part
    return jnp.concatenate([jnp.sum(t, axis=0, keepdims=True) for t in totals], axis=0)


def causal_mask(meta, tok):
    size = 2 * tok
    core = meta.core
    base_own = core * tok
    base_other = (1 - core) * tok - tok

    def place(axis):
        at = lax.broadcasted_iota(jnp.int32, (size, size), axis)
        return at + jnp.where(at < tok, base_own, base_other)

    return place(0) >= place(1)


def in_order(meta, x, tok):
    turned = jnp.concatenate([x[:, tok:], x[:, :tok]], axis=1)
    return jnp.where(meta.core == 0, x, turned)


def head_sums(meta, sums, tok):
    total = sums[0]
    for at in range(1, sums.shape[0]):
        total = total + sums[at]
    return in_order(meta, total, tok)


def lanes_of(h):
    return pl.ds(h * DH, DH)


def states_kernel(meta, scale, k_own, k_other, v_own, v_other, scaled, delta):
    tok = k_own.shape[0]
    spans = 2 * tok // SPAN
    for h in range(delta.shape[0]):
        lanes = lanes_of(h)
        value = pair(v_own, v_other, lanes).astype(F32)
        low = (rows_of_members(meta, scale, lanes, spans) * value).astype(BF16)
        scaled[:, lanes] = low
        delta[h] = dot(pair(k_own, k_other, lanes), low, TN).astype(BF16)


def inside_kernel(
    meta, q_own, q_other, k_own, k_other, v_own, v_other, c_own, c_other, scaled,
    inside, q, k, v, c,
):
    tok = q_own.shape[0]
    causal = causal_mask(meta, tok)
    for both, own, other in ((q, q_own, q_other), (k, k_own, k_other), (v, v_own, v_other), (c, c_own, c_other)):
        both[:tok] = own[...]
        both[tok:] = other[...]
    for h in range(scaled.shape[1] // DH):
        lanes = lanes_of(h)
        scores = dot(q[:, lanes], k[:, lanes], NT)
        weights = jnp.where(causal, scores, 0.0).astype(BF16)
        inside[:, lanes] = dot(weights, scaled[:, lanes], NN).astype(BF16)


def mixed_kernel(
    meta, scale, q, c, state, inside, mixed, sums, squares, crosses
):
    rows = q.shape[0]
    tok = rows // 2
    spans = rows // SPAN
    step = pl.program_id(0)

    @pl.when(step == 0)
    def _():
        squares[...] = jnp.zeros_like(squares)
        crosses[...] = jnp.zeros_like(crosses)

    square, cross = squares[...], crosses[...]
    for h in range(state.shape[0]):
        lanes = lanes_of(h)
        mix = inside[:, lanes].astype(F32) + dot(q[:, lanes], state[h], NN)
        mixed[:, lanes] = mix.astype(BF16)
        cot = c[:, lanes].astype(F32)
        square = square + mix * mix
        cross = cross + rows_of_members(meta, scale, lanes, spans) * cot * mix
    squares[...] = square
    crosses[...] = cross

    @pl.when(step == pl.num_programs(0) - 1)
    def _():
        totals = [jnp.sum(jnp.transpose(t), axis=0, keepdims=True) for t in (square, cross)]
        totals = in_order(meta, jnp.concatenate(totals, axis=0), tok)
        sums[...] = jnp.broadcast_to(totals[None], sums.shape)


def grads_kernel(
    full_width, meta, scale, q, c, mixed, sums, grad, delta, turned
):
    rows = q.shape[0]
    tok = rows // 2
    spans = rows // SPAN

    @pl.when(pl.program_id(0) == 0)
    def _():
        totals = head_sums(meta, sums, tok)
        rms = jnp.sqrt(totals[0:1] / full_width + EPS)
        turned[0] = jnp.transpose(jnp.broadcast_to(1.0 / rms, (DH, 2 * tok)))
        factor = totals[1:2] / (full_width * rms * rms * rms)
        turned[1] = jnp.transpose(jnp.broadcast_to(factor, (DH, 2 * tok)))

    inverse, factor = turned[0], turned[1]
    for h in range(delta.shape[0]):
        lanes = lanes_of(h)
        cot = c[:, lanes].astype(F32) * inverse
        mix = mixed[:, lanes].astype(F32)
        low = (rows_of_members(meta, scale, lanes, spans) * cot - mix * factor).astype(BF16)
        grad[:, lanes] = low
        delta[h] = dot(q[:, lanes], low, TN).astype(BF16)


def query_kernel(meta, k, scaled, grad, state, query_own, query_other):
    tok = k.shape[0] // 2
    causal = causal_mask(meta, tok)
    for h in range(state.shape[0]):
        lanes = lanes_of(h)
        g = grad[:, lanes]
        grad_weights = jnp.where(causal, dot(g, scaled[:, lanes], NT), 0.0).astype(BF16)
        query_grad = (dot(grad_weights, k[:, lanes], NN) + dot(g, state[h], NT)).astype(BF16)
        query_own[:, lanes] = query_grad[:tok]
        query_other[:, lanes] = query_grad[tok:]


def outs_kernel(full_width, meta, c, mixed, sums, out_part):
    rows = c.shape[0]
    spans = rows // SPAN
    totals = head_sums(meta, sums, rows // 2)
    inverse = 1.0 / jnp.sqrt(totals[0:1] / full_width + EPS)
    inverse = jnp.transpose(jnp.broadcast_to(inverse, (DH, rows)))
    for h in range(mixed.shape[1] // DH):
        lanes = lanes_of(h)
        normed = c[:, lanes].astype(F32) * (mixed[:, lanes].astype(F32) * inverse)
        out_part[:, lanes] = member_sums(meta, normed, spans)


def back_kernel(meta, q, k, v, scaled, grad, key_in, value_in, in_part):
    rows = k.shape[0]
    tok = rows // 2
    spans = rows // SPAN
    causal = causal_mask(meta, tok)
    for h in range(scaled.shape[1] // DH):
        lanes = lanes_of(h)
        query, g = q[:, lanes], grad[:, lanes]
        weights = jnp.where(causal, dot(query, k[:, lanes], NT), 0.0).astype(BF16)
        grad_weights = jnp.where(causal, dot(g, scaled[:, lanes], NT), 0.0).astype(BF16)
        key_in[:, lanes] = dot(grad_weights, query, TN)
        inner = dot(weights, g, TN)
        value_in[:, lanes] = inner
        in_part[:, lanes] = member_sums(meta, v[:, lanes].astype(F32) * inner, spans)


def copies_kernel(meta, k, v, state, known, extra, copies, parts):
    spans = k.shape[0] // SPAN
    step = pl.program_id(0)
    found = []
    for h in range(state.shape[0]):
        lanes = lanes_of(h)
        value = v[:, lanes].astype(F32)
        across = dot(k[:, lanes], state[h], NN)
        found.append(known[:, lanes] + member_sums(meta, value * across, spans))
    per_row = parts.shape[1] // DH
    rows = [
        jnp.concatenate(found[at : at + per_row], axis=1) for at in range(0, len(found), per_row)
    ]
    rows = jnp.concatenate(rows, axis=0)
    count = rows.shape[0]
    parts[pl.ds(pl.multiple_of(step * count, count), count)] = rows

    @pl.when(step == pl.num_programs(0) - 1)
    def _():
        whole = jnp.concatenate([parts[...], extra[...]], axis=1).astype(BF16)
        copies[...] = jnp.broadcast_to(whole[None], copies.shape)


def last_kernel(
    meta, scale, k, scaled, state, key_in, value_in,
    key_grad_own, key_grad_other, value_grad_own, value_grad_other,
):
    rows = k.shape[0]
    tok = rows // 2
    spans = rows // SPAN
    for h in range(state.shape[0]):
        lanes = lanes_of(h)
        key_grad = (key_in[:, lanes] + dot(scaled[:, lanes], state[h], NT)).astype(BF16)
        key_grad_own[:, lanes] = key_grad[:tok]
        key_grad_other[:, lanes] = key_grad[tok:]
        scaled_grad = value_in[:, lanes] + dot(k[:, lanes], state[h], NN)
        value_grad = (rows_of_members(meta, scale, lanes, spans) * scaled_grad).astype(BF16)
        value_grad_own[:, lanes] = value_grad[:tok]
        value_grad_other[:, lanes] = value_grad[tok:]


def total_kernel(copies, parts):
    count, _, lanes = copies.shape
    halves = []
    for first in range(2):
        total = copies[first].astype(F32)
        for at in range(first + 2, count, 2):
            total = total + copies[at].astype(F32)
        halves.append(total)
    wide_line = lanes - DH
    both = halves[0][:, :wide_line] + halves[1][:, :wide_line]
    groups = [both[i : i + MEMBERS] for i in range(0, both.shape[0], MEMBERS)]
    found = [jnp.concatenate(groups, axis=1)]
    for total in halves:
        lines = total[:, wide_line:]
        width = parts.shape[1] // DH
        for m in range(lines.shape[0] // width):
            row = [lines[m * width + i : m * width + i + 1] for i in range(width)]
            found.append(jnp.concatenate(row, axis=1))
    parts[...] = jnp.concatenate(found, axis=0)


def running_kernel(backward, pieces, sums):
    count = pieces.shape[0]
    total = jnp.zeros(pieces.shape[1:], F32)
    order = range(count - 1, -1, -1) if backward else range(count)
    for at in order:
        sums[at] = total.astype(BF16)
        total = total + pieces[at].astype(F32)


class Local:
    def __init__(self, tok, width):
        self.tok = tok
        self.width = width
        self.block = STEP_HEADS * DH
        self.steps = width // self.block

    def shared(self, rows):
        steps = self.steps
        return pl.BlockSpec((rows, self.block), lambda i, place, *_: (0, place[0] * steps + i))

    def cols(self, rows):
        return pl.BlockSpec((rows, self.block), lambda i, *_: (0, i))

    def state(self):
        return pl.BlockSpec((STEP_HEADS, DH, DH), lambda i, *_: (i, 0, 0))

    def whole(self, shape):
        return pl.BlockSpec(shape, lambda i, *_: (0,) * len(shape))

    def call(self, body, meta, ins, outs, args, shapes, name, scratch=(), flops=0):
        moved = sum(a.size * a.dtype.itemsize for a in args)
        return pl.pallas_call(
            with_meta(body),
            grid_spec=pltpu.PrefetchScalarGridSpec(
                num_scalar_prefetch=len(meta),
                grid=(self.steps,),
                in_specs=ins,
                out_specs=outs,
                scratch_shapes=scratch,
            ),
            out_shape=shapes,
            name=name,
            compiler_params=pltpu.CompilerParams(vmem_limit_bytes=VMEM_BYTES),
            cost_estimate=pl.CostEstimate(flops=flops, bytes_accessed=2 * moved, transcendentals=0),
        )(*meta, *args)


def fast(x):
    return pltpu.with_memory_space_constraint(x, pltpu.VMEM)


def slow(x):
    return pltpu.with_memory_space_constraint(x, pltpu.HBM)


def running_sums(pieces, backward):
    return pl.pallas_call(
        functools.partial(running_kernel, backward),
        out_shape=pltpu.HBM(pieces.shape, BF16),
        name="running_sums",
        compiler_params=pltpu.CompilerParams(vmem_limit_bytes=VMEM_BYTES),
    )(fast(pieces))


def make_shards(n_seq, n_head):
    chips = n_seq // CORES
    group = CORES * n_head

    def swap(x):
        return lax.ppermute(x, "core", [(0, 1), (1, 0)])

    def scattered(pieces):
        return lax.all_to_all(pieces, "chip", 0, 0, tiled=True)

    def scanned(delta, backward, beside=None):
        heads = delta.shape[0]
        pieces = scattered(delta.reshape(chips, heads * DH // chips, DH))
        if beside is not None:
            pieces, beside = lax.optimization_barrier((pieces, beside))
        state = scattered(running_sums(pieces, backward)).reshape(heads, DH, DH)
        return state if beside is None else (state,) + beside

    def side_by_side(core, own, other):
        return jnp.where(
            core == 0,
            jnp.concatenate([own, other], axis=1),
            jnp.concatenate([other, own], axis=1),
        )

    def shards(queries, key_vectors, value_vectors, cotangent, member_ids, in_scale, out_scale):
        tok, both = queries.shape
        width = both // CORES
        heads = width // DH
        full_width = both * n_head
        rows = 2 * tok
        core = lax.axis_index("core")

        other_ids = swap(member_ids)
        v_other = swap(value_vectors)
        k_other = swap(key_vectors)
        place = core[None].astype(jnp.int32)
        local = Local(tok, width)
        shared, cols, state = local.shared, local.cols, local.state
        half = pltpu.HBM((tok, width), BF16)
        low = pltpu.HBM((rows, width), BF16)
        wide = pltpu.HBM((rows, width), F32)
        part = pltpu.HBM((MEMBERS, width), F32)
        sent = pltpu.HBM((heads, DH, DH), BF16)
        pairs = [shared(tok), shared(tok)]
        lines, wide_line = LANE_GROUPS * MEMBERS, width // LANE_GROUPS
        packed = (chips, lines, wide_line + DH)
        unit = 2 * heads * rows * DH * DH

        meta = (place, member_ids, other_ids)
        scaled, delta = local.call(
            states_kernel,
            meta,
            [shared(MEMBERS)] + pairs * 2,
            [cols(rows), state()],
            (slow(in_scale), slow(key_vectors), fast(k_other), slow(value_vectors), fast(v_other)),
            [low, sent],
            "states",
            flops=unit,
        )
        queries_late, cotangent_late, delta = lax.optimization_barrier((queries, cotangent, delta))
        q_other = swap(queries_late)
        c_other = swap(cotangent_late)
        state_in = scanned(delta, False)
        inside, q, k, v, c = local.call(
            inside_kernel,
            meta,
            pairs * 4 + [cols(rows)],
            [cols(rows)] * 5,
            (
                slow(queries), slow(q_other), slow(key_vectors), slow(k_other),
                slow(value_vectors), slow(v_other), slow(cotangent), slow(c_other), slow(scaled),
            ),
            [low] * 5,
            "inside",
            flops=4 * unit,
        )
        q, k, v, c = slow(q), slow(k), slow(v), slow(c)
        mixed, sums = local.call(
            mixed_kernel,
            meta,
            [shared(MEMBERS), cols(rows), cols(rows), state(), cols(rows)],
            [cols(rows), local.whole((group, 2, rows))],
            (slow(out_scale), q, c, fast(state_in), slow(inside)),
            [low, pltpu.HBM((group, 2, rows), F32)],
            "mixed",
            scratch=[pltpu.VMEM((rows, DH), F32)] * 2,
            flops=unit,
        )
        sums = lax.all_to_all(sums, ("core", "head"), 0, 0, tiled=True)
        grad, delta_after = local.call(
            functools.partial(grads_kernel, full_width),
            meta,
            [shared(MEMBERS)] + [cols(rows)] * 3 + [local.whole((group, 2, rows))],
            [cols(rows), state()],
            (slow(out_scale), q, c, slow(mixed), sums),
            [low, sent],
            "grads",
            scratch=[pltpu.VMEM((2, rows, DH), F32)],
            flops=unit,
        )
        out_part = local.call(
            functools.partial(outs_kernel, full_width),
            meta,
            [cols(rows)] * 2 + [local.whole((group, 2, rows))],
            cols(MEMBERS),
            (c, slow(mixed), sums),
            part,
            "outs",
        )
        query_own, query_send = local.call(
            query_kernel,
            meta,
            [cols(rows)] * 3 + [state()],
            [cols(tok)] * 2,
            (k, slow(scaled), slow(grad), slow(state_in)),
            [half] * 2,
            "query",
            flops=5 * unit,
        )
        out_part = out_part + lax.ppermute(out_part, "chip", [(i, i ^ 1) for i in range(chips)])
        mine = MEMBERS // 2
        first = lax.axis_index("chip") % 2 * mine
        extra = lax.dynamic_slice_in_dim(out_part, first, mine, 0).reshape(lines, DH)
        state_after, query_own, extra = scanned(delta_after, True, (query_own, extra))
        key_in, value_in, in_part = local.call(
            back_kernel,
            meta,
            [cols(rows)] * 5,
            [cols(rows), cols(rows), cols(MEMBERS)],
            (q, k, v, slow(scaled), slow(grad)),
            [wide, wide, part],
            "back",
            flops=8 * unit,
        )
        query_grad = side_by_side(core, query_own, swap(query_send))
        copies = local.call(
            copies_kernel,
            meta,
            [cols(rows), cols(rows), state(), cols(MEMBERS), local.whole((lines, DH))],
            local.whole(packed),
            (k, v, fast(state_after), slow(in_part), extra),
            pltpu.HBM(packed, BF16),
            "copies",
            scratch=[pltpu.VMEM((lines, wide_line), F32)],
            flops=unit,
        )
        copies = scattered(copies)
        key_own, key_send, value_own, value_send = local.call(
            last_kernel,
            meta,
            [shared(MEMBERS), cols(rows), cols(rows), state(), cols(rows), cols(rows)],
            [cols(tok)] * 4,
            (slow(in_scale), k, slow(scaled), slow(state_after), slow(key_in), slow(value_in)),
            [half] * 4,
            "last",
            flops=2 * unit,
        )
        key_grad = side_by_side(core, key_own, swap(key_send))
        value_grad = side_by_side(core, value_own, swap(value_send))
        copies, key_grad, value_grad, query_grad = lax.optimization_barrier(
            (copies, key_grad, value_grad, query_grad)
        )
        parts = pl.pallas_call(
            total_kernel,
            out_shape=jax.ShapeDtypeStruct((2 * MEMBERS, width), F32),
            name="total",
            compiler_params=pltpu.CompilerParams(vmem_limit_bytes=VMEM_BYTES),
        )(copies)
        parts = side_by_side(core, parts, swap(parts))
        return query_grad, key_grad, value_grad, parts[:MEMBERS], parts[MEMBERS:]

    return shards


def solution(mesh):
    n_seq, n_head = mesh.shape["seq"], mesh.shape["head"]
    chips = n_seq // CORES
    finer = Mesh(mesh.devices.reshape(chips, CORES, n_head), ("chip", "core", "head"))
    tokens = ("chip", "core")
    wide = P(tokens, "head")
    scale = P(None, "head")
    return jax.shard_map(
        make_shards(n_seq, n_head),
        mesh=finer,
        in_specs=(wide, wide, wide, wide, P(tokens), scale, scale),
        out_specs=(wide, wide, wide, scale, scale),
        check_vma=False,
    )
```

```python
import functools

import jax
import jax.numpy as jnp
from jax import lax
from jax.experimental import pallas as pl
from jax.experimental.pallas import tpu as pltpu
from jax.sharding import Mesh, PartitionSpec as P

DH = 128
SPAN = 16
MEMBERS = 4
EPS = 1e-06
CORES = 2
STEP_HEADS = 4
LANE_GROUPS = 4
VMEM_BYTES = 24 * 2**20
F32 = jnp.float32
BF16 = jnp.bfloat16

NN = (((1,), (0,)), ((), ()))
NT = (((1,), (1,)), ((), ()))
TN = (((0,), (0,)), ((), ()))


class Meta:
    def __init__(self, place, own_ids, other_ids):
        self.core = place[0]
        self.ids = [own_ids[s] for s in range(own_ids.shape[0])]
        self.ids += [other_ids[s] for s in range(other_ids.shape[0])]


def with_meta(body):
    def kernel(place, own_ids, other_ids, *refs):
        body(Meta(place, own_ids, other_ids), *refs)

    return kernel


def dot(a, b, dims):
    return lax.dot_general(a, b, dims, preferred_element_type=F32)


def pair(own, other, lanes):
    return jnp.concatenate([own[:, lanes], other[:, lanes]], axis=0)


def rows_of_members(meta, scale, lanes, spans):
    choices = [scale[m : m + 1, lanes] for m in range(MEMBERS)]
    rows = []
    for s in range(spans):
        row = choices[0]
        for m in range(1, MEMBERS):
            row = jnp.where(meta.ids[s] == m, choices[m], row)
        rows.append(jnp.broadcast_to(row, (SPAN, DH)))
    return jnp.concatenate(rows, axis=0)


def member_sums(meta, x, spans):
    totals = [jnp.zeros((8, DH), F32) for _ in range(MEMBERS)]
    for s in range(spans):
        part = x[s * SPAN : s * SPAN + 8] + x[s * SPAN + 8 : (s + 1) * SPAN]
        for m in range(MEMBERS):
            keep = jnp.where(meta.ids[s] == m, 1.0, 0.0).astype(F32)
            totals[m] = totals[m] + keep * part
    return jnp.concatenate([jnp.sum(t, axis=0, keepdims=True) for t in totals], axis=0)


def causal_mask(meta, tok):
    size = 2 * tok
    core = meta.core
    base_own = core * tok
    base_other = (1 - core) * tok - tok

    def place(axis):
        at = lax.broadcasted_iota(jnp.int32, (size, size), axis)
        return at + jnp.where(at < tok, base_own, base_other)

    return place(0) >= place(1)


def in_order(meta, x, tok):
    turned = jnp.concatenate([x[:, tok:], x[:, :tok]], axis=1)
    return jnp.where(meta.core == 0, x, turned)


def head_sums(meta, sums, tok):
    total = sums[0]
    for at in range(1, sums.shape[0]):
        total = total + sums[at]
    return in_order(meta, total, tok)


def lanes_of(h):
    return pl.ds(h * DH, DH)


def states_kernel(meta, scale, k_own, k_other, v_own, v_other, scaled, delta):
    tok = k_own.shape[0]
    spans = 2 * tok // SPAN
    for h in range(delta.shape[0]):
        lanes = lanes_of(h)
        value = pair(v_own, v_other, lanes).astype(F32)
        low = (rows_of_members(meta, scale, lanes, spans) * value).astype(BF16)
        scaled[:, lanes] = low
        delta[h] = dot(pair(k_own, k_other, lanes), low, TN).astype(BF16)


def inside_kernel(
    meta, q_own, q_other, k_own, k_other, v_own, v_other, c_own, c_other, scaled,
    inside, q, k, v, c,
):
    tok = q_own.shape[0]
    causal = causal_mask(meta, tok)
    for both, own, other in ((q, q_own, q_other), (k, k_own, k_other), (v, v_own, v_other), (c, c_own, c_other)):
        both[:tok] = own[...]
        both[tok:] = other[...]
    for h in range(scaled.shape[1] // DH):
        lanes = lanes_of(h)
        scores = dot(q[:, lanes], k[:, lanes], NT)
        weights = jnp.where(causal, scores, 0.0).astype(BF16)
        inside[:, lanes] = dot(weights, scaled[:, lanes], NN)


def mixed_kernel(
    meta, scale, q, c, state, inside, mixed, sums, squares, crosses
):
    rows = q.shape[0]
    tok = rows // 2
    spans = rows // SPAN
    step = pl.program_id(0)

    @pl.when(step == 0)
    def _():
        squares[...] = jnp.zeros_like(squares)
        crosses[...] = jnp.zeros_like(crosses)

    heads = [lanes_of(h) for h in range(state.shape[0])]
    for h, lanes in enumerate(heads):
        mixed[:, lanes] = inside[:, lanes] + dot(q[:, lanes], state[h], NN)
    for s in range(spans):
        span = pl.ds(s * SPAN, SPAN)
        square, cross = squares[span], crosses[span]
        for lanes in heads:
            row = scale[0:1, lanes]
            for m in range(1, MEMBERS):
                row = jnp.where(meta.ids[s] == m, scale[m : m + 1, lanes], row)
            mix = mixed[span, lanes]
            square = square + mix * mix
            cross = cross + row * c[span, lanes].astype(F32) * mix
        squares[span] = square
        crosses[span] = cross

    @pl.when(step == pl.num_programs(0) - 1)
    def _():
        totals = [jnp.sum(jnp.transpose(t[...]), axis=0, keepdims=True) for t in (squares, crosses)]
        totals = in_order(meta, jnp.concatenate(totals, axis=0), tok)
        sums[...] = jnp.broadcast_to(totals[None], sums.shape)


def grads_kernel(
    full_width, meta, scale, q, c, mixed, sums, grad, delta, turned
):
    rows = q.shape[0]
    tok = rows // 2
    spans = rows // SPAN

    @pl.when(pl.program_id(0) == 0)
    def _():
        totals = head_sums(meta, sums, tok)
        rms = jnp.sqrt(totals[0:1] / full_width + EPS)
        turned[0] = jnp.transpose(jnp.broadcast_to(1.0 / rms, (DH, 2 * tok)))
        factor = totals[1:2] / (full_width * rms * rms * rms)
        turned[1] = jnp.transpose(jnp.broadcast_to(factor, (DH, 2 * tok)))

    inverse, factor = turned[0], turned[1]
    for h in range(delta.shape[0]):
        lanes = lanes_of(h)
        cot = c[:, lanes].astype(F32) * inverse
        mix = mixed[:, lanes]
        low = (rows_of_members(meta, scale, lanes, spans) * cot - mix * factor).astype(BF16)
        grad[:, lanes] = low
        delta[h] = dot(q[:, lanes], low, TN).astype(BF16)


def query_kernel(meta, k, scaled, grad, state, query_own, query_other):
    tok = k.shape[0] // 2
    causal = causal_mask(meta, tok)
    for h in range(state.shape[0]):
        lanes = lanes_of(h)
        g = grad[:, lanes]
        grad_weights = jnp.where(causal, dot(g, scaled[:, lanes], NT), 0.0).astype(BF16)
        query_grad = (dot(grad_weights, k[:, lanes], NN) + dot(g, state[h], NT)).astype(BF16)
        query_own[:, lanes] = query_grad[:tok]
        query_other[:, lanes] = query_grad[tok:]


def outs_kernel(full_width, meta, c, mixed, sums, out_part):
    rows = c.shape[0]
    spans = rows // SPAN
    totals = head_sums(meta, sums, rows // 2)
    inverse = 1.0 / jnp.sqrt(totals[0:1] / full_width + EPS)
    inverse = jnp.transpose(jnp.broadcast_to(inverse, (DH, rows)))
    for h in range(mixed.shape[1] // DH):
        lanes = lanes_of(h)
        normed = c[:, lanes].astype(F32) * (mixed[:, lanes] * inverse)
        out_part[:, lanes] = member_sums(meta, normed, spans)


def back_kernel(meta, q, k, v, scaled, grad, key_in, value_in, in_part):
    rows = k.shape[0]
    tok = rows // 2
    spans = rows // SPAN
    causal = causal_mask(meta, tok)
    for h in range(scaled.shape[1] // DH):
        lanes = lanes_of(h)
        query, g = q[:, lanes], grad[:, lanes]
        weights = jnp.where(causal, dot(query, k[:, lanes], NT), 0.0).astype(BF16)
        grad_weights = jnp.where(causal, dot(g, scaled[:, lanes], NT), 0.0).astype(BF16)
        key_in[:, lanes] = dot(grad_weights, query, TN)
        inner = dot(weights, g, TN)
        value_in[:, lanes] = inner
        in_part[:, lanes] = member_sums(meta, v[:, lanes].astype(F32) * inner, spans)


def copies_kernel(meta, k, v, state, known, extra, copies, parts):
    spans = k.shape[0] // SPAN
    step = pl.program_id(0)
    found = []
    for h in range(state.shape[0]):
        lanes = lanes_of(h)
        value = v[:, lanes].astype(F32)
        across = dot(k[:, lanes], state[h], NN)
        found.append(known[:, lanes] + member_sums(meta, value * across, spans))
    per_row = parts.shape[1] // DH
    rows = [
        jnp.concatenate(found[at : at + per_row], axis=1) for at in range(0, len(found), per_row)
    ]
    rows = jnp.concatenate(rows, axis=0)
    count = rows.shape[0]
    parts[pl.ds(pl.multiple_of(step * count, count), count)] = rows

    @pl.when(step == pl.num_programs(0) - 1)
    def _():
        whole = jnp.concatenate([parts[...], extra[...]], axis=1).astype(BF16)
        copies[...] = jnp.broadcast_to(whole[None], copies.shape)


def last_kernel(
    meta, scale, k, scaled, state, key_in, value_in,
    key_grad_own, key_grad_other, value_grad_own, value_grad_other,
):
    rows = k.shape[0]
    tok = rows // 2
    spans = rows // SPAN
    for h in range(state.shape[0]):
        lanes = lanes_of(h)
        key_grad = (key_in[:, lanes] + dot(scaled[:, lanes], state[h], NT)).astype(BF16)
        key_grad_own[:, lanes] = key_grad[:tok]
        key_grad_other[:, lanes] = key_grad[tok:]
        scaled_grad = value_in[:, lanes] + dot(k[:, lanes], state[h], NN)
        value_grad = (rows_of_members(meta, scale, lanes, spans) * scaled_grad).astype(BF16)
        value_grad_own[:, lanes] = value_grad[:tok]
        value_grad_other[:, lanes] = value_grad[tok:]


def total_kernel(copies, parts):
    count, _, lanes = copies.shape
    halves = []
    for first in range(2):
        total = copies[first].astype(F32)
        for at in range(first + 2, count, 2):
            total = total + copies[at].astype(F32)
        halves.append(total)
    wide_line = lanes - DH
    both = halves[0][:, :wide_line] + halves[1][:, :wide_line]
    groups = [both[i : i + MEMBERS] for i in range(0, both.shape[0], MEMBERS)]
    found = [jnp.concatenate(groups, axis=1)]
    for total in halves:
        lines = total[:, wide_line:]
        width = parts.shape[1] // DH
        for m in range(lines.shape[0] // width):
            row = [lines[m * width + i : m * width + i + 1] for i in range(width)]
            found.append(jnp.concatenate(row, axis=1))
    parts[...] = jnp.concatenate(found, axis=0)


def running_kernel(backward, pieces, sums):
    count = pieces.shape[0]
    total = jnp.zeros(pieces.shape[1:], F32)
    order = range(count - 1, -1, -1) if backward else range(count)
    for at in order:
        sums[at] = total.astype(BF16)
        total = total + pieces[at].astype(F32)


class Local:
    def __init__(self, tok, width):
        self.tok = tok
        self.width = width
        self.block = STEP_HEADS * DH
        self.steps = width // self.block

    def shared(self, rows):
        steps = self.steps
        return pl.BlockSpec((rows, self.block), lambda i, place, *_: (0, place[0] * steps + i))

    def cols(self, rows):
        return pl.BlockSpec((rows, self.block), lambda i, *_: (0, i))

    def state(self):
        return pl.BlockSpec((STEP_HEADS, DH, DH), lambda i, *_: (i, 0, 0))

    def whole(self, shape):
        return pl.BlockSpec(shape, lambda i, *_: (0,) * len(shape))

    def call(self, body, meta, ins, outs, args, shapes, name, scratch=(), flops=0):
        moved = sum(a.size * a.dtype.itemsize for a in args)
        return pl.pallas_call(
            with_meta(body),
            grid_spec=pltpu.PrefetchScalarGridSpec(
                num_scalar_prefetch=len(meta),
                grid=(self.steps,),
                in_specs=ins,
                out_specs=outs,
                scratch_shapes=scratch,
            ),
            out_shape=shapes,
            name=name,
            compiler_params=pltpu.CompilerParams(vmem_limit_bytes=VMEM_BYTES),
            cost_estimate=pl.CostEstimate(flops=flops, bytes_accessed=2 * moved, transcendentals=0),
        )(*meta, *args)


def fast(x):
    return pltpu.with_memory_space_constraint(x, pltpu.VMEM)


def slow(x):
    return pltpu.with_memory_space_constraint(x, pltpu.HBM)


def running_sums(pieces, backward):
    return pl.pallas_call(
        functools.partial(running_kernel, backward),
        out_shape=pltpu.HBM(pieces.shape, BF16),
        name="running_sums",
        compiler_params=pltpu.CompilerParams(vmem_limit_bytes=VMEM_BYTES),
    )(fast(pieces))


def make_shards(n_seq, n_head):
    chips = n_seq // CORES
    group = CORES * n_head

    def swap(x):
        return lax.ppermute(x, "core", [(0, 1), (1, 0)])

    def scattered(pieces):
        return lax.all_to_all(pieces, "chip", 0, 0, tiled=True)

    def scanned(delta, backward, beside=None):
        heads = delta.shape[0]
        pieces = scattered(delta.reshape(chips, heads * DH // chips, DH))
        if beside is not None:
            pieces, beside = lax.optimization_barrier((pieces, beside))
        state = scattered(running_sums(pieces, backward)).reshape(heads, DH, DH)
        return state if beside is None else (state,) + beside

    def side_by_side(core, own, other):
        return jnp.where(
            core == 0,
            jnp.concatenate([own, other], axis=1),
            jnp.concatenate([other, own], axis=1),
        )

    def shards(queries, key_vectors, value_vectors, cotangent, member_ids, in_scale, out_scale):
        tok, both = queries.shape
        width = both // CORES
        heads = width // DH
        full_width = both * n_head
        rows = 2 * tok
        core = lax.axis_index("core")

        other_ids = swap(member_ids)
        v_other = swap(value_vectors)
        k_other = swap(key_vectors)
        place = core[None].astype(jnp.int32)
        local = Local(tok, width)
        shared, cols, state = local.shared, local.cols, local.state
        half = pltpu.HBM((tok, width), BF16)
        low = pltpu.HBM((rows, width), BF16)
        wide = pltpu.HBM((rows, width), F32)
        part = pltpu.HBM((MEMBERS, width), F32)
        sent = pltpu.HBM((heads, DH, DH), BF16)
        pairs = [shared(tok), shared(tok)]
        lines, wide_line = LANE_GROUPS * MEMBERS, width // LANE_GROUPS
        packed = (chips, lines, wide_line + DH)
        unit = 2 * heads * rows * DH * DH

        meta = (place, member_ids, other_ids)
        scaled, delta = local.call(
            states_kernel,
            meta,
            [shared(MEMBERS)] + pairs * 2,
            [cols(rows), state()],
            (slow(in_scale), slow(key_vectors), fast(k_other), slow(value_vectors), fast(v_other)),
            [low, sent],
            "states",
            flops=unit,
        )
        queries_late, cotangent_late, delta = lax.optimization_barrier((queries, cotangent, delta))
        q_other = swap(queries_late)
        c_other = swap(cotangent_late)
        state_in = scanned(delta, False)
        inside, q, k, v, c = local.call(
            inside_kernel,
            meta,
            pairs * 4 + [cols(rows)],
            [cols(rows)] * 5,
            (
                slow(queries), slow(q_other), slow(key_vectors), slow(k_other),
                slow(value_vectors), slow(v_other), slow(cotangent), slow(c_other), slow(scaled),
            ),
            [wide] + [low] * 4,
            "inside",
            flops=4 * unit,
        )
        q, k, v, c = slow(q), slow(k), slow(v), slow(c)
        mixed, sums = local.call(
            mixed_kernel,
            meta,
            [shared(MEMBERS), cols(rows), cols(rows), state(), cols(rows)],
            [cols(rows), local.whole((group, 2, rows))],
            (slow(out_scale), q, c, fast(state_in), slow(inside)),
            [wide, pltpu.HBM((group, 2, rows), F32)],
            "mixed",
            scratch=[pltpu.VMEM((rows, DH), F32)] * 2,
            flops=unit,
        )
        sums = lax.all_to_all(sums, ("core", "head"), 0, 0, tiled=True)
        grad, delta_after = local.call(
            functools.partial(grads_kernel, full_width),
            meta,
            [shared(MEMBERS)] + [cols(rows)] * 3 + [local.whole((group, 2, rows))],
            [cols(rows), state()],
            (slow(out_scale), q, c, slow(mixed), sums),
            [low, sent],
            "grads",
            scratch=[pltpu.VMEM((2, rows, DH), F32)],
            flops=unit,
        )
        out_part = local.call(
            functools.partial(outs_kernel, full_width),
            meta,
            [cols(rows)] * 2 + [local.whole((group, 2, rows))],
            cols(MEMBERS),
            (c, slow(mixed), sums),
            part,
            "outs",
        )
        query_own, query_send = local.call(
            query_kernel,
            meta,
            [cols(rows)] * 3 + [state()],
            [cols(tok)] * 2,
            (k, slow(scaled), slow(grad), slow(state_in)),
            [half] * 2,
            "query",
            flops=5 * unit,
        )
        out_part = out_part + lax.ppermute(out_part, "chip", [(i, i ^ 1) for i in range(chips)])
        mine = MEMBERS // 2
        first = lax.axis_index("chip") % 2 * mine
        extra = lax.dynamic_slice_in_dim(out_part, first, mine, 0).reshape(lines, DH)
        state_after, query_own, extra = scanned(delta_after, True, (query_own, extra))
        key_in, value_in, in_part = local.call(
            back_kernel,
            meta,
            [cols(rows)] * 5,
            [cols(rows), cols(rows), cols(MEMBERS)],
            (q, k, v, slow(scaled), slow(grad)),
            [wide, wide, part],
            "back",
            flops=8 * unit,
        )
        query_grad = side_by_side(core, query_own, swap(query_send))
        copies = local.call(
            copies_kernel,
            meta,
            [cols(rows), cols(rows), state(), cols(MEMBERS), local.whole((lines, DH))],
            local.whole(packed),
            (k, v, fast(state_after), slow(in_part), extra),
            pltpu.HBM(packed, BF16),
            "copies",
            scratch=[pltpu.VMEM((lines, wide_line), F32)],
            flops=unit,
        )
        copies = scattered(copies)
        key_own, key_send, value_own, value_send = local.call(
            last_kernel,
            meta,
            [shared(MEMBERS), cols(rows), cols(rows), state(), cols(rows), cols(rows)],
            [cols(tok)] * 4,
            (slow(in_scale), k, slow(scaled), slow(state_after), slow(key_in), slow(value_in)),
            [half] * 4,
            "last",
            flops=2 * unit,
        )
        key_grad = side_by_side(core, key_own, swap(key_send))
        value_grad = side_by_side(core, value_own, swap(value_send))
        copies, key_grad, value_grad, query_grad = lax.optimization_barrier(
            (copies, key_grad, value_grad, query_grad)
        )
        parts = pl.pallas_call(
            total_kernel,
            out_shape=jax.ShapeDtypeStruct((2 * MEMBERS, width), F32),
            name="total",
            compiler_params=pltpu.CompilerParams(vmem_limit_bytes=VMEM_BYTES),
        )(copies)
        parts = side_by_side(core, parts, swap(parts))
        return query_grad, key_grad, value_grad, parts[:MEMBERS], parts[MEMBERS:]

    return shards


def solution(mesh):
    n_seq, n_head = mesh.shape["seq"], mesh.shape["head"]
    chips = n_seq // CORES
    finer = Mesh(mesh.devices.reshape(chips, CORES, n_head), ("chip", "core", "head"))
    tokens = ("chip", "core")
    wide = P(tokens, "head")
    scale = P(None, "head")
    return jax.shard_map(
        make_shards(n_seq, n_head),
        mesh=finer,
        in_specs=(wide, wide, wide, wide, P(tokens), scale, scale),
        out_specs=(wide, wide, wide, scale, scale),
        check_vma=False,
    )
```

```python
import functools

import jax
import jax.numpy as jnp
from jax import lax
from jax.experimental import pallas as pl
from jax.experimental.pallas import tpu as pltpu
from jax.sharding import Mesh, PartitionSpec as P

DH = 128
SPAN = 16
MEMBERS = 4
EPS = 1e-06
CORES = 2
STEP_HEADS = 4
LANE_GROUPS = 4
VMEM_BYTES = 24 * 2**20
F32 = jnp.float32
BF16 = jnp.bfloat16

NN = (((1,), (0,)), ((), ()))
NT = (((1,), (1,)), ((), ()))
TN = (((0,), (0,)), ((), ()))


class Meta:
    def __init__(self, place, own_ids, other_ids):
        self.core = place[0]
        self.ids = [own_ids[s] for s in range(own_ids.shape[0])]
        self.ids += [other_ids[s] for s in range(other_ids.shape[0])]


def with_meta(body):
    def kernel(place, own_ids, other_ids, *refs):
        body(Meta(place, own_ids, other_ids), *refs)

    return kernel


def dot(a, b, dims):
    return lax.dot_general(a, b, dims, preferred_element_type=F32)


def pair(own, other, lanes):
    return jnp.concatenate([own[:, lanes], other[:, lanes]], axis=0)


def rows_of_members(meta, scale, lanes, spans):
    choices = [scale[m : m + 1, lanes] for m in range(MEMBERS)]
    rows = []
    for s in range(spans):
        row = choices[0]
        for m in range(1, MEMBERS):
            row = jnp.where(meta.ids[s] == m, choices[m], row)
        rows.append(jnp.broadcast_to(row, (SPAN, DH)))
    return jnp.concatenate(rows, axis=0)


def member_sums(meta, x, spans):
    totals = [jnp.zeros((8, DH), F32) for _ in range(MEMBERS)]
    for s in range(spans):
        part = x[s * SPAN : s * SPAN + 8] + x[s * SPAN + 8 : (s + 1) * SPAN]
        for m in range(MEMBERS):
            keep = jnp.where(meta.ids[s] == m, 1.0, 0.0).astype(F32)
            totals[m] = totals[m] + keep * part
    return jnp.concatenate([jnp.sum(t, axis=0, keepdims=True) for t in totals], axis=0)


def causal_mask(meta, tok):
    size = 2 * tok
    core = meta.core
    base_own = core * tok
    base_other = (1 - core) * tok - tok

    def place(axis):
        at = lax.broadcasted_iota(jnp.int32, (size, size), axis)
        return at + jnp.where(at < tok, base_own, base_other)

    return place(0) >= place(1)


def in_order(meta, x, tok):
    turned = jnp.concatenate([x[:, tok:], x[:, :tok]], axis=1)
    return jnp.where(meta.core == 0, x, turned)


def head_sums(meta, sums, tok):
    total = sums[0]
    for at in range(1, sums.shape[0]):
        total = total + sums[at]
    return in_order(meta, total, tok)


def lanes_of(h):
    return pl.ds(h * DH, DH)


def states_kernel(meta, scale, k_own, k_other, v_own, v_other, scaled, delta):
    tok = k_own.shape[0]
    spans = 2 * tok // SPAN
    for h in range(delta.shape[0]):
        lanes = lanes_of(h)
        value = pair(v_own, v_other, lanes).astype(F32)
        low = (rows_of_members(meta, scale, lanes, spans) * value).astype(BF16)
        scaled[:, lanes] = low
        delta[h] = dot(pair(k_own, k_other, lanes), low, TN).astype(BF16)


def inside_kernel(
    meta, q_own, q_other, k_own, k_other, v_own, v_other, c_own, c_other, scaled,
    inside, q, k, v, c,
):
    tok = q_own.shape[0]
    causal = causal_mask(meta, tok)
    for both, own, other in ((q, q_own, q_other), (k, k_own, k_other), (v, v_own, v_other), (c, c_own, c_other)):
        both[:tok] = own[...]
        both[tok:] = other[...]
    for h in range(scaled.shape[1] // DH):
        lanes = lanes_of(h)
        scores = dot(q[:, lanes], k[:, lanes], NT)
        weights = jnp.where(causal, scores, 0.0).astype(BF16)
        inside[:, lanes] = dot(weights, scaled[:, lanes], NN).astype(BF16)


def mixed_kernel(
    meta, scale, q, c, state, inside, mixed, sums, squares, crosses
):
    rows = q.shape[0]
    tok = rows // 2
    spans = rows // SPAN
    step = pl.program_id(0)

    @pl.when(step == 0)
    def _():
        squares[...] = jnp.zeros_like(squares)
        crosses[...] = jnp.zeros_like(crosses)

    heads = [lanes_of(h) for h in range(state.shape[0])]
    for h, lanes in enumerate(heads):
        mix = inside[:, lanes].astype(F32) + dot(q[:, lanes], state[h], NN)
        mixed[:, lanes] = mix.astype(BF16)
    for s in range(spans):
        span = pl.ds(s * SPAN, SPAN)
        square, cross = squares[span], crosses[span]
        for lanes in heads:
            row = scale[0:1, lanes]
            for m in range(1, MEMBERS):
                row = jnp.where(meta.ids[s] == m, scale[m : m + 1, lanes], row)
            mix = mixed[span, lanes].astype(F32)
            square = square + mix * mix
            cross = cross + row * c[span, lanes].astype(F32) * mix
        squares[span] = square
        crosses[span] = cross

    @pl.when(step == pl.num_programs(0) - 1)
    def _():
        totals = [jnp.sum(jnp.transpose(t[...]), axis=0, keepdims=True) for t in (squares, crosses)]
        totals = in_order(meta, jnp.concatenate(totals, axis=0), tok)
        sums[...] = jnp.broadcast_to(totals[None], sums.shape)


def grads_kernel(
    full_width, meta, scale, q, c, mixed, sums, grad, delta, turned
):
    rows = q.shape[0]
    tok = rows // 2
    spans = rows // SPAN

    @pl.when(pl.program_id(0) == 0)
    def _():
        totals = head_sums(meta, sums, tok)
        rms = jnp.sqrt(totals[0:1] / full_width + EPS)
        turned[0] = jnp.transpose(jnp.broadcast_to(1.0 / rms, (DH, 2 * tok)))
        factor = totals[1:2] / (full_width * rms * rms * rms)
        turned[1] = jnp.transpose(jnp.broadcast_to(factor, (DH, 2 * tok)))

    inverse, factor = turned[0], turned[1]
    for h in range(delta.shape[0]):
        lanes = lanes_of(h)
        cot = c[:, lanes].astype(F32) * inverse
        mix = mixed[:, lanes].astype(F32)
        low = (rows_of_members(meta, scale, lanes, spans) * cot - mix * factor).astype(BF16)
        grad[:, lanes] = low
        delta[h] = dot(q[:, lanes], low, TN).astype(BF16)


def query_kernel(meta, k, scaled, grad, state, query_own, query_other):
    tok = k.shape[0] // 2
    causal = causal_mask(meta, tok)
    for h in range(state.shape[0]):
        lanes = lanes_of(h)
        g = grad[:, lanes]
        grad_weights = jnp.where(causal, dot(g, scaled[:, lanes], NT), 0.0).astype(BF16)
        query_grad = (dot(grad_weights, k[:, lanes], NN) + dot(g, state[h], NT)).astype(BF16)
        query_own[:, lanes] = query_grad[:tok]
        query_other[:, lanes] = query_grad[tok:]


def outs_kernel(full_width, meta, c, mixed, sums, out_part):
    rows = c.shape[0]
    spans = rows // SPAN
    totals = head_sums(meta, sums, rows // 2)
    inverse = 1.0 / jnp.sqrt(totals[0:1] / full_width + EPS)
    inverse = jnp.transpose(jnp.broadcast_to(inverse, (DH, rows)))
    for h in range(mixed.shape[1] // DH):
        lanes = lanes_of(h)
        normed = c[:, lanes].astype(F32) * (mixed[:, lanes].astype(F32) * inverse)
        out_part[:, lanes] = member_sums(meta, normed, spans)


def back_kernel(meta, q, k, v, scaled, grad, key_in, value_in, in_part):
    rows = k.shape[0]
    tok = rows // 2
    spans = rows // SPAN
    causal = causal_mask(meta, tok)
    for h in range(scaled.shape[1] // DH):
        lanes = lanes_of(h)
        query, g = q[:, lanes], grad[:, lanes]
        weights = jnp.where(causal, dot(query, k[:, lanes], NT), 0.0).astype(BF16)
        grad_weights = jnp.where(causal, dot(g, scaled[:, lanes], NT), 0.0).astype(BF16)
        key_in[:, lanes] = dot(grad_weights, query, TN)
        inner = dot(weights, g, TN)
        value_in[:, lanes] = inner
        in_part[:, lanes] = member_sums(meta, v[:, lanes].astype(F32) * inner, spans)


def copies_kernel(meta, k, v, state, known, extra, copies, parts):
    spans = k.shape[0] // SPAN
    step = pl.program_id(0)
    found = []
    for h in range(state.shape[0]):
        lanes = lanes_of(h)
        value = v[:, lanes].astype(F32)
        across = dot(k[:, lanes], state[h], NN)
        found.append(known[:, lanes] + member_sums(meta, value * across, spans))
    per_row = parts.shape[1] // DH
    rows = [
        jnp.concatenate(found[at : at + per_row], axis=1) for at in range(0, len(found), per_row)
    ]
    rows = jnp.concatenate(rows, axis=0)
    count = rows.shape[0]
    parts[pl.ds(pl.multiple_of(step * count, count), count)] = rows

    @pl.when(step == pl.num_programs(0) - 1)
    def _():
        whole = jnp.concatenate([parts[...], extra[...]], axis=1).astype(BF16)
        copies[...] = jnp.broadcast_to(whole[None], copies.shape)


def last_kernel(
    meta, scale, k, scaled, state, key_in, value_in,
    key_grad_own, key_grad_other, value_grad_own, value_grad_other,
):
    rows = k.shape[0]
    tok = rows // 2
    spans = rows // SPAN
    for h in range(state.shape[0]):
        lanes = lanes_of(h)
        key_grad = (key_in[:, lanes] + dot(scaled[:, lanes], state[h], NT)).astype(BF16)
        key_grad_own[:, lanes] = key_grad[:tok]
        key_grad_other[:, lanes] = key_grad[tok:]
        scaled_grad = value_in[:, lanes] + dot(k[:, lanes], state[h], NN)
        value_grad = (rows_of_members(meta, scale, lanes, spans) * scaled_grad).astype(BF16)
        value_grad_own[:, lanes] = value_grad[:tok]
        value_grad_other[:, lanes] = value_grad[tok:]


def total_kernel(copies, parts):
    count, _, lanes = copies.shape
    halves = []
    for first in range(2):
        total = copies[first].astype(F32)
        for at in range(first + 2, count, 2):
            total = total + copies[at].astype(F32)
        halves.append(total)
    wide_line = lanes - DH
    both = halves[0][:, :wide_line] + halves[1][:, :wide_line]
    groups = [both[i : i + MEMBERS] for i in range(0, both.shape[0], MEMBERS)]
    found = [jnp.concatenate(groups, axis=1)]
    for total in halves:
        lines = total[:, wide_line:]
        width = parts.shape[1] // DH
        for m in range(lines.shape[0] // width):
            row = [lines[m * width + i : m * width + i + 1] for i in range(width)]
            found.append(jnp.concatenate(row, axis=1))
    parts[...] = jnp.concatenate(found, axis=0)


def running_kernel(backward, pieces, sums):
    count = pieces.shape[0]
    total = jnp.zeros(pieces.shape[1:], F32)
    order = range(count - 1, -1, -1) if backward else range(count)
    for at in order:
        sums[at] = total.astype(BF16)
        total = total + pieces[at].astype(F32)


class Local:
    def __init__(self, tok, width):
        self.tok = tok
        self.width = width
        self.block = STEP_HEADS * DH
        self.steps = width // self.block

    def shared(self, rows):
        steps = self.steps
        return pl.BlockSpec((rows, self.block), lambda i, place, *_: (0, place[0] * steps + i))

    def cols(self, rows):
        return pl.BlockSpec((rows, self.block), lambda i, *_: (0, i))

    def state(self):
        return pl.BlockSpec((STEP_HEADS, DH, DH), lambda i, *_: (i, 0, 0))

    def whole(self, shape):
        return pl.BlockSpec(shape, lambda i, *_: (0,) * len(shape))

    def call(self, body, meta, ins, outs, args, shapes, name, scratch=(), flops=0):
        moved = sum(a.size * a.dtype.itemsize for a in args)
        return pl.pallas_call(
            with_meta(body),
            grid_spec=pltpu.PrefetchScalarGridSpec(
                num_scalar_prefetch=len(meta),
                grid=(self.steps,),
                in_specs=ins,
                out_specs=outs,
                scratch_shapes=scratch,
            ),
            out_shape=shapes,
            name=name,
            compiler_params=pltpu.CompilerParams(vmem_limit_bytes=VMEM_BYTES),
            cost_estimate=pl.CostEstimate(flops=flops, bytes_accessed=2 * moved, transcendentals=0),
        )(*meta, *args)


def fast(x):
    return pltpu.with_memory_space_constraint(x, pltpu.VMEM)


def slow(x):
    return pltpu.with_memory_space_constraint(x, pltpu.HBM)


def running_sums(pieces, backward):
    return pl.pallas_call(
        functools.partial(running_kernel, backward),
        out_shape=pltpu.HBM(pieces.shape, BF16),
        name="running_sums",
        compiler_params=pltpu.CompilerParams(vmem_limit_bytes=VMEM_BYTES),
    )(fast(pieces))


def make_shards(n_seq, n_head):
    chips = n_seq // CORES
    group = CORES * n_head

    def swap(x):
        return lax.ppermute(x, "core", [(0, 1), (1, 0)])

    def scattered(pieces):
        return lax.all_to_all(pieces, "chip", 0, 0, tiled=True)

    def scanned(delta, backward, beside=None):
        heads = delta.shape[0]
        pieces = scattered(delta.reshape(chips, heads * DH // chips, DH))
        if beside is not None:
            pieces, beside = lax.optimization_barrier((pieces, beside))
        state = scattered(running_sums(pieces, backward)).reshape(heads, DH, DH)
        return state if beside is None else (state,) + beside

    def side_by_side(core, own, other):
        return jnp.where(
            core == 0,
            jnp.concatenate([own, other], axis=1),
            jnp.concatenate([other, own], axis=1),
        )

    def shards(queries, key_vectors, value_vectors, cotangent, member_ids, in_scale, out_scale):
        tok, both = queries.shape
        width = both // CORES
        heads = width // DH
        full_width = both * n_head
        rows = 2 * tok
        core = lax.axis_index("core")

        other_ids = swap(member_ids)
        v_other = swap(value_vectors)
        k_other = swap(key_vectors)
        place = core[None].astype(jnp.int32)
        local = Local(tok, width)
        shared, cols, state = local.shared, local.cols, local.state
        half = pltpu.HBM((tok, width), BF16)
        low = pltpu.HBM((rows, width), BF16)
        wide = pltpu.HBM((rows, width), F32)
        part = pltpu.HBM((MEMBERS, width), F32)
        sent = pltpu.HBM((heads, DH, DH), BF16)
        pairs = [shared(tok), shared(tok)]
        lines, wide_line = LANE_GROUPS * MEMBERS, width // LANE_GROUPS
        packed = (chips, lines, wide_line + DH)
        unit = 2 * heads * rows * DH * DH

        meta = (place, member_ids, other_ids)
        scaled, delta = local.call(
            states_kernel,
            meta,
            [shared(MEMBERS)] + pairs * 2,
            [cols(rows), state()],
            (slow(in_scale), slow(key_vectors), fast(k_other), slow(value_vectors), fast(v_other)),
            [low, sent],
            "states",
            flops=unit,
        )
        queries_late, cotangent_late, delta = lax.optimization_barrier((queries, cotangent, delta))
        q_other = swap(queries_late)
        c_other = swap(cotangent_late)
        state_in = scanned(delta, False)
        inside, q, k, v, c = local.call(
            inside_kernel,
            meta,
            pairs * 4 + [cols(rows)],
            [cols(rows)] * 5,
            (
                slow(queries), slow(q_other), slow(key_vectors), slow(k_other),
                slow(value_vectors), slow(v_other), slow(cotangent), slow(c_other), slow(scaled),
            ),
            [low] * 5,
            "inside",
            flops=4 * unit,
        )
        q, k, v, c = slow(q), slow(k), slow(v), slow(c)
        mixed, sums = local.call(
            mixed_kernel,
            meta,
            [shared(MEMBERS), cols(rows), cols(rows), state(), cols(rows)],
            [cols(rows), local.whole((group, 2, rows))],
            (slow(out_scale), q, c, fast(state_in), slow(inside)),
            [low, pltpu.HBM((group, 2, rows), F32)],
            "mixed",
            scratch=[pltpu.VMEM((rows, DH), F32)] * 2,
            flops=unit,
        )
        sums = lax.all_to_all(sums, ("core", "head"), 0, 0, tiled=True)
        grad, delta_after = local.call(
            functools.partial(grads_kernel, full_width),
            meta,
            [shared(MEMBERS)] + [cols(rows)] * 3 + [local.whole((group, 2, rows))],
            [cols(rows), state()],
            (slow(out_scale), q, c, slow(mixed), sums),
            [low, sent],
            "grads",
            scratch=[pltpu.VMEM((2, rows, DH), F32)],
            flops=unit,
        )
        out_part = local.call(
            functools.partial(outs_kernel, full_width),
            meta,
            [cols(rows)] * 2 + [local.whole((group, 2, rows))],
            cols(MEMBERS),
            (c, slow(mixed), sums),
            part,
            "outs",
        )
        query_own, query_send = local.call(
            query_kernel,
            meta,
            [cols(rows)] * 3 + [state()],
            [cols(tok)] * 2,
            (k, slow(scaled), slow(grad), slow(state_in)),
            [half] * 2,
            "query",
            flops=5 * unit,
        )
        out_part = out_part + lax.ppermute(out_part, "chip", [(i, i ^ 1) for i in range(chips)])
        mine = MEMBERS // 2
        first = lax.axis_index("chip") % 2 * mine
        extra = lax.dynamic_slice_in_dim(out_part, first, mine, 0).reshape(lines, DH)
        state_after, query_own, extra = scanned(delta_after, True, (query_own, extra))
        key_in, value_in, in_part = local.call(
            back_kernel,
            meta,
            [cols(rows)] * 5,
            [cols(rows), cols(rows), cols(MEMBERS)],
            (q, k, v, slow(scaled), slow(grad)),
            [wide, wide, part],
            "back",
            flops=8 * unit,
        )
        query_grad = side_by_side(core, query_own, swap(query_send))
        copies = local.call(
            copies_kernel,
            meta,
            [cols(rows), cols(rows), state(), cols(MEMBERS), local.whole((lines, DH))],
            local.whole(packed),
            (k, v, fast(state_after), slow(in_part), extra),
            pltpu.HBM(packed, BF16),
            "copies",
            scratch=[pltpu.VMEM((lines, wide_line), F32)],
            flops=unit,
        )
        copies = scattered(copies)
        key_own, key_send, value_own, value_send = local.call(
            last_kernel,
            meta,
            [shared(MEMBERS), cols(rows), cols(rows), state(), cols(rows), cols(rows)],
            [cols(tok)] * 4,
            (slow(in_scale), k, slow(scaled), slow(state_after), slow(key_in), slow(value_in)),
            [half] * 4,
            "last",
            flops=2 * unit,
        )
        key_grad = side_by_side(core, key_own, swap(key_send))
        value_grad = side_by_side(core, value_own, swap(value_send))
        copies, key_grad, value_grad, query_grad = lax.optimization_barrier(
            (copies, key_grad, value_grad, query_grad)
        )
        parts = pl.pallas_call(
            total_kernel,
            out_shape=jax.ShapeDtypeStruct((2 * MEMBERS, width), F32),
            name="total",
            compiler_params=pltpu.CompilerParams(vmem_limit_bytes=VMEM_BYTES),
        )(copies)
        parts = side_by_side(core, parts, swap(parts))
        return query_grad, key_grad, value_grad, parts[:MEMBERS], parts[MEMBERS:]

    return shards


def solution(mesh):
    n_seq, n_head = mesh.shape["seq"], mesh.shape["head"]
    chips = n_seq // CORES
    finer = Mesh(mesh.devices.reshape(chips, CORES, n_head), ("chip", "core", "head"))
    tokens = ("chip", "core")
    wide = P(tokens, "head")
    scale = P(None, "head")
    return jax.shard_map(
        make_shards(n_seq, n_head),
        mesh=finer,
        in_specs=(wide, wide, wide, wide, P(tokens), scale, scale),
        out_specs=(wide, wide, wide, scale, scale),
        check_vma=False,
    )
```
